128 devices in a mesh: lat: 4 (over y_hi, core), lon: 32 (over y_lo, x, z).
Axes of the slice: x: 4, y: 4 (y_hi: 2, y_lo: 2; y = y_hi * 2 + y_lo), z: 4, core: 2. Of those that a mesh axis runs over, the one named last changes fastest.
Arguments:
- tokens: bfloat16 [2, 24, 768, 512], P(None, 'lat', 'lon'), may hold values from -6 to 6
- cotangent: bfloat16 [2, 24, 768, 512], P(None, 'lat', 'lon'), may hold values from -6 to 6
- key_keep: int32 [2, 24, 768], P(None, 'lat', 'lon'), may hold values 0 or 1
- norm_gain: float32 [512], replicated, may hold values from 0.5 to 1.5
- w_qkv: bfloat16 [512, 1536], replicated, may hold values from -0.25 to 0.25
- w_proj: bfloat16 [512, 512], replicated, may hold values from -0.25 to 0.25
- attn_scale: float32 [8], replicated, may hold values from 1 to 10
Outputs:
- mixed: bfloat16 [2, 24, 768, 512], P(None, 'lat', 'lon')
- grad_tokens: bfloat16 [2, 24, 768, 512], P(None, 'lat', 'lon')
- grad_qkv: float32 [512, 1536], replicated
- grad_proj: float32 [512, 512], replicated
- grad_gain: float32 [512], replicated
- grad_scale: float32 [8], replicated
The draws below stay inside these ranges and needn't reach their ends.
Inputs may be any that keep to these rules, and one draw needn't show every extreme that they name: `key_keep`: 1 marks a token that may serve as a key, 0 a padded one.
All inputs are finite; a program needn't handle non-finite values. No bound on the sum of `key_keep` on one device may be relied on, other than what follows from the above.
Results may differ from the reference program's by a relative error of at most 0.0089.
Values may be sent and summed in bfloat16 or wider, within the bound.
A program may use at most 128 MiB of HBM per device.

```python
import math
import jax
import jax.numpy as jnp
from jax import lax

D = 512
HEADS = 8
LEV = 2
NLAT = 24
NLON = 768


def plant(values, key, smallest, largest):
    longest = values.shape.index(max(values.shape))
    spots = []
    for shift in (0, 1):
        where = [jax.random.randint(jax.random.fold_in(key, axis), (), 0, length) for axis, length in enumerate(values.shape)]
        where[longest] = (where[longest] + shift) % values.shape[longest]
        spots.append(tuple(where))
    return values.at[spots[0]].set(smallest).at[spots[1]].set(largest)


def shard_levels(key, dims, pieces, smallest, high):
    def one(dim, parts):
        heights = jax.random.uniform(jax.random.fold_in(jax.random.fold_in(key, 6), dim), (parts,), jnp.float32, smallest / len(pieces), high / len(pieces))
        return jnp.repeat(jnp.exp(heights), dims[dim] // parts).reshape((-1,) + (1,) * (len(dims) - dim - 1))

    level = one(*pieces[0])
    for cut in pieces[1:]:
        level = level * one(*cut)
    return level


def scatter_about(rng, extent, deviation, most, cuts=(), held_as=jnp.bfloat16):
    loudness = shard_levels(rng, extent, cuts, -0.22, 0.18) if cuts else 1.0
    array = jax.random.normal(rng, extent, jnp.float32) * deviation * loudness
    return jnp.minimum(jnp.maximum(array, -most), most).astype(held_as)


def setup_inputs(seed: int = 0) -> dict:
    key_of = jax.random.split(jax.random.key(seed), 8)
    return {
        "tokens": scatter_about(key_of[0], (LEV, NLAT, NLON, D), 1.0, 6.0, ((1, 4), (2, 32))),
        "cotangent": scatter_about(key_of[1], (LEV, NLAT, NLON, D), 1.0, 6.0, ((1, 4), (2, 32))),
        "key_keep": plant((jax.random.randint(key_of[2], (LEV, NLAT, NLON), 0, 8) < 7).astype(jnp.int32), jax.random.fold_in(key_of[2], 1), 0, 1),
        "norm_gain": jnp.clip(1.0 + 0.1 * jax.random.normal(key_of[3], (D,), jnp.float32), 0.5, 1.5),
        "w_qkv": scatter_about(key_of[4], (D, 3 * D), D ** -0.5, 0.25),
        "w_proj": scatter_about(key_of[5], (D, D), D ** -0.5, 0.25),
        "attn_scale": jnp.clip(jnp.exp(jax.random.uniform(key_of[6], (HEADS,), jnp.float32, math.log(1.0), math.log(10.0))), 1.0, 10.0),
    }


EPS_NORM = 1e-05
EPS_DIR = 1e-06

def normed(row_data, norm_gain):
    row_mean = lax.optimization_barrier(jnp.mean(row_data, axis=-1, keepdims=True))
    centered = row_data - row_mean
    variance = lax.optimization_barrier(jnp.mean(centered * centered, axis=-1, keepdims=True))
    return centered * lax.rsqrt(variance + EPS_NORM) * norm_gain

def unit_dir(vectors):
    return vectors * lax.rsqrt(lax.optimization_barrier(jnp.sum(vectors * vectors, axis=-1, keepdims=True)) + EPS_DIR)

def attend(query, keys, values, allowed, scale):
    num_heads = scale.shape[0]
    blocks, query_count, channels = query.shape
    key_count = keys.shape[1]
    head_size = channels // num_heads
    query_dir = unit_dir(query.reshape(blocks, query_count, num_heads, head_size))
    key_dir = unit_dir(keys.reshape(blocks, key_count, num_heads, head_size))
    value_heads = values.reshape(blocks, key_count, num_heads, head_size)
    cosine = jnp.einsum('bqhd,bkhd->bhqk', query_dir, key_dir, precision=lax.Precision.HIGHEST)
    scale_row = scale[None, :, None, None]
    numer = jnp.exp(scale_row * cosine - scale_row) * allowed[:, None, :, :]
    weights = numer / lax.optimization_barrier(jnp.sum(numer, axis=-1, keepdims=True))
    result = jnp.einsum('bhqk,bkhd->bqhd', weights, value_heads, precision=lax.Precision.HIGHEST)
    return result.reshape(blocks, query_count, channels)

def contract(left, right, left_dim, right_dim):
    return lax.dot_general(left, right, (((left_dim,), (right_dim,)), ((), ())), preferred_element_type=jnp.float32)

def reference(tokens, cotangent, key_keep, norm_gain, w_qkv, w_proj, attn_scale):
    row_wins = NLAT // 6 + 1
    stripes = NLON // 12
    win_tokens = LEV * 72

    def to_windows(grid, width):
        padded = jnp.pad(grid, ((0, 0), (3, 3), (0, 0), (0, 0)))
        return padded.reshape(LEV, row_wins, 6, 12, width).transpose(1, 0, 2, 3, 4).reshape(row_wins, win_tokens, width)

    def from_windows(arr, width):
        grid = arr.reshape(row_wins, LEV, 6, 12, width).transpose(1, 0, 2, 3, 4).reshape(LEV, NLAT + 6, 12, width)
        return grid[:, 3:-3]

    def stripe_pass(carry, data):
        stripe_x, stripe_g, stripe_keep = data
        row_data = stripe_x.reshape(-1, D).astype(jnp.float32)
        normal_y = normed(row_data, norm_gain).astype(jnp.bfloat16)
        qkv = jnp.dot(normal_y, w_qkv, preferred_element_type=jnp.float32).astype(jnp.bfloat16)
        windows = to_windows(qkv.reshape(LEV, NLAT, 12, 3 * D), 3 * D).astype(jnp.float32)
        keep_pad = jnp.pad(stripe_keep, ((0, 0), (3, 3), (0, 0)))
        keep_win = keep_pad.reshape(LEV, row_wins, 6, 12).transpose(1, 0, 2, 3).reshape(row_wins, win_tokens).astype(jnp.float32)
        allowed = jnp.maximum(keep_win[:, None, :], jnp.eye(win_tokens, dtype=jnp.float32)[None])

        def core_local(q_in, k_in, v_in, s_in):
            return attend(q_in, k_in, v_in, allowed, s_in)
        att_win, pull = jax.vjp(core_local, windows[..., :D], windows[..., D:2 * D], windows[..., 2 * D:], attn_scale)
        attended = from_windows(att_win, D).reshape(-1, D).astype(jnp.bfloat16)
        mixed_rows = (row_data + jnp.dot(attended, w_proj, preferred_element_type=jnp.float32)).astype(jnp.bfloat16)
        g_rows = stripe_g.reshape(-1, D)
        part_proj = contract(attended, g_rows, 0, 0)
        d_att = contract(g_rows, w_proj, 1, 1).astype(jnp.bfloat16)
        d_win = to_windows(d_att.reshape(LEV, NLAT, 12, D).astype(jnp.float32), D)
        d_query, d_key, d_value, d_scale = pull(d_win)
        d_all = jnp.concatenate([d_query, d_key, d_value], axis=-1)
        d_qkv = from_windows(d_all, 3 * D).reshape(-1, 3 * D).astype(jnp.bfloat16)
        part_qkv = contract(normal_y, d_qkv, 0, 0)
        d_normal = contract(d_qkv, w_qkv, 1, 1)
        pull_norm = jax.vjp(normed, row_data, norm_gain)[1]
        d_rows, d_gain = pull_norm(d_normal)
        grad_rows = (g_rows.astype(jnp.float32) + d_rows).astype(jnp.bfloat16)
        sum_qkv, sum_proj, sum_gain, sum_scale = carry
        carry = (sum_qkv + part_qkv, sum_proj + part_proj, sum_gain + d_gain, sum_scale + d_scale)
        return (carry, (mixed_rows.reshape(LEV, NLAT, 12, D), grad_rows.reshape(LEV, NLAT, 12, D)))

    def to_stripes(arr):
        rolled = jnp.roll(arr, 6, axis=2)
        shape_tail = arr.shape[3:]
        split = rolled.reshape((LEV, NLAT, stripes, 12) + shape_tail)
        order = (2, 0, 1, 3) + tuple(range(4, 4 + len(shape_tail)))
        return split.transpose(order)

    def from_stripes(arr):
        joined = arr.transpose(1, 2, 0, 3, 4).reshape(LEV, NLAT, NLON, D)
        return jnp.roll(joined, -6, axis=2)
    start = (jnp.zeros((D, 3 * D), jnp.float32), jnp.zeros((D, D), jnp.float32), jnp.zeros((D,), jnp.float32), jnp.zeros((HEADS,), jnp.float32))
    sums, outs = lax.scan(stripe_pass, start, (to_stripes(tokens), to_stripes(cotangent), to_stripes(key_keep)))
    grad_qkv, grad_proj, grad_gain, grad_scale = sums
    return (from_stripes(outs[0]), from_stripes(outs[1]), grad_qkv, grad_proj, grad_gain, grad_scale)
```

```python
import functools

import jax
import jax.numpy as jnp
import numpy as np
from jax import lax
from jax.experimental import pallas as pl
from jax.experimental.pallas import tpu as pltpu
from jax.sharding import PartitionSpec as P

EPS_NORM = 1e-05
EPS_DIR = 1e-06
MESH = pl.DeviceIdType.MESH
BF = jnp.bfloat16
F32 = jnp.float32

QUARTERS = ((1, 1), (1, 2), (0, 1), (0, 2), (1, 3), (1, 0), (0, 3), (0, 0))
QT = 40
ROWS = 80
WIN = 160
FLAG_ROW = 36


def token_of(quarter, t):
    half, cq = QUARTERS[quarter]
    lev, rest = divmod(t, 18)
    rr, cc = divmod(rest, 6)
    return lev * 144 + (half * 3 + rr) * 24 + cq * 6 + cc


def tables():
    perm = np.zeros((8 * QT, 288), np.float32)
    member = np.zeros((8, 288), np.float32)
    place = np.zeros((288, 256), np.float32)
    for quarter in range(8):
        for t in range(36):
            src = token_of(quarter, t)
            perm[quarter * QT + t, src] = 1.0
            member[quarter, src] = 1.0
            place[src, QT * (quarter % 4) + t] = 1.0
    return perm, member, place


def dot(a, b, ca=1, cb=0):
    return lax.dot_general(a, b, (((ca,), (cb,)), ((), ())), preferred_element_type=F32)


def position():
    lat = lax.axis_index("lat")
    lon = lax.axis_index("lon")
    return lat, lon


def wrap(value, count):
    return lax.rem(value + count, count)


SLOT_SENDS = ((2, "lat"), (5, "lon"), (7, "diag"), (6, "lat"), (3, "lat"))
KEPT_SLOTS = (0, 1, 4)

GROUPS = (
    (0, 768, "xzy"),
    (768, 512, "yxz"),
    (1280, 768, "zyx"),
    (2048, 768, "xzy"),
    (2816, 512, "yxz"),
    (3328, 768, "zyx"),
)


def slot_pieces(slot):
    if slot < 4:
        first = 2 * (slot // 2)
        kind = "xg"[slot % 2]
        return ((kind, first), (kind, first + 1))
    return (("x", slot), ("g", slot))


def coordinates():
    lat, lon = position()
    core = lax.rem(lat, 2)
    y = (lat // 2) * 2 + lon // 16
    x = lax.rem(lon // 4, 4)
    z = lax.rem(lon, 4)
    return {"x": x, "y": y, "z": z, "core": core}


def device_at(co):
    return ((co["y"] // 2) * 2 + co["core"], lax.rem(co["y"], 2) * 16 + co["x"] * 4 + co["z"])


def peer(co, axis, j):
    moved = dict(co)
    moved[axis] = lax.rem(co[axis] + j, 4)
    return device_at(moved)


def sibling(co):
    moved = dict(co)
    moved["core"] = 1 - co["core"]
    return device_at(moved)


def shift_in_kernel(
    x_hbm, g_hbm, keep_hbm, perm_hbm, member_hbm, place_hbm, wqkv_hbm, wproj_hbm, gain_hbm,
    win_ref, wqkv_ref, wproj_ref, gain_ref,
    x_ref, g_ref, keep_ref, perm_ref, member_ref, place_ref, in_buf, w_sem, in_send, in_recv,
):
    lat, lon = position()
    lat_lo, lat_hi = wrap(lat - 1, 4), wrap(lat + 1, 4)
    lon_lo, lon_hi = wrap(lon - 1, 32), wrap(lon + 1, 32)
    barrier = pltpu.get_barrier_semaphore()
    for dev in ((lat_hi, lon), (lat, lon_hi), (lat_hi, lon_hi)):
        pl.semaphore_signal(barrier, inc=1, device_id=dev, device_id_type=MESH)
    loads = []
    for i, (src, dst) in enumerate((
        (perm_hbm, perm_ref),
        (x_hbm, x_ref),
        (keep_hbm, keep_ref),
        (member_hbm, member_ref),
        (place_hbm, place_ref),
        (g_hbm, g_ref),
        (wqkv_hbm, wqkv_ref),
        (wproj_hbm, wproj_ref),
        (gain_hbm, gain_ref),
    )):
        loads.append(pltpu.make_async_copy(src, dst, w_sem.at[i]))
        loads[-1].start()
    for load in loads[:6]:
        load.wait()
    perm = perm_ref[...]
    xs = dot(perm, x_ref[...])
    gs = dot(perm, g_ref[...])
    keep_rows = [keep_ref[row, lev : lev + 1, :].astype(F32) for lev in range(2) for row in range(6)]
    marks = (jnp.concatenate(keep_rows, axis=1) * member_ref[...].astype(F32)).astype(BF)
    flags = dot(marks, place_ref[...])
    row_id = lax.broadcasted_iota(jnp.int32, (QT, 512), 0)

    def piece(kind, quarter):
        rows = slice(quarter * QT, (quarter + 1) * QT)
        if kind == "g":
            return gs[rows]
        flag = jnp.concatenate([flags[quarter : quarter + 1], jnp.zeros((1, 256), F32)], axis=1)
        return jnp.where(row_id == FLAG_ROW, flag, xs[rows])

    def payload(slot):
        return jnp.concatenate([piece(*p) for p in slot_pieces(slot)], axis=0).astype(BF)

    for i, (slot, _) in enumerate(SLOT_SENDS):
        in_buf[i] = payload(slot)
    pl.semaphore_wait(barrier, 3)
    low = {"lat": (lat_lo, lon), "lon": (lat, lon_lo), "diag": (lat_lo, lon_lo)}
    copies = []
    for i, (slot, way) in enumerate(SLOT_SENDS):
        copy = pltpu.make_async_remote_copy(
            src_ref=in_buf.at[i],
            dst_ref=win_ref.at[slot],
            send_sem=in_send.at[i],
            recv_sem=in_recv.at[i],
            device_id=low[way],
            device_id_type=MESH,
        )
        copy.start()
        copies.append(copy)
    for slot in KEPT_SLOTS:
        win_ref[slot] = payload(slot)
    for load in loads[6:]:
        load.wait()
    for copy in copies:
        copy.wait()


def block_sum_matrix():
    r = lax.broadcasted_iota(jnp.int32, (512, 512), 0)
    c = lax.broadcasted_iota(jnp.int32, (512, 512), 1)
    return jnp.where((r // 64) == (c // 64), 1.0, 0.0).astype(BF)


def head_sum(values, ones):
    hi = values.astype(BF)
    lo = (values - hi.astype(F32)).astype(BF)
    return dot(hi, ones) + dot(lo, ones)


def compute_kernel(
    win_ref, wqkv_ref, wproj_ref, gain_ref, scale_hbm,
    back_ref, grads_ref, small_ref,
    scale_ref, scale_sem, qd_s, kd_s, v_s, do_s, dq_s, dk_s, dv_s, att_s, allow_s, gs_s,
):
    scale_load = pltpu.make_async_copy(scale_hbm, scale_ref, scale_sem)
    scale_load.start()
    lat = lax.axis_index("lat")
    gain = gain_ref[...]
    slots = [win_ref[slot].astype(F32) for slot in range(8)]
    data = jnp.concatenate([slots[0], slots[2]] + [slots[slot][:QT] for slot in (4, 5, 6, 7)], axis=0)
    data = data.reshape(8, QT, 512)
    row_q = lax.broadcasted_iota(jnp.int32, (QT, 512), 0)
    x = jnp.where((row_q < 36)[None], data, 0.0).reshape(8 * QT, 512)
    g = jnp.concatenate([slots[1], slots[3]] + [slots[slot][QT:] for slot in (4, 5, 6, 7)], axis=0)
    g_b = g.astype(BF)
    mean = jnp.mean(x, axis=-1, keepdims=True)
    xc = x - mean
    var = jnp.mean(xc * xc, axis=-1, keepdims=True)
    rstd = lax.rsqrt(var + EPS_NORM)
    xhat = xc * rstd
    y = (xhat * gain).astype(BF)

    ones = block_sum_matrix()
    q = dot(y, wqkv_ref[:, 0:512]).astype(BF).astype(F32)
    k = dot(y, wqkv_ref[:, 512:1024]).astype(BF).astype(F32)
    v_s[...] = dot(y, wqkv_ref[:, 1024:1536]).astype(BF)
    rq = lax.rsqrt(head_sum(q * q, ones) + EPS_DIR)
    rk = lax.rsqrt(head_sum(k * k, ones) + EPS_DIR)
    qd = q * rq
    kd = k * rk
    qd_s[...] = qd.astype(BF)
    kd_s[...] = kd.astype(BF)
    do_s[...] = dot(g_b, wproj_ref[...], 1, 1).astype(BF)

    key_id = lax.broadcasted_iota(jnp.int32, (WIN, WIN), 0)
    query_id = lax.broadcasted_iota(jnp.int32, (WIN, WIN), 1)
    same_half = (key_id >= 2 * QT) == (query_id >= 2 * QT)
    joined = jnp.logical_or(same_half, lat != 3)
    first_row = lax.broadcasted_iota(jnp.int32, (8, WIN), 0) == 0
    one_row = jnp.where(first_row, 1.0, 0.0).astype(BF)
    for w in range(2):
        marks = data[4 * w, FLAG_ROW : FLAG_ROW + 1, :]
        for i in range(1, 4):
            marks = marks + data[4 * w + i, FLAG_ROW : FLAG_ROW + 1, :]
        marks = jnp.where(first_row, marks[:, :WIN], 0.0).astype(BF)
        keep = dot(marks, one_row, 0, 0)
        keep = jnp.where(joined, keep, 0.0)
        allow_s[w] = jnp.where(key_id == query_id, 1.0, keep)

    lane = lax.broadcasted_iota(jnp.int32, (1, 128), 1)
    scale_load.wait()

    def pair_window(pair, w):
        step = w * 4 + pair
        rows = slice(w * WIN, (w + 1) * WIN)
        cols = pl.ds(pl.multiple_of(pair * 128, 128), 128)
        qd_p = qd_s[rows, cols]
        kd_p = kd_s[rows, cols]
        v_p = v_s[rows, cols]
        do_p = do_s[rows, cols]
        allow = allow_s[w]
        acc_o = jnp.zeros((WIN, 128), F32)
        acc_q = jnp.zeros((WIN, 128), F32)
        acc_k = jnp.zeros((WIN, 128), F32)
        acc_v = jnp.zeros((WIN, 128), F32)
        zero = jnp.zeros((WIN, 128), BF)
        scales = [scale_ref[pair * 2 + i] for i in range(2)]
        for i in range(2):
            s = scales[i]
            mine = jnp.broadcast_to((lane < 64) if i == 0 else (lane >= 64), (WIN, 128))
            qd_h = jnp.where(mine, qd_p, zero)
            kd_h = jnp.where(mine, kd_p, zero)
            v_h = jnp.where(mine, v_p, zero)
            do_h = jnp.where(mine, do_p, zero)
            cos = dot(kd_p, qd_h, 1, 1)
            e = jnp.exp(s * cos - s) * allow
            p = e * (1.0 / jnp.sum(e, axis=0, keepdims=True))
            dp = dot(v_p, do_h, 1, 1)
            dl = p * (dp - jnp.sum(p * dp, axis=0, keepdims=True))
            gs_s[step, i : i + 1, :] = jnp.sum(dl * cos, axis=0, keepdims=True)
            p_b = p.astype(BF)
            dl_b = dl.astype(BF)
            acc_o = acc_o + dot(p_b, v_h, 0, 0)
            acc_v = acc_v + dot(p_b, do_h)
            acc_k = acc_k + dot(dl_b, qd_h)
            acc_q = acc_q + dot(dl_b, kd_h, 0, 0)
        s_lane = jnp.where(lane < 64, scales[0], scales[1])
        att_s[rows, cols] = acc_o.astype(BF)
        dv_s[rows, cols] = acc_v.astype(BF)
        dk_s[rows, cols] = acc_k * s_lane
        dq_s[rows, cols] = acc_q * s_lane

    def pair_step(pair, carry):
        pair_window(pair, 0)
        pair_window(pair, 1)
        return carry

    lax.fori_loop(0, 4, pair_step, 0)

    att = att_s[...]
    mixed = x + dot(att, wproj_ref[...])

    def put(block, value):
        for half in range(2):
            for ct in range(4):
                first = block * 1024 + ct * 256
                tile = value[half * 256 : (half + 1) * 256, ct * 128 : (ct + 1) * 128]
                grads_ref[half, first : first + 256] = tile.astype(BF)

    put(3, dot(att, g_b, 0, 0))
    dqd = dq_s[...]
    dq = (rq * (dqd - qd * head_sum(qd * dqd, ones))).astype(BF)
    dkd = dk_s[...]
    dk = (rk * (dkd - kd * head_sum(kd * dkd, ones))).astype(BF)
    dv = dv_s[...]
    put(2, dot(y, dv, 0, 0))
    put(1, dot(y, dk, 0, 0))
    put(0, dot(y, dq, 0, 0))
    dn = dot(dq, wqkv_ref[:, 0:512], 1, 1)
    dn = dn + dot(dk, wqkv_ref[:, 512:1024], 1, 1)
    dn = dn + dot(dv, wqkv_ref[:, 1024:1536], 1, 1)
    d_gain = jnp.sum(dn * xhat, axis=0, keepdims=True)
    dxh = dn * gain
    dx = rstd * (dxh - jnp.mean(dxh, axis=-1, keepdims=True) - xhat * jnp.mean(dxh * xhat, axis=-1, keepdims=True))
    gtok = g + dx
    for slot in (0, 2):
        rows = slice(slot * QT, (slot + 2) * QT)
        back_ref[slot] = mixed[rows].astype(BF)
        back_ref[slot + 1] = gtok[rows].astype(BF)
    for slot in (4, 5, 6, 7):
        rows = slice(slot * QT, (slot + 1) * QT)
        back_ref[slot] = jnp.concatenate([mixed[rows], gtok[rows]], axis=0).astype(BF)

    small_ref[...] = jnp.zeros((16, 128), F32)
    for i in range(4):
        small_ref[i : i + 1, :] = d_gain[:, i * 128 : (i + 1) * 128]
    for h in range(8):
        row = gs_s[h // 2, h % 2 : h % 2 + 1, :] + gs_s[4 + h // 2, h % 2 : h % 2 + 1, :]
        small_ref[8 + h : 9 + h, :] = jnp.broadcast_to(jnp.sum(row, axis=1, keepdims=True), (1, 128))


def reduce_kernel(
    back_ref, grads_ref, small_ref,
    ret_ref, sum_ref, small_out_ref,
    r0, a1, r1, a2, r2, a3, sv0, sv1, sv2, sv3,
    out_send, out_recv, sib_send, sib_recv, st_send, st_recv, sv_send, sv_recv,
):
    lat, lon = position()
    lat_lo, lat_hi = wrap(lat - 1, 4), wrap(lat + 1, 4)
    lon_lo, lon_hi = wrap(lon - 1, 32), wrap(lon + 1, 32)
    co = coordinates()
    core = co["core"]
    sib = sibling(co)
    peers = {axis: [peer(co, axis, j) for j in (1, 2, 3)] for axis in "xyz"}
    high = {"lat": (lat_hi, lon), "lon": (lat, lon_hi), "diag": (lat_hi, lon_hi)}
    barrier = pltpu.get_barrier_semaphore()
    greet = [(lat_lo, lon), (lat, lon_lo), (lat_lo, lon_lo), sib]
    for axis in "xyz":
        greet.extend(peers[axis])
    for dev in greet:
        pl.semaphore_signal(barrier, inc=1, device_id=dev, device_id_type=MESH)
    pl.semaphore_wait(barrier, len(greet))

    started = []

    def send(src, dst, s_sem, r_sem, dev):
        copy = pltpu.make_async_remote_copy(
            src_ref=src, dst_ref=dst, send_sem=s_sem, recv_sem=r_sem, device_id=dev, device_id_type=MESH
        )
        copy.start()
        started.append(copy)
        return copy

    flight = {}

    def send_stage(group, stage, axis, pairs):
        copies = []
        for j in range(3):
            src, dst = pairs(j)
            index = (group, stage, j)
            copies.append(send(src, dst, st_send.at[index], st_recv.at[index], peers[axis][j]))
        flight[group] = copies

    def arrived(group):
        for copy in flight[group]:
            copy.wait_recv()

    def size_of(group, level):
        return GROUPS[group][1] // (4, 16)[level]

    def start_of(group, level):
        return GROUPS[group][0] // (1, 4)[level]

    def own_rows(group, level, j=0):
        first, size = start_of(group, level), size_of(group, level)
        turn = lax.rem(co[GROUPS[group][2][level]] + j, 4)
        return pl.ds(pl.multiple_of(first + turn * size, 16), size)

    def landing(group, level):
        return pl.ds(GROUPS[group][0] // (4, 16)[level], size_of(group, level))

    def scatter(group, level, src, dst):
        def pairs(j):
            return src.at[own_rows(group, level, j + 1)], dst.at[j, landing(group, level)]

        send_stage(group, level, GROUPS[group][2][level], pairs)

    def gathered(group, level, src, dst):
        arrived(group)
        total = src[own_rows(group, level)].astype(F32)
        for j in range(3):
            total = total + dst[j, landing(group, level)].astype(F32)
        return total.astype(BF)

    def final_rows(group, level):
        first, rows, axes = GROUPS[group]
        off = first + co[axes[0]] * (rows // 4)
        if level == 1:
            off = off + co[axes[1]] * (rows // 16)
        return pl.ds(pl.multiple_of(off, 16), size_of(group, level))

    def spread(group, level):
        where = sum_ref.at[core, final_rows(group, level)]
        send_stage(group, 4 - level, GROUPS[group][2][level], lambda j: (where, where))

    sib_in = {}
    for group, (first, count, _) in enumerate(GROUPS):
        rows = pl.ds(first, count)
        sib_in[group] = send(grads_ref.at[1 - core, rows], r0.at[rows], sib_send.at[group], sib_recv.at[group], sib)

    def join(group):
        sib_in[group].wait_recv()
        rows = pl.ds(GROUPS[group][0], GROUPS[group][1])
        a1[rows] = (grads_ref[core, rows].astype(F32) + r0[rows].astype(F32)).astype(BF)

    def advance(group, stage):
        if stage == 0:
            join(group)
            scatter(group, 0, a1, r1)
        elif stage == 1:
            a2[landing(group, 0)] = gathered(group, 0, a1, r1)
            scatter(group, 1, a2, r2)
        elif stage == 2:
            me = co[GROUPS[group][2][2]]
            a3[me, landing(group, 1)] = gathered(group, 1, a2, r2)
            here = a3.at[me, landing(group, 1)]
            send_stage(group, 2, GROUPS[group][2][2], lambda j: (here, here))
        elif stage == 3:
            arrived(group)
            total = a3[0, landing(group, 1)].astype(F32)
            for i in range(1, 4):
                total = total + a3[i, landing(group, 1)].astype(F32)
            sum_ref[core, final_rows(group, 1)] = total.astype(BF)
            spread(group, 1)
        elif stage == 4:
            arrived(group)
            spread(group, 0)
        elif stage == 5:
            arrived(group)
            whole = sum_ref.at[core, pl.ds(GROUPS[group][0], GROUPS[group][1])]
            flight[group] = [send(whole, whole, sib_send.at[6 + group], sib_recv.at[6 + group], sib)]
        else:
            arrived(group)

    def small_stage(stage, values):
        axis = ("core", "x", "y", "z")[stage]
        buf = (sv0, sv1, sv2, sv3)[stage]
        me = co[axis]
        buf[me] = values
        copies = []
        for j, dev in enumerate([sib] if stage == 0 else peers[axis]):
            index = 0 if stage == 0 else 1 + 3 * (stage - 1) + j
            copies.append(send(buf.at[me], buf.at[me], sv_send.at[index], sv_recv.at[index], dev))
        return copies

    def small_sum(stage, copies):
        buf = (sv0, sv1, sv2, sv3)[stage]
        for copy in copies:
            copy.wait_recv()
        total = buf[0]
        for i in range(1, 2 if stage == 0 else 4):
            total = total + buf[i]
        return total

    small_copies = small_stage(0, small_ref[...])
    back = {}
    for i, (slot, way) in enumerate(SLOT_SENDS):
        back[slot] = send(back_ref.at[slot], ret_ref.at[slot], out_send.at[i], out_recv.at[i], high[way])
    for slot in KEPT_SLOTS:
        ret_ref[slot] = back_ref[slot]
    for stage in range(7):
        for group in range(len(GROUPS)):
            advance(group, stage)
        if stage < 3:
            small_copies = small_stage(stage + 1, small_sum(stage, small_copies))
        elif stage == 3:
            small_out_ref[...] = small_sum(3, small_copies)
    for slot in back:
        back[slot].wait_recv()
    for copy in started:
        copy.wait_send()


def finish_kernel(
    ret_ref, sum_ref, small_ref, perm_ref,
    mixed_hbm, gtok_hbm, gqkv_hbm, gproj_hbm, gain_ref, gscale_ref,
    mixed_s, gtok_s, gqkv_s, gproj_s, sems,
):
    copies = []

    def write_out(src, dst):
        copies.append(pltpu.make_async_copy(src, dst, sems.at[len(copies)]))
        copies[-1].start()

    for b in (3, 0, 1, 2):
        for half in range(2):
            rows = slice(half * 256, (half + 1) * 256)
            for ct in range(4):
                first = b * 1024 + ct * 256
                tile = sum_ref[half, first : first + 256].astype(F32)
                if b < 3:
                    gqkv_s[b, rows, ct * 128 : (ct + 1) * 128] = tile
                else:
                    gproj_s[rows, ct * 128 : (ct + 1) * 128] = tile
            where = pl.ds(half * 256, 256)
            if b < 3:
                write_out(gqkv_s.at[b, where], gqkv_hbm.at[where, pl.ds(b * 512, 512)])
            else:
                write_out(gproj_s.at[where], gproj_hbm.at[where])
    ret = ret_ref[...].astype(F32)
    perm = perm_ref[...]
    mixed = jnp.concatenate([ret[0], ret[2]] + [ret[slot][:QT] for slot in (4, 5, 6, 7)], axis=0).astype(BF)
    mixed_s[...] = dot(perm, mixed, 0, 0).astype(BF)
    write_out(mixed_s, mixed_hbm)
    gtok = jnp.concatenate([ret[1], ret[3]] + [ret[slot][QT:] for slot in (4, 5, 6, 7)], axis=0).astype(BF)
    gtok_s[...] = dot(perm, gtok, 0, 0).astype(BF)
    write_out(gtok_s, gtok_hbm)
    for i in range(4):
        gain_ref[:, i * 128 : (i + 1) * 128] = small_ref[i : i + 1, :]
    eye = lax.broadcasted_iota(jnp.int32, (8, 128), 0) == lax.broadcasted_iota(jnp.int32, (8, 128), 1)
    row = jnp.sum(jnp.where(eye, small_ref[8:16, :], 0.0), axis=0, keepdims=True)
    gscale_ref[...] = row[:, :8]
    for copy in copies:
        copy.wait()


VM = pl.BlockSpec(memory_space=pltpu.VMEM)
HBM = pl.BlockSpec(memory_space=pltpu.HBM)
DMA = pltpu.SemaphoreType.DMA
MIB = 1024 * 1024


def per_device(tokens, cotangent, key_keep, norm_gain, w_qkv, w_proj, attn_scale):
    perm, member, place = tables()
    perm = jnp.asarray(perm, BF)
    x = tokens.reshape(288, 512)
    g = cotangent.reshape(288, 512)
    operands = (
        x, g, key_keep.transpose(1, 0, 2), perm, jnp.asarray(member, BF), jnp.asarray(place, BF),
        w_qkv, w_proj, norm_gain.reshape(1, 512),
    )
    operands = [pltpu.with_memory_space_constraint(operand, pltpu.HBM) for operand in operands]
    win, wqkv_near, wproj_near, gain_near = pl.pallas_call(
        shift_in_kernel,
        out_shape=(
            jax.ShapeDtypeStruct((8, ROWS, 512), BF),
            jax.ShapeDtypeStruct((512, 1536), BF),
            jax.ShapeDtypeStruct((512, 512), BF),
            jax.ShapeDtypeStruct((1, 512), F32),
        ),
        in_specs=[HBM] * 9,
        out_specs=(VM,) * 4,
        scratch_shapes=[
            pltpu.VMEM((288, 512), BF),
            pltpu.VMEM((288, 512), BF),
            pltpu.VMEM((6, 2, 24), jnp.int32),
            pltpu.VMEM((8 * QT, 288), BF),
            pltpu.VMEM((8, 288), BF),
            pltpu.VMEM((288, 256), BF),
            pltpu.VMEM((5, ROWS, 512), BF),
            DMA((9,)),
            DMA((5,)),
            DMA((5,)),
        ],
        compiler_params=pltpu.CompilerParams(collective_id=1, has_side_effects=True, vmem_limit_bytes=12 * MIB),
        name="shift_in",
    )(*operands)

    tok = (2 * WIN, 512)
    back, grads, small = pl.pallas_call(
        compute_kernel,
        out_shape=(
            jax.ShapeDtypeStruct((8, ROWS, 512), BF),
            jax.ShapeDtypeStruct((2, 4096, 128), BF),
            jax.ShapeDtypeStruct((16, 128), F32),
        ),
        in_specs=[VM, VM, VM, VM, HBM],
        out_specs=(VM, VM, VM),
        scratch_shapes=[pltpu.SMEM((8,), F32), DMA] + [pltpu.VMEM(tok, BF)] * 4
        + [pltpu.VMEM(tok, F32)] * 2
        + [pltpu.VMEM(tok, BF)] * 2
        + [pltpu.VMEM((2, WIN, WIN), F32), pltpu.VMEM((8, 2, WIN), F32)],
        compiler_params=pltpu.CompilerParams(vmem_limit_bytes=32 * MIB),
        name="windows",
    )(win, wqkv_near, wproj_near, gain_near, pltpu.with_memory_space_constraint(attn_scale, pltpu.HBM))

    ret, total, small = pl.pallas_call(
        reduce_kernel,
        out_shape=(
            jax.ShapeDtypeStruct((8, ROWS, 512), BF),
            jax.ShapeDtypeStruct((2, 4096, 128), BF),
            jax.ShapeDtypeStruct((16, 128), F32),
        ),
        in_specs=[VM] * 3,
        out_specs=(VM,) * 3,
        scratch_shapes=[
            pltpu.VMEM((4096, 128), BF),
            pltpu.VMEM((4096, 128), BF),
            pltpu.VMEM((3, 1024, 128), BF),
            pltpu.VMEM((1024, 128), BF),
            pltpu.VMEM((3, 256, 128), BF),
            pltpu.VMEM((4, 256, 128), BF),
            pltpu.VMEM((2, 16, 128), F32),
            pltpu.VMEM((4, 16, 128), F32),
            pltpu.VMEM((4, 16, 128), F32),
            pltpu.VMEM((4, 16, 128), F32),
            DMA((5,)), DMA((5,)),
            DMA((12,)), DMA((12,)),
            DMA((6, 5, 3)), DMA((6, 5, 3)),
            DMA((10,)), DMA((10,)),
        ],
        compiler_params=pltpu.CompilerParams(collective_id=2, has_side_effects=True, vmem_limit_bytes=24 * MIB),
        name="reduce_grads",
    )(back, grads, small)

    mixed, gtok, gqkv, gproj, gain, gscale = pl.pallas_call(
        finish_kernel,
        out_shape=(
            jax.ShapeDtypeStruct((288, 512), BF),
            jax.ShapeDtypeStruct((288, 512), BF),
            jax.ShapeDtypeStruct((512, 1536), F32),
            jax.ShapeDtypeStruct((512, 512), F32),
            jax.ShapeDtypeStruct((1, 512), F32),
            jax.ShapeDtypeStruct((1, 8), F32),
        ),
        in_specs=[VM] * 4,
        out_specs=(HBM,) * 4 + (VM,) * 2,
        scratch_shapes=[
            pltpu.VMEM((288, 512), BF),
            pltpu.VMEM((288, 512), BF),
            pltpu.VMEM((3, 512, 512), F32),
            pltpu.VMEM((512, 512), F32),
            DMA((10,)),
        ],
        compiler_params=pltpu.CompilerParams(vmem_limit_bytes=24 * MIB),
        name="finish",
    )(ret, total, small, perm)
    return (
        mixed.reshape(tokens.shape),
        gtok.reshape(tokens.shape),
        gqkv,
        gproj,
        gain.reshape(512),
        gscale.reshape(8),
    )


def solution(mesh):
    grid = P(None, "lat", "lon", None)
    return jax.shard_map(
        per_device,
        mesh=mesh,
        in_specs=(grid, grid, P(None, "lat", "lon"), P(), P(), P(), P()),
        out_specs=(grid, grid, P(), P(), P(), P()),
        check_vma=False,
    )
```

```python
import functools

import jax
import jax.numpy as jnp
import numpy as np
from jax import lax
from jax.experimental import pallas as pl
from jax.experimental.pallas import tpu as pltpu
from jax.sharding import PartitionSpec as P

EPS_NORM = 1e-05
EPS_DIR = 1e-06
MESH = pl.DeviceIdType.MESH
BF = jnp.bfloat16
F32 = jnp.float32

QUARTERS = ((1, 1), (1, 2), (0, 1), (0, 2), (1, 3), (1, 0), (0, 3), (0, 0))
QT = 40
ROWS = 80
WIN = 160
FLAG_ROW = 36


def token_of(quarter, t):
    half, cq = QUARTERS[quarter]
    lev, rest = divmod(t, 18)
    rr, cc = divmod(rest, 6)
    return lev * 144 + (half * 3 + rr) * 24 + cq * 6 + cc


def tables():
    perm = np.zeros((8 * QT, 288), np.float32)
    member = np.zeros((8, 288), np.float32)
    place = np.zeros((288, 256), np.float32)
    for quarter in range(8):
        for t in range(36):
            src = token_of(quarter, t)
            perm[quarter * QT + t, src] = 1.0
            member[quarter, src] = 1.0
            place[src, QT * (quarter % 4) + t] = 1.0
    return perm, member, place


def dot(a, b, ca=1, cb=0):
    return lax.dot_general(a, b, (((ca,), (cb,)), ((), ())), preferred_element_type=F32)


def position():
    lat = lax.axis_index("lat")
    lon = lax.axis_index("lon")
    return lat, lon


def wrap(value, count):
    return lax.rem(value + count, count)


SLOT_SENDS = ((2, "lat"), (5, "lon"), (7, "diag"), (6, "lat"), (3, "lat"))
KEPT_SLOTS = (0, 1, 4)

GROUPS = (
    (0, 768, "xzy"),
    (768, 512, "yxz"),
    (1280, 768, "zyx"),
    (2048, 768, "xzy"),
    (2816, 512, "yxz"),
    (3328, 768, "zyx"),
)
WAVES = ((0, 1, 2), (3, 4, 5))


def slot_pieces(slot):
    if slot < 4:
        first = 2 * (slot // 2)
        kind = "xg"[slot % 2]
        return ((kind, first), (kind, first + 1))
    return (("x", slot), ("g", slot))


def coordinates():
    lat, lon = position()
    core = lax.rem(lat, 2)
    y = (lat // 2) * 2 + lon // 16
    x = lax.rem(lon // 4, 4)
    z = lax.rem(lon, 4)
    return {"x": x, "y": y, "z": z, "core": core}


def device_at(co):
    return ((co["y"] // 2) * 2 + co["core"], lax.rem(co["y"], 2) * 16 + co["x"] * 4 + co["z"])


def peer(co, axis, j):
    moved = dict(co)
    moved[axis] = lax.rem(co[axis] + j, 4)
    return device_at(moved)


def sibling(co):
    moved = dict(co)
    moved["core"] = 1 - co["core"]
    return device_at(moved)


def block_kernel(
    x_hbm, g_hbm, keep_hbm, perm_hbm, member_hbm, place_hbm, wqkv_hbm, wproj_hbm, gain_hbm, scale_hbm,
    ret_ref, sum_ref, small_out_ref,
    x_ref, g_ref, keep_ref, perm_ref, member_ref, place_ref, wqkv_ref, wproj_ref, gain_ref, scale_ref, in_buf, win_ref, back_ref,
    x_s, xh_s, rstd_s, y_s, g_s, rq_s, rk_s, rq_rows_s, q_s, k_s, qd_s, kd_s, v_s, do_s, dq_s, dk_s, dv_s, att_s, allow_s, gs_s, small_s,
    grads_ref, r0, a1, r1, a2, r2, a3, sv0, sv1, sv2, sv3,
    w_sem, in_send, in_recv, out_send, out_recv, sib_send, sib_recv, st_send, st_recv, sv_send, sv_recv,
):
    lat, lon = position()
    lat_lo, lat_hi = wrap(lat - 1, 4), wrap(lat + 1, 4)
    lon_lo, lon_hi = wrap(lon - 1, 32), wrap(lon + 1, 32)
    co = coordinates()
    core = co["core"]
    sib = sibling(co)
    peers = {axis: [peer(co, axis, j) for j in (1, 2, 3)] for axis in "xyz"}

    loads = {}
    for i, (name, src, dst) in enumerate((
        ("perm", perm_hbm, perm_ref),
        ("x", x_hbm, x_ref),
        ("keep", keep_hbm, keep_ref),
        ("member", member_hbm, member_ref),
        ("place", place_hbm, place_ref),
        ("g", g_hbm, g_ref),
        ("gain", gain_hbm, gain_ref),
        ("qkv", wqkv_hbm, wqkv_ref),
        ("proj", wproj_hbm, wproj_ref),
        ("scale", scale_hbm, scale_ref),
    )):
        loads[name] = pltpu.make_async_copy(src, dst, w_sem.at[i])
        loads[name].start()

    barrier = pltpu.get_barrier_semaphore()
    greet = [(lat_lo, lon), (lat, lon_lo), (lat_lo, lon_lo), (lat_hi, lon), (lat, lon_hi), (lat_hi, lon_hi), sib]
    for axis in "xyz":
        greet.extend(peers[axis])
    for dev in greet:
        pl.semaphore_signal(barrier, inc=1, device_id=dev, device_id_type=MESH)

    started = []

    def send(src, dst, s_sem, r_sem, dev):
        copy = pltpu.make_async_remote_copy(
            src_ref=src, dst_ref=dst, send_sem=s_sem, recv_sem=r_sem, device_id=dev, device_id_type=MESH
        )
        copy.start()
        started.append(copy)
        return copy

    for name in ("perm", "x", "keep", "member", "place", "g"):
        loads[name].wait()
    perm = perm_ref[...]
    xs = dot(perm, x_ref[...])
    gs = dot(perm, g_ref[...])
    keep_rows = [keep_ref[row, lev : lev + 1, :].astype(F32) for lev in range(2) for row in range(6)]
    marks = (jnp.concatenate(keep_rows, axis=1) * member_ref[...].astype(F32)).astype(BF)
    flags = dot(marks, place_ref[...])
    row_id = lax.broadcasted_iota(jnp.int32, (QT, 512), 0)

    def piece(kind, quarter):
        rows = slice(quarter * QT, (quarter + 1) * QT)
        if kind == "g":
            return gs[rows]
        flag = jnp.concatenate([flags[quarter : quarter + 1], jnp.zeros((1, 256), F32)], axis=1)
        return jnp.where(row_id == FLAG_ROW, flag, xs[rows])

    def payload(slot):
        return jnp.concatenate([piece(*p) for p in slot_pieces(slot)], axis=0).astype(BF)

    for i, (slot, _) in enumerate(SLOT_SENDS):
        in_buf[i] = payload(slot)
    pl.semaphore_wait(barrier, len(greet))
    low = {"lat": (lat_lo, lon), "lon": (lat, lon_lo), "diag": (lat_lo, lon_lo)}
    high = {"lat": (lat_hi, lon), "lon": (lat, lon_hi), "diag": (lat_hi, lon_hi)}
    arrive = {}
    for i, (slot, way) in enumerate(SLOT_SENDS):
        arrive[slot] = send(in_buf.at[i], win_ref.at[slot], in_send.at[i], in_recv.at[i], low[way])
    for slot in KEPT_SLOTS:
        win_ref[slot] = payload(slot)
    loads["gain"].wait()
    loads["qkv"].wait()

    gain = gain_ref[...]
    r = lax.broadcasted_iota(jnp.int32, (256, 256), 0)
    c = lax.broadcasted_iota(jnp.int32, (256, 256), 1)
    ones = jnp.where((r // 64) == (c // 64), 1.0, 0.0).astype(BF)

    r = lax.broadcasted_iota(jnp.int32, (8, 512), 0)
    c = lax.broadcasted_iota(jnp.int32, (8, 512), 1)
    head_of = jnp.where(r == c // 64, 1.0, 0.0).astype(BF)

    def head_sum(values):
        hi = values.astype(BF)
        lo = (values - hi.astype(F32)).astype(BF)
        halves = [dot(hi[:, i : i + 256], ones) + dot(lo[:, i : i + 256], ones) for i in (0, 256)]
        return jnp.concatenate(halves, axis=1)

    real = lax.broadcasted_iota(jnp.int32, (QT, 512), 0) < 36
    key_id = lax.broadcasted_iota(jnp.int32, (WIN, WIN), 0)
    query_id = lax.broadcasted_iota(jnp.int32, (WIN, WIN), 1)
    same_half = (key_id >= 2 * QT) == (query_id >= 2 * QT)
    joined = jnp.logical_or(same_half, lat != 3)
    first_row = lax.broadcasted_iota(jnp.int32, (8, WIN), 0) == 0
    one_row = jnp.where(first_row, 1.0, 0.0).astype(BF)

    def front(w):
        rows = slice(w * WIN, (w + 1) * WIN)
        if w == 0:
            data = jnp.concatenate([win_ref[0].astype(F32), win_ref[2].astype(F32)], axis=0)
        else:
            data = jnp.concatenate([win_ref[slot].astype(F32)[:QT] for slot in (4, 5, 6, 7)], axis=0)
        data = data.reshape(4, QT, 512)
        x = jnp.where(real[None], data, 0.0).reshape(WIN, 512)
        marks = data[0, FLAG_ROW : FLAG_ROW + 1, :]
        for i in range(1, 4):
            marks = marks + data[i, FLAG_ROW : FLAG_ROW + 1, :]
        marks = jnp.where(first_row, marks[:, :WIN], 0.0).astype(BF)
        keep = jnp.where(joined, dot(marks, one_row, 0, 0), 0.0)
        allow_s[w] = jnp.where(key_id == query_id, 1.0, keep)
        mean = jnp.mean(x, axis=-1, keepdims=True)
        xc = x - mean
        var = jnp.mean(xc * xc, axis=-1, keepdims=True)
        rstd = lax.rsqrt(var + EPS_NORM)
        xhat = xc * rstd
        y = (xhat * gain).astype(BF)
        x_s[rows] = x
        xh_s[rows] = xhat
        rstd_s[rows] = jnp.broadcast_to(rstd, (WIN, 128))
        y_s[rows] = y
        q_b = dot(y, wqkv_ref[:, 0:512]).astype(BF)
        k_b = dot(y, wqkv_ref[:, 512:1024]).astype(BF)
        q_s[rows] = q_b
        k_s[rows] = k_b
        q = q_b.astype(F32)
        k = k_b.astype(F32)
        v_s[rows] = dot(y, wqkv_ref[:, 1024:1536]).astype(BF)
        q_sq = q * q
        rq = lax.rsqrt(head_sum(q_sq) + EPS_DIR)
        sq_hi = q_sq.astype(BF)
        sq_lo = (q_sq - sq_hi.astype(F32)).astype(BF)
        rq_rows_s[w] = lax.rsqrt(dot(head_of, sq_hi, 1, 1) + dot(head_of, sq_lo, 1, 1) + EPS_DIR)
        rk = lax.rsqrt(head_sum(k * k) + EPS_DIR)
        rq_s[rows] = rq
        rk_s[rows] = rk
        qd_s[rows] = (q * rq).astype(BF)
        kd_s[rows] = (k * rk).astype(BF)

    arrive[2].wait_recv()
    front(0)
    for slot in (5, 7, 6):
        arrive[slot].wait_recv()
    front(1)
    arrive[3].wait_recv()
    g = jnp.concatenate(
        [win_ref[1].astype(F32), win_ref[3].astype(F32)] + [win_ref[slot].astype(F32)[QT:] for slot in (4, 5, 6, 7)],
        axis=0,
    ).astype(BF)
    g_s[...] = g
    loads["proj"].wait()
    loads["scale"].wait()
    do_s[...] = dot(g, wproj_ref[...], 1, 1).astype(BF)
    y_t = jnp.transpose(y_s[...])

    flight = {}

    def send_stage(group, stage, axis, pairs):
        copies = []
        for j in range(3):
            src, dst = pairs(j)
            index = (group, stage, j)
            copies.append(send(src, dst, st_send.at[index], st_recv.at[index], peers[axis][j]))
        flight[group] = copies

    def arrived(group):
        for copy in flight[group]:
            copy.wait_recv()

    def size_of(group, level):
        return GROUPS[group][1] // (4, 16)[level]

    def start_of(group, level):
        return GROUPS[group][0] // (1, 4)[level]

    def own_rows(group, level, j=0):
        first, size = start_of(group, level), size_of(group, level)
        turn = lax.rem(co[GROUPS[group][2][level]] + j, 4)
        return pl.ds(pl.multiple_of(first + turn * size, 16), size)

    def landing(group, level):
        return pl.ds(GROUPS[group][0] // (4, 16)[level], size_of(group, level))

    def scatter(group, level, src, dst):
        def pairs(j):
            return src.at[own_rows(group, level, j + 1)], dst.at[j, landing(group, level)]

        send_stage(group, level, GROUPS[group][2][level], pairs)

    def gathered(group, level, src, dst):
        arrived(group)
        total = src[own_rows(group, level)].astype(F32)
        for j in range(3):
            total = total + dst[j, landing(group, level)].astype(F32)
        return total.astype(BF)

    def final_rows(group, level):
        first, rows, axes = GROUPS[group]
        off = first + co[axes[0]] * (rows // 4)
        if level == 1:
            off = off + co[axes[1]] * (rows // 16)
        return pl.ds(pl.multiple_of(off, 16), size_of(group, level))

    def spread(group, level):
        where = sum_ref.at[core, final_rows(group, level)]
        send_stage(group, 4 - level, GROUPS[group][2][level], lambda j: (where, where))

    sib_in = {}

    def begin(part):
        rows = pl.ds(part * 1024, 1024)
        sib_in[part] = send(grads_ref.at[1 - core, rows], r0.at[rows], sib_send.at[part], sib_recv.at[part], sib)

    def join(part):
        sib_in[part].wait_recv()
        rows = pl.ds(part * 1024, 1024)
        a1[rows] = (grads_ref[core, rows].astype(F32) + r0[rows].astype(F32)).astype(BF)

    def advance(group, stage):
        if stage == 0:
            scatter(group, 0, a1, r1)
        elif stage == 1:
            a2[landing(group, 0)] = gathered(group, 0, a1, r1)
            scatter(group, 1, a2, r2)
        elif stage == 2:
            me = co[GROUPS[group][2][2]]
            a3[me, landing(group, 1)] = gathered(group, 1, a2, r2)
            here = a3.at[me, landing(group, 1)]
            send_stage(group, 2, GROUPS[group][2][2], lambda j: (here, here))
        elif stage == 3:
            arrived(group)
            total = a3[0, landing(group, 1)].astype(F32)
            for i in range(1, 4):
                total = total + a3[i, landing(group, 1)].astype(F32)
            sum_ref[core, final_rows(group, 1)] = total.astype(BF)
            spread(group, 1)
        elif stage == 4:
            arrived(group)
            spread(group, 0)
        elif stage == 5:
            arrived(group)
            whole = sum_ref.at[core, pl.ds(GROUPS[group][0], GROUPS[group][1])]
            flight[group] = [send(whole, whole, sib_send.at[4 + group], sib_recv.at[4 + group], sib)]
        else:
            arrived(group)

    def advance_wave(wave, stage):
        for group in WAVES[wave]:
            advance(group, stage)

    lane = lax.broadcasted_iota(jnp.int32, (1, 128), 1)
    small_ones = ones[:128, :128]

    def pair_of_heads(pair):
        cols = slice(pair * 128, (pair + 1) * 128)
        scales = [scale_ref[pair * 2 + i] for i in range(2)]
        s_lane = jnp.where(lane < 64, scales[0], scales[1])

        def window(w):
            rows = slice(w * WIN, (w + 1) * WIN)
            q_p = q_s[rows, cols]
            k_p = k_s[rows, cols]
            qd_p = qd_s[rows, cols]
            kd_p = kd_s[rows, cols]
            v_p = v_s[rows, cols]
            do_p = do_s[rows, cols]
            allow = allow_s[w]
            acc_o = jnp.zeros((WIN, 128), F32)
            acc_q = jnp.zeros((WIN, 128), F32)
            acc_k = jnp.zeros((WIN, 128), F32)
            acc_v = jnp.zeros((WIN, 128), F32)
            zero = jnp.zeros((WIN, 128), BF)
            for i in range(2):
                s = scales[i]
                mine = jnp.broadcast_to((lane < 64) if i == 0 else (lane >= 64), (WIN, 128))
                qd_h = jnp.where(mine, qd_p, zero)
                kd_h = jnp.where(mine, kd_p, zero)
                v_h = jnp.where(mine, v_p, zero)
                do_h = jnp.where(mine, do_p, zero)
                rq_row = rq_rows_s[w, pair * 2 + i : pair * 2 + i + 1, :]
                rk_col = rk_s[rows, pair * 128 + i * 64 : pair * 128 + i * 64 + 1]
                cos = dot(k_p, jnp.where(mine, q_p, zero), 1, 1) * rk_col * rq_row
                e = jnp.exp(s * cos - s) * allow
                p = e * (1.0 / jnp.sum(e, axis=0, keepdims=True))
                dp = dot(v_p, do_h, 1, 1)
                dl = p * (dp - jnp.sum(p * dp, axis=0, keepdims=True))
                gs_s[w * 4 + pair, i : i + 1, :] = jnp.sum(dl * cos, axis=0, keepdims=True)
                p_b = p.astype(BF)
                dl_b = dl.astype(BF)
                acc_o = acc_o + dot(p_b, v_h, 0, 0)
                acc_v = acc_v + dot(p_b, do_h)
                acc_k = acc_k + dot(dl_b, qd_h)
                acc_q = acc_q + dot(dl_b, kd_h, 0, 0)
            att_s[rows, cols] = acc_o.astype(BF)
            dv_s[rows, cols] = acc_v.astype(BF)
            qd = qd_p.astype(F32)
            kd = kd_p.astype(F32)
            dqd = acc_q * s_lane
            dkd = acc_k * s_lane
            dq_s[rows, cols] = (rq_s[rows, cols] * (dqd - qd * dot((qd * dqd).astype(BF), small_ones))).astype(BF)
            dk_s[rows, cols] = (rk_s[rows, cols] * (dkd - kd * dot((kd * dkd).astype(BF), small_ones))).astype(BF)

        window(0)
        window(1)
        d_all = jnp.concatenate([dq_s[:, cols], dk_s[:, cols], dv_s[:, cols]], axis=1)
        gq = dot(y_t, d_all).astype(BF)
        gp = dot(att_s[:, cols], g_s[...], 0, 0).astype(BF)
        for half in range(2):
            for i in range(3):
                first = pair * 1024 + i * 256
                grads_ref[half, first : first + 256] = gq[half * 256 : (half + 1) * 256, i * 128 : (i + 1) * 128]
            for ct in range(4):
                first = pair * 1024 + 768 + ct * 64
                grads_ref[half, first : first + 64] = gp[half * 64 : (half + 1) * 64, ct * 128 : (ct + 1) * 128]
        begin(pair)

    for pair in range(4):
        pair_of_heads(pair)
        if pair == 2:
            join(0)
            join(1)
            advance_wave(0, 0)

    def out_slot(slot, pieces):
        back_ref[slot] = jnp.concatenate(pieces, axis=0).astype(BF)

    back = {}

    def send_back(slots):
        for i, (slot, way) in enumerate(SLOT_SENDS):
            if slot in slots:
                back[slot] = send(back_ref.at[slot], ret_ref.at[slot], out_send.at[i], out_recv.at[i], high[way])

    mixed = x_s[...] + dot(att_s[...], wproj_ref[...])
    for slot in (0, 2):
        out_slot(slot, [mixed[slot * QT : (slot + 2) * QT]])
    send_back((2,))
    dn = dot(dq_s[...], wqkv_ref[:, 0:512], 1, 1)
    dn = dn + dot(dk_s[...], wqkv_ref[:, 512:1024], 1, 1)
    dn = dn + dot(dv_s[...], wqkv_ref[:, 1024:1536], 1, 1)
    xhat = xh_s[...]
    d_gain = jnp.sum(dn * xhat, axis=0, keepdims=True)
    small_s[...] = jnp.zeros((16, 128), F32)
    for i in range(4):
        small_s[i : i + 1, :] = d_gain[:, i * 128 : (i + 1) * 128]
    for h in range(8):
        row = gs_s[h // 2, h % 2 : h % 2 + 1, :] + gs_s[4 + h // 2, h % 2 : h % 2 + 1, :]
        small_s[8 + h : 9 + h, :] = jnp.broadcast_to(jnp.sum(row, axis=1, keepdims=True), (1, 128))

    def small_stage(stage, values):
        axis = ("core", "x", "y", "z")[stage]
        buf = (sv0, sv1, sv2, sv3)[stage]
        me = co[axis]
        buf[me] = values
        copies = []
        for j, dev in enumerate([sib] if stage == 0 else peers[axis]):
            index = 0 if stage == 0 else 1 + 3 * (stage - 1) + j
            copies.append(send(buf.at[me], buf.at[me], sv_send.at[index], sv_recv.at[index], dev))
        return copies

    def small_sum(stage, copies):
        buf = (sv0, sv1, sv2, sv3)[stage]
        for copy in copies:
            copy.wait_recv()
        total = buf[0]
        for i in range(1, 2 if stage == 0 else 4):
            total = total + buf[i]
        return total

    small_copies = small_stage(0, small_s[...])
    dxh = dn * gain
    rstd = rstd_s[:, 0:1]
    dx = rstd * (dxh - jnp.mean(dxh, axis=-1, keepdims=True) - xhat * jnp.mean(dxh * xhat, axis=-1, keepdims=True))
    gtok = g_s[...].astype(F32) + dx
    for slot in (1, 3):
        out_slot(slot, [gtok[(slot - 1) * QT : (slot + 1) * QT]])
    for slot in (4, 5, 6, 7):
        rows = slice(slot * QT, (slot + 1) * QT)
        out_slot(slot, [mixed[rows], gtok[rows]])
    for slot in KEPT_SLOTS:
        ret_ref[slot] = back_ref[slot]
    join(2)
    join(3)
    advance_wave(1, 0)
    send_back((5, 7, 6, 3))
    for stage in range(1, 7):
        advance_wave(0, stage)
        advance_wave(1, stage)
        if stage < 4:
            small_copies = small_stage(stage, small_sum(stage - 1, small_copies))
        elif stage == 4:
            small_out_ref[...] = small_sum(3, small_copies)
    for slot in back:
        back[slot].wait_recv()
    for copy in started:
        copy.wait_send()


def finish_kernel(ret_ref, sum_ref, small_ref, perm_ref, mixed_ref, gtok_ref, gqkv_ref, gproj_ref, gain_ref, gscale_ref):
    ret = ret_ref[...].astype(F32)
    perm = perm_ref[...]
    mixed = jnp.concatenate([ret[0], ret[2]] + [ret[slot][:QT] for slot in (4, 5, 6, 7)], axis=0).astype(BF)
    gtok = jnp.concatenate([ret[1], ret[3]] + [ret[slot][QT:] for slot in (4, 5, 6, 7)], axis=0).astype(BF)
    mixed_ref[...] = dot(perm, mixed, 0, 0).astype(BF)
    gtok_ref[...] = dot(perm, gtok, 0, 0).astype(BF)
    for half in range(2):
        for p in range(4):
            for i in range(3):
                cols = slice(i * 512 + p * 128, i * 512 + (p + 1) * 128)
                first = p * 1024 + i * 256
                tile = sum_ref[half, first : first + 256]
                gqkv_ref[half * 256 : (half + 1) * 256, cols] = tile.astype(F32)
            for ct in range(4):
                first = p * 1024 + 768 + ct * 64
                tile = sum_ref[half, first : first + 64]
                rows = slice(p * 128 + half * 64, p * 128 + (half + 1) * 64)
                gproj_ref[rows, ct * 128 : (ct + 1) * 128] = tile.astype(F32)
    for i in range(4):
        gain_ref[:, i * 128 : (i + 1) * 128] = small_ref[i : i + 1, :]
    eye = lax.broadcasted_iota(jnp.int32, (8, 128), 0) == lax.broadcasted_iota(jnp.int32, (8, 128), 1)
    row = jnp.sum(jnp.where(eye, small_ref[8:16, :], 0.0), axis=0, keepdims=True)
    gscale_ref[...] = row[:, :8]


VM = pl.BlockSpec(memory_space=pltpu.VMEM)
HBM = pl.BlockSpec(memory_space=pltpu.HBM)
DMA = pltpu.SemaphoreType.DMA
MIB = 1024 * 1024


def per_device(tokens, cotangent, key_keep, norm_gain, w_qkv, w_proj, attn_scale):
    perm, member, place = tables()
    perm = jnp.asarray(perm, BF)
    x = tokens.reshape(288, 512)
    g = cotangent.reshape(288, 512)
    tok = (2 * WIN, 512)
    operands = (
        x, g, key_keep.transpose(1, 0, 2), perm, jnp.asarray(member, BF), jnp.asarray(place, BF),
        w_qkv, w_proj, norm_gain.reshape(1, 512), attn_scale,
    )
    operands = [pltpu.with_memory_space_constraint(operand, pltpu.HBM) for operand in operands]
    ret, total, small = pl.pallas_call(
        block_kernel,
        out_shape=(
            jax.ShapeDtypeStruct((8, ROWS, 512), BF),
            jax.ShapeDtypeStruct((2, 4096, 128), BF),
            jax.ShapeDtypeStruct((16, 128), F32),
        ),
        in_specs=[HBM] * 10,
        out_specs=(VM,) * 3,
        scratch_shapes=[
            pltpu.VMEM((288, 512), BF),
            pltpu.VMEM((288, 512), BF),
            pltpu.VMEM((6, 2, 24), jnp.int32),
            pltpu.VMEM((8 * QT, 288), BF),
            pltpu.VMEM((8, 288), BF),
            pltpu.VMEM((288, 256), BF),
            pltpu.VMEM((512, 1536), BF),
            pltpu.VMEM((512, 512), BF),
            pltpu.VMEM((1, 512), F32),
            pltpu.SMEM((8,), F32),
            pltpu.VMEM((5, ROWS, 512), BF),
            pltpu.VMEM((8, ROWS, 512), BF),
            pltpu.VMEM((8, ROWS, 512), BF),
            pltpu.VMEM(tok, F32),
            pltpu.VMEM(tok, F32),
            pltpu.VMEM((2 * WIN, 128), F32),
            pltpu.VMEM(tok, BF),
            pltpu.VMEM(tok, BF),
            pltpu.VMEM(tok, F32),
            pltpu.VMEM(tok, F32),
        ]
        + [pltpu.VMEM((2, 8, WIN), F32)]
        + [pltpu.VMEM(tok, BF)] * 10
        + [
            pltpu.VMEM((2, WIN, WIN), F32),
            pltpu.VMEM((8, 2, WIN), F32),
            pltpu.VMEM((16, 128), F32),
            pltpu.VMEM((2, 4096, 128), BF),
            pltpu.VMEM((4096, 128), BF),
            pltpu.VMEM((4096, 128), BF),
            pltpu.VMEM((3, 1024, 128), BF),
            pltpu.VMEM((1024, 128), BF),
            pltpu.VMEM((3, 256, 128), BF),
            pltpu.VMEM((4, 256, 128), BF),
            pltpu.VMEM((2, 16, 128), F32),
            pltpu.VMEM((4, 16, 128), F32),
            pltpu.VMEM((4, 16, 128), F32),
            pltpu.VMEM((4, 16, 128), F32),
            DMA((10,)),
            DMA((5,)), DMA((5,)),
            DMA((5,)), DMA((5,)),
            DMA((10,)), DMA((10,)),
            DMA((6, 5, 3)), DMA((6, 5, 3)),
            DMA((10,)), DMA((10,)),
        ],
        compiler_params=pltpu.CompilerParams(collective_id=1, has_side_effects=True, vmem_limit_bytes=40 * MIB),
        name="block",
    )(*operands)

    mixed, gtok, gqkv, gproj, gain, gscale = pl.pallas_call(
        finish_kernel,
        out_shape=(
            jax.ShapeDtypeStruct((288, 512), BF),
            jax.ShapeDtypeStruct((288, 512), BF),
            jax.ShapeDtypeStruct((512, 1536), F32),
            jax.ShapeDtypeStruct((512, 512), F32),
            jax.ShapeDtypeStruct((1, 512), F32),
            jax.ShapeDtypeStruct((1, 8), F32),
        ),
        in_specs=[VM] * 4,
        out_specs=(VM,) * 6,
        compiler_params=pltpu.CompilerParams(vmem_limit_bytes=24 * MIB),
        name="finish",
    )(ret, total, small, perm)
    return (
        mixed.reshape(tokens.shape),
        gtok.reshape(tokens.shape),
        gqkv,
        gproj,
        gain.reshape(512),
        gscale.reshape(8),
    )


def solution(mesh):
    grid = P(None, "lat", "lon", None)
    return jax.shard_map(
        per_device,
        mesh=mesh,
        in_specs=(grid, grid, P(None, "lat", "lon"), P(), P(), P(), P()),
        out_specs=(grid, grid, P(), P(), P(), P()),
        check_vma=False,
    )
```

```python
import functools

import jax
import jax.numpy as jnp
import numpy as np
from jax import lax
from jax.experimental import pallas as pl
from jax.experimental.pallas import tpu as pltpu
from jax.sharding import PartitionSpec as P

EPS_NORM = 1e-05
EPS_DIR = 1e-06
MESH = pl.DeviceIdType.MESH
BF = jnp.bfloat16
F32 = jnp.float32

QUARTERS = ((1, 1), (1, 2), (0, 1), (0, 2), (1, 3), (1, 0), (0, 3), (0, 0))
QT = 40
ROWS = 80
WIN = 160
FLAG_ROW = 36


def token_of(quarter, t):
    half, cq = QUARTERS[quarter]
    lev, rest = divmod(t, 18)
    rr, cc = divmod(rest, 6)
    return lev * 144 + (half * 3 + rr) * 24 + cq * 6 + cc


def tables():
    perm = np.zeros((8 * QT, 288), np.float32)
    member = np.zeros((8, 288), np.float32)
    place = np.zeros((288, 256), np.float32)
    for quarter in range(8):
        for t in range(36):
            src = token_of(quarter, t)
            perm[quarter * QT + t, src] = 1.0
            member[quarter, src] = 1.0
            place[src, QT * (quarter % 4) + t] = 1.0
    return perm, member, place


def dot(a, b, ca=1, cb=0):
    return lax.dot_general(a, b, (((ca,), (cb,)), ((), ())), preferred_element_type=F32)


def position():
    lat = lax.axis_index("lat")
    lon = lax.axis_index("lon")
    return lat, lon


def wrap(value, count):
    return lax.rem(value + count, count)


SLOT_SENDS = ((2, "lat"), (5, "lon"), (7, "diag"), (6, "lat"), (3, "lat"))
KEPT_SLOTS = (0, 1, 4)

GROUPS = (
    (0, 704, "xzy"),
    (704, 640, "yxz"),
    (1344, 704, "zyx"),
    (2048, 384, "xzy"),
    (2432, 256, "yxz"),
    (2688, 384, "zyx"),
    (3072, 384, "xzy"),
    (3456, 256, "yxz"),
    (3712, 384, "zyx"),
)
WAVES = ((0, 1, 2), (3, 4, 5), (6, 7, 8))
WAVE_PAIRS = ((0, 1), (2,), (3,))


def slot_pieces(slot):
    if slot < 4:
        first = 2 * (slot // 2)
        kind = "xg"[slot % 2]
        return ((kind, first), (kind, first + 1))
    return (("x", slot), ("g", slot))


def coordinates():
    lat, lon = position()
    core = lax.rem(lat, 2)
    y = (lat // 2) * 2 + lon // 16
    x = lax.rem(lon // 4, 4)
    z = lax.rem(lon, 4)
    return {"x": x, "y": y, "z": z, "core": core}


def device_at(co):
    return ((co["y"] // 2) * 2 + co["core"], lax.rem(co["y"], 2) * 16 + co["x"] * 4 + co["z"])


def peer(co, axis, j):
    moved = dict(co)
    moved[axis] = lax.rem(co[axis] + j, 4)
    return device_at(moved)


def sibling(co):
    moved = dict(co)
    moved["core"] = 1 - co["core"]
    return device_at(moved)


def block_kernel(
    x_hbm, g_hbm, keep_hbm, perm_hbm, member_hbm, place_hbm, wqkv_hbm, wproj_hbm, gain_hbm, scale_hbm,
    mixed_ref, gtok_ref, gqkv_ref, gproj_ref, gain_out_ref, gscale_ref,
    ret_ref, sum_ref,
    x_ref, g_ref, keep_ref, perm_ref, member_ref, place_ref, wqkv_ref, wproj_ref, gain_ref, scale_ref, in_buf, win_ref, back_ref,
    x_s, xh_s, rstd_s, y_s, g_s, rq_s, rk_s, rq_rows_s, q_s, k_s, qd_s, kd_s, v_s, do_s, dq_s, dk_s, dv_s, att_s, allow_s, gs_s, small_s,
    grads_ref, r0, a1, r1, a2, a3, sv0, sv1, sv2, sv3,
    w_sem, in_send, in_recv, out_send, out_recv, sib_send, sib_recv, st_send, st_recv, sv_send, sv_recv,
):
    lat, lon = position()
    lat_lo, lat_hi = wrap(lat - 1, 4), wrap(lat + 1, 4)
    lon_lo, lon_hi = wrap(lon - 1, 32), wrap(lon + 1, 32)
    co = coordinates()
    core = co["core"]
    sib = sibling(co)
    peers = {axis: [peer(co, axis, j) for j in (1, 2, 3)] for axis in "xyz"}

    loads = {}
    for i, (name, src, dst) in enumerate((
        ("perm", perm_hbm, perm_ref),
        ("x", x_hbm, x_ref),
        ("keep", keep_hbm, keep_ref),
        ("member", member_hbm, member_ref),
        ("place", place_hbm, place_ref),
        ("g", g_hbm, g_ref),
        ("gain", gain_hbm, gain_ref),
        ("qkv", wqkv_hbm, wqkv_ref),
        ("proj", wproj_hbm, wproj_ref),
        ("scale", scale_hbm, scale_ref),
    )):
        loads[name] = pltpu.make_async_copy(src, dst, w_sem.at[i])
        loads[name].start()

    barrier = pltpu.get_barrier_semaphore()
    greet = [(lat_lo, lon), (lat, lon_lo), (lat_lo, lon_lo), (lat_hi, lon), (lat, lon_hi), (lat_hi, lon_hi), sib]
    for axis in "xyz":
        greet.extend(peers[axis])
    for dev in greet:
        pl.semaphore_signal(barrier, inc=1, device_id=dev, device_id_type=MESH)

    started = []

    def send(src, dst, s_sem, r_sem, dev):
        copy = pltpu.make_async_remote_copy(
            src_ref=src, dst_ref=dst, send_sem=s_sem, recv_sem=r_sem, device_id=dev, device_id_type=MESH
        )
        copy.start()
        started.append(copy)
        return copy

    for name in ("perm", "x", "keep", "member", "place", "g"):
        loads[name].wait()
    perm = perm_ref[...]
    xs = dot(perm, x_ref[...])
    gs = dot(perm, g_ref[...])
    keep_rows = [keep_ref[row, lev : lev + 1, :].astype(F32) for lev in range(2) for row in range(6)]
    marks = (jnp.concatenate(keep_rows, axis=1) * member_ref[...].astype(F32)).astype(BF)
    flags = dot(marks, place_ref[...])
    row_id = lax.broadcasted_iota(jnp.int32, (QT, 512), 0)

    def piece(kind, quarter):
        rows = slice(quarter * QT, (quarter + 1) * QT)
        if kind == "g":
            return gs[rows]
        flag = jnp.concatenate([flags[quarter : quarter + 1], jnp.zeros((1, 256), F32)], axis=1)
        return jnp.where(row_id == FLAG_ROW, flag, xs[rows])

    def payload(slot):
        return jnp.concatenate([piece(*p) for p in slot_pieces(slot)], axis=0).astype(BF)

    for i, (slot, _) in enumerate(SLOT_SENDS):
        in_buf[i] = payload(slot)
    pl.semaphore_wait(barrier, len(greet))
    low = {"lat": (lat_lo, lon), "lon": (lat, lon_lo), "diag": (lat_lo, lon_lo)}
    high = {"lat": (lat_hi, lon), "lon": (lat, lon_hi), "diag": (lat_hi, lon_hi)}
    arrive = {}
    for i, (slot, way) in enumerate(SLOT_SENDS):
        arrive[slot] = send(in_buf.at[i], win_ref.at[slot], in_send.at[i], in_recv.at[i], low[way])
    for slot in KEPT_SLOTS:
        win_ref[slot] = payload(slot)
    loads["gain"].wait()
    loads["qkv"].wait()

    gain = gain_ref[...]
    r = lax.broadcasted_iota(jnp.int32, (256, 256), 0)
    c = lax.broadcasted_iota(jnp.int32, (256, 256), 1)
    ones = jnp.where((r // 64) == (c // 64), 1.0, 0.0).astype(BF)

    r = lax.broadcasted_iota(jnp.int32, (8, 512), 0)
    c = lax.broadcasted_iota(jnp.int32, (8, 512), 1)
    head_of = jnp.where(r == c // 64, 1.0, 0.0).astype(BF)

    def head_sum(values):
        hi = values.astype(BF)
        lo = (values - hi.astype(F32)).astype(BF)
        halves = [dot(hi[:, i : i + 256], ones) + dot(lo[:, i : i + 256], ones) for i in (0, 256)]
        return jnp.concatenate(halves, axis=1)

    real = lax.broadcasted_iota(jnp.int32, (QT, 512), 0) < 36
    key_id = lax.broadcasted_iota(jnp.int32, (WIN, WIN), 0)
    query_id = lax.broadcasted_iota(jnp.int32, (WIN, WIN), 1)
    same_half = (key_id >= 2 * QT) == (query_id >= 2 * QT)
    joined = jnp.logical_or(same_half, lat != 3)
    first_row = lax.broadcasted_iota(jnp.int32, (8, WIN), 0) == 0
    one_row = jnp.where(first_row, 1.0, 0.0).astype(BF)

    def front(w):
        rows = slice(w * WIN, (w + 1) * WIN)
        if w == 0:
            data = jnp.concatenate([win_ref[0].astype(F32), win_ref[2].astype(F32)], axis=0)
        else:
            data = jnp.concatenate([win_ref[slot].astype(F32)[:QT] for slot in (4, 5, 6, 7)], axis=0)
        data = data.reshape(4, QT, 512)
        x = jnp.where(real[None], data, 0.0).reshape(WIN, 512)
        marks = data[0, FLAG_ROW : FLAG_ROW + 1, :]
        for i in range(1, 4):
            marks = marks + data[i, FLAG_ROW : FLAG_ROW + 1, :]
        marks = jnp.where(first_row, marks[:, :WIN], 0.0).astype(BF)
        keep = jnp.where(joined, dot(marks, one_row, 0, 0), 0.0)
        allow_s[w] = jnp.where(key_id == query_id, 1.0, keep)
        mean = jnp.mean(x, axis=-1, keepdims=True)
        xc = x - mean
        var = jnp.mean(xc * xc, axis=-1, keepdims=True)
        rstd = lax.rsqrt(var + EPS_NORM)
        xhat = xc * rstd
        y = (xhat * gain).astype(BF)
        x_s[rows] = x
        xh_s[rows] = xhat
        rstd_s[rows] = jnp.broadcast_to(rstd, (WIN, 128))
        y_s[rows] = y
        q_b = dot(y, wqkv_ref[:, 0:512]).astype(BF)
        k_b = dot(y, wqkv_ref[:, 512:1024]).astype(BF)
        q_s[rows] = q_b
        k_s[rows] = k_b
        q = q_b.astype(F32)
        k = k_b.astype(F32)
        v_s[rows] = dot(y, wqkv_ref[:, 1024:1536]).astype(BF)
        q_sq = q * q
        rq = lax.rsqrt(head_sum(q_sq) + EPS_DIR)
        sq_hi = q_sq.astype(BF)
        sq_lo = (q_sq - sq_hi.astype(F32)).astype(BF)
        rq_rows_s[w] = lax.rsqrt(dot(head_of, sq_hi, 1, 1) + dot(head_of, sq_lo, 1, 1) + EPS_DIR)
        rk = lax.rsqrt(head_sum(k * k) + EPS_DIR)
        rq_s[rows] = rq
        rk_s[rows] = rk
        qd_s[rows] = (q * rq).astype(BF)
        kd_s[rows] = (k * rk).astype(BF)

    arrive[2].wait_recv()
    front(0)
    for slot in (5, 7, 6):
        arrive[slot].wait_recv()
    front(1)
    arrive[3].wait_recv()
    g = jnp.concatenate(
        [win_ref[1].astype(F32), win_ref[3].astype(F32)] + [win_ref[slot].astype(F32)[QT:] for slot in (4, 5, 6, 7)],
        axis=0,
    ).astype(BF)
    g_s[...] = g
    loads["proj"].wait()
    loads["scale"].wait()
    do_s[...] = dot(g, wproj_ref[...], 1, 1).astype(BF)
    y_t = jnp.transpose(y_s[...])

    flight = {}

    def send_stage(group, stage, axis, pairs):
        copies = []
        for j in range(3):
            src, dst = pairs(j)
            index = (group, stage, j)
            copies.append(send(src, dst, st_send.at[index], st_recv.at[index], peers[axis][j]))
        flight[group] = copies

    def arrived(group):
        for copy in flight[group]:
            copy.wait_recv()

    def own_rows(group, j=0):
        first, rows, axes = GROUPS[group]
        size = rows // 4
        turn = lax.rem(co[axes[0]] + j, 4)
        return pl.ds(pl.multiple_of(first + turn * size, 16), size)

    def landing(group):
        return pl.ds(GROUPS[group][0] // 4, GROUPS[group][1] // 4)

    def exchange(group, stage, buf, total):
        axis = GROUPS[group][2][stage]
        me = co[axis]
        buf[me, landing(group)] = total.astype(BF)
        here = buf.at[me, landing(group)]
        send_stage(group, stage, axis, lambda j: (here, here))

    def exchanged(group, buf):
        arrived(group)
        total = buf[0, landing(group)].astype(F32)
        for i in range(1, 4):
            total = total + buf[i, landing(group)].astype(F32)
        return total

    sib_in = {}

    def begin(part):
        rows = pl.ds(part * 1024, 1024)
        sib_in[part] = send(grads_ref.at[1 - core, rows], r0.at[rows], sib_send.at[part], sib_recv.at[part], sib)

    def join(part):
        sib_in[part].wait_recv()
        rows = pl.ds(part * 1024, 1024)
        a1[rows] = (grads_ref[core, rows].astype(F32) + r0[rows].astype(F32)).astype(BF)

    def advance(group, stage):
        if stage == 0:
            send_stage(
                group, 0, GROUPS[group][2][0], lambda j: (a1.at[own_rows(group, j + 1)], r1.at[j, landing(group)])
            )
        elif stage == 1:
            arrived(group)
            total = a1[own_rows(group)].astype(F32)
            for j in range(3):
                total = total + r1[j, landing(group)].astype(F32)
            exchange(group, 1, a2, total)
        elif stage == 2:
            exchange(group, 2, a3, exchanged(group, a2))
        elif stage == 3:
            sum_ref[core, own_rows(group)] = exchanged(group, a3).astype(BF)
            where = sum_ref.at[core, own_rows(group)]
            send_stage(group, 3, GROUPS[group][2][0], lambda j: (where, where))
        elif stage == 4:
            arrived(group)
            whole = sum_ref.at[core, pl.ds(GROUPS[group][0], GROUPS[group][1])]
            flight[group] = [send(whole, whole, sib_send.at[4 + group], sib_recv.at[4 + group], sib)]
        else:
            arrived(group)

    def widen(pair):
        for half in range(2):
            for i in range(3):
                first = pair * 1024 + i * 256
                cols = slice(i * 512 + pair * 128, i * 512 + (pair + 1) * 128)
                gqkv_ref[half * 256 : (half + 1) * 256, cols] = sum_ref[half, first : first + 256].astype(F32)
            rows = slice(pair * 128 + half * 64, pair * 128 + (half + 1) * 64)
            for ct in range(4):
                first = pair * 1024 + 768 + ct * 64
                gproj_ref[rows, ct * 128 : (ct + 1) * 128] = sum_ref[half, first : first + 64].astype(F32)

    def advance_wave(wave, stage):
        for group in WAVES[wave]:
            advance(group, stage)

    lane = lax.broadcasted_iota(jnp.int32, (1, 128), 1)
    small_ones = ones[:128, :128]

    def pair_of_heads(pair):
        cols = slice(pair * 128, (pair + 1) * 128)
        scales = [scale_ref[pair * 2 + i] for i in range(2)]
        s_lane = jnp.where(lane < 64, scales[0], scales[1])

        def window(w):
            rows = slice(w * WIN, (w + 1) * WIN)
            q_p = q_s[rows, cols]
            k_p = k_s[rows, cols]
            qd_p = qd_s[rows, cols]
            kd_p = kd_s[rows, cols]
            v_p = v_s[rows, cols]
            do_p = do_s[rows, cols]
            allow = allow_s[w]
            acc_o = jnp.zeros((WIN, 128), F32)
            acc_q = jnp.zeros((WIN, 128), F32)
            acc_k = jnp.zeros((WIN, 128), F32)
            acc_v = jnp.zeros((WIN, 128), F32)
            zero = jnp.zeros((WIN, 128), BF)
            for i in range(2):
                s = scales[i]
                mine = jnp.broadcast_to((lane < 64) if i == 0 else (lane >= 64), (WIN, 128))
                qd_h = jnp.where(mine, qd_p, zero)
                kd_h = jnp.where(mine, kd_p, zero)
                v_h = jnp.where(mine, v_p, zero)
                do_h = jnp.where(mine, do_p, zero)
                rq_row = rq_rows_s[w, pair * 2 + i : pair * 2 + i + 1, :]
                rk_col = rk_s[rows, pair * 128 + i * 64 : pair * 128 + i * 64 + 1]
                cos = dot(k_p, jnp.where(mine, q_p, zero), 1, 1) * rk_col * rq_row
                e = jnp.exp(s * cos - s) * allow
                p = e * (1.0 / jnp.sum(e, axis=0, keepdims=True))
                dp = dot(v_p, do_h, 1, 1)
                dl = p * (dp - jnp.sum(p * dp, axis=0, keepdims=True))
                gs_s[w * 4 + pair, i : i + 1, :] = jnp.sum(dl * cos, axis=0, keepdims=True)
                p_b = p.astype(BF)
                dl_b = dl.astype(BF)
                acc_o = acc_o + dot(p_b, v_h, 0, 0)
                acc_v = acc_v + dot(p_b, do_h)
                acc_k = acc_k + dot(dl_b, qd_h)
                acc_q = acc_q + dot(dl_b, kd_h, 0, 0)
            att_s[rows, cols] = acc_o.astype(BF)
            dv_s[rows, cols] = acc_v.astype(BF)
            qd = qd_p.astype(F32)
            kd = kd_p.astype(F32)
            dqd = acc_q * s_lane
            dkd = acc_k * s_lane
            dq_s[rows, cols] = (rq_s[rows, cols] * (dqd - qd * dot((qd * dqd).astype(BF), small_ones))).astype(BF)
            dk_s[rows, cols] = (rk_s[rows, cols] * (dkd - kd * dot((kd * dkd).astype(BF), small_ones))).astype(BF)

        window(0)
        window(1)
        d_all = jnp.concatenate([dq_s[:, cols], dk_s[:, cols], dv_s[:, cols]], axis=1)
        gq = dot(y_t, d_all).astype(BF)
        gp = dot(att_s[:, cols], g_s[...], 0, 0).astype(BF)
        for half in range(2):
            for i in range(3):
                first = pair * 1024 + i * 256
                grads_ref[half, first : first + 256] = gq[half * 256 : (half + 1) * 256, i * 128 : (i + 1) * 128]
            for ct in range(4):
                first = pair * 1024 + 768 + ct * 64
                grads_ref[half, first : first + 64] = gp[half * 64 : (half + 1) * 64, ct * 128 : (ct + 1) * 128]
        begin(pair)

    for pair in range(4):
        pair_of_heads(pair)
        if pair == 2:
            join(0)
            join(1)
            advance_wave(0, 0)
        elif pair == 3:
            join(2)
            advance_wave(1, 0)

    def out_slot(slot, pieces):
        back_ref[slot] = jnp.concatenate(pieces, axis=0).astype(BF)

    back = {}

    def send_back(slots):
        for i, (slot, way) in enumerate(SLOT_SENDS):
            if slot in slots:
                back[slot] = send(back_ref.at[slot], ret_ref.at[slot], out_send.at[i], out_recv.at[i], high[way])

    mixed = x_s[...] + dot(att_s[...], wproj_ref[...])
    for slot in (0, 2):
        out_slot(slot, [mixed[slot * QT : (slot + 2) * QT]])
    send_back((2,))
    dn = dot(dq_s[...], wqkv_ref[:, 0:512], 1, 1)
    dn = dn + dot(dk_s[...], wqkv_ref[:, 512:1024], 1, 1)
    dn = dn + dot(dv_s[...], wqkv_ref[:, 1024:1536], 1, 1)
    xhat = xh_s[...]
    d_gain = jnp.sum(dn * xhat, axis=0, keepdims=True)
    small_s[...] = jnp.zeros((16, 128), F32)
    for i in range(4):
        small_s[i : i + 1, :] = d_gain[:, i * 128 : (i + 1) * 128]
    for h in range(8):
        row = gs_s[h // 2, h % 2 : h % 2 + 1, :] + gs_s[4 + h // 2, h % 2 : h % 2 + 1, :]
        small_s[8 + h : 9 + h, :] = jnp.broadcast_to(jnp.sum(row, axis=1, keepdims=True), (1, 128))

    def small_stage(stage, values):
        axis = ("core", "x", "y", "z")[stage]
        buf = (sv0, sv1, sv2, sv3)[stage]
        me = co[axis]
        buf[me] = values
        copies = []
        for j, dev in enumerate([sib] if stage == 0 else peers[axis]):
            index = 0 if stage == 0 else 1 + 3 * (stage - 1) + j
            copies.append(send(buf.at[me], buf.at[me], sv_send.at[index], sv_recv.at[index], dev))
        return copies

    def small_sum(stage, copies):
        buf = (sv0, sv1, sv2, sv3)[stage]
        for copy in copies:
            copy.wait_recv()
        total = buf[0]
        for i in range(1, 2 if stage == 0 else 4):
            total = total + buf[i]
        return total

    small_copies = small_stage(0, small_s[...])
    dxh = dn * gain
    rstd = rstd_s[:, 0:1]
    dx = rstd * (dxh - jnp.mean(dxh, axis=-1, keepdims=True) - xhat * jnp.mean(dxh * xhat, axis=-1, keepdims=True))
    gtok = g_s[...].astype(F32) + dx
    for slot in (1, 3):
        out_slot(slot, [gtok[(slot - 1) * QT : (slot + 1) * QT]])
    for slot in (4, 5, 6, 7):
        rows = slice(slot * QT, (slot + 1) * QT)
        out_slot(slot, [mixed[rows], gtok[rows]])
    for slot in KEPT_SLOTS:
        ret_ref[slot] = back_ref[slot]
    join(3)
    advance_wave(2, 0)
    send_back((5, 7, 6, 3))
    for stage in range(1, 6):
        for wave in range(3):
            advance_wave(wave, stage)
            if stage == 5:
                for pair in WAVE_PAIRS[wave]:
                    widen(pair)
        if stage < 4:
            small_copies = small_stage(stage, small_sum(stage - 1, small_copies))
        if stage == 4:
            small = small_sum(3, small_copies)
            for i in range(4):
                gain_out_ref[:, i * 128 : (i + 1) * 128] = small[i : i + 1, :]
            eye = lax.broadcasted_iota(jnp.int32, (8, 128), 0) == lax.broadcasted_iota(jnp.int32, (8, 128), 1)
            gscale_ref[...] = jnp.sum(jnp.where(eye, small[8:16, :], 0.0), axis=0, keepdims=True)
        if stage == 2:
            for slot in back:
                back[slot].wait_recv()
            ret = [ret_ref[slot].astype(F32) for slot in range(8)]
            out = jnp.concatenate([ret[0], ret[2]] + [ret[slot][:QT] for slot in (4, 5, 6, 7)], axis=0).astype(BF)
            mixed_ref[...] = dot(perm_ref[...], out, 0, 0).astype(BF)
            out = jnp.concatenate([ret[1], ret[3]] + [ret[slot][QT:] for slot in (4, 5, 6, 7)], axis=0).astype(BF)
            gtok_ref[...] = dot(perm_ref[...], out, 0, 0).astype(BF)
    for copy in started:
        copy.wait_send()


def finish_kernel(*refs):
    sources, targets, sems = refs[:6], refs[6:12], refs[12]
    copies = [pltpu.make_async_copy(sources[i], targets[i], sems.at[i]) for i in range(5)]
    for copy in copies:
        copy.start()
    targets[5][...] = sources[5][:, :8]
    for copy in copies:
        copy.wait()


VM = pl.BlockSpec(memory_space=pltpu.VMEM)
HBM = pl.BlockSpec(memory_space=pltpu.HBM)
DMA = pltpu.SemaphoreType.DMA
MIB = 1024 * 1024


def per_device(tokens, cotangent, key_keep, norm_gain, w_qkv, w_proj, attn_scale):
    perm, member, place = tables()
    perm = jnp.asarray(perm, BF)
    x = tokens.reshape(288, 512)
    g = cotangent.reshape(288, 512)
    tok = (2 * WIN, 512)
    operands = (
        x, g, key_keep.transpose(1, 0, 2), perm, jnp.asarray(member, BF), jnp.asarray(place, BF),
        w_qkv, w_proj, norm_gain.reshape(1, 512), attn_scale,
    )
    operands = [pltpu.with_memory_space_constraint(operand, pltpu.HBM) for operand in operands]
    results = (
        jax.ShapeDtypeStruct((288, 512), BF),
        jax.ShapeDtypeStruct((288, 512), BF),
        jax.ShapeDtypeStruct((512, 1536), F32),
        jax.ShapeDtypeStruct((512, 512), F32),
        jax.ShapeDtypeStruct((1, 512), F32),
        jax.ShapeDtypeStruct((1, 128), F32),
    )
    near = pl.pallas_call(
        block_kernel,
        out_shape=results,
        in_specs=[HBM] * 10,
        out_specs=(VM,) * 6,
        scratch_shapes=[
            pltpu.VMEM((8, ROWS, 512), BF),
            pltpu.VMEM((2, 4096, 128), BF),
            pltpu.VMEM((288, 512), BF),
            pltpu.VMEM((288, 512), BF),
            pltpu.VMEM((6, 2, 24), jnp.int32),
            pltpu.VMEM((8 * QT, 288), BF),
            pltpu.VMEM((8, 288), BF),
            pltpu.VMEM((288, 256), BF),
            pltpu.VMEM((512, 1536), BF),
            pltpu.VMEM((512, 512), BF),
            pltpu.VMEM((1, 512), F32),
            pltpu.SMEM((8,), F32),
            pltpu.VMEM((5, ROWS, 512), BF),
            pltpu.VMEM((8, ROWS, 512), BF),
            pltpu.VMEM((8, ROWS, 512), BF),
            pltpu.VMEM(tok, F32),
            pltpu.VMEM(tok, F32),
            pltpu.VMEM((2 * WIN, 128), F32),
            pltpu.VMEM(tok, BF),
            pltpu.VMEM(tok, BF),
            pltpu.VMEM(tok, F32),
            pltpu.VMEM(tok, F32),
        ]
        + [pltpu.VMEM((2, 8, WIN), F32)]
        + [pltpu.VMEM(tok, BF)] * 10
        + [
            pltpu.VMEM((2, WIN, WIN), F32),
            pltpu.VMEM((8, 2, WIN), F32),
            pltpu.VMEM((16, 128), F32),
            pltpu.VMEM((2, 4096, 128), BF),
            pltpu.VMEM((4096, 128), BF),
            pltpu.VMEM((4096, 128), BF),
            pltpu.VMEM((3, 1024, 128), BF),
            pltpu.VMEM((4, 1024, 128), BF),
            pltpu.VMEM((4, 1024, 128), BF),
            pltpu.VMEM((2, 16, 128), F32),
            pltpu.VMEM((4, 16, 128), F32),
            pltpu.VMEM((4, 16, 128), F32),
            pltpu.VMEM((4, 16, 128), F32),
            DMA((10,)),
            DMA((5,)), DMA((5,)),
            DMA((5,)), DMA((5,)),
            DMA((13,)), DMA((13,)),
            DMA((9, 4, 3)), DMA((9, 4, 3)),
            DMA((10,)), DMA((10,)),
        ],
        compiler_params=pltpu.CompilerParams(collective_id=1, has_side_effects=True, vmem_limit_bytes=40 * MIB),
        name="block",
    )(*operands)

    mixed, gtok, gqkv, gproj, gain, gscale = pl.pallas_call(
        finish_kernel,
        out_shape=results[:5] + (jax.ShapeDtypeStruct((1, 8), F32),),
        in_specs=[VM] * 6,
        out_specs=(HBM,) * 5 + (VM,),
        scratch_shapes=[DMA((5,))],
        compiler_params=pltpu.CompilerParams(vmem_limit_bytes=8 * MIB),
        name="finish",
    )(*near)
    return (
        mixed.reshape(tokens.shape),
        gtok.reshape(tokens.shape),
        gqkv,
        gproj,
        gain.reshape(512),
        gscale.reshape(8),
    )


def solution(mesh):
    grid = P(None, "lat", "lon", None)
    return jax.shard_map(
        per_device,
        mesh=mesh,
        in_specs=(grid, grid, P(None, "lat", "lon"), P(), P(), P(), P()),
        out_specs=(grid, grid, P(), P(), P(), P()),
        check_vma=False,
    )
```

```python
import functools

import jax
import jax.numpy as jnp
import numpy as np
from jax import lax
from jax.experimental import pallas as pl
from jax.experimental.pallas import tpu as pltpu
from jax.sharding import PartitionSpec as P

EPS_NORM = 1e-05
EPS_DIR = 1e-06
MESH = pl.DeviceIdType.MESH
BF = jnp.bfloat16
F32 = jnp.float32

QUARTERS = ((1, 1), (1, 2), (0, 1), (0, 2), (1, 3), (1, 0), (0, 3), (0, 0))
QT = 40
ROWS = 80
WIN = 160
FLAG_ROW = 36


def token_of(quarter, t):
    half, cq = QUARTERS[quarter]
    lev, rest = divmod(t, 18)
    rr, cc = divmod(rest, 6)
    return lev * 144 + (half * 3 + rr) * 24 + cq * 6 + cc


def tables():
    perm = np.zeros((8 * QT, 288), np.float32)
    member = np.zeros((8, 288), np.float32)
    place = np.zeros((288, 256), np.float32)
    for quarter in range(8):
        for t in range(36):
            src = token_of(quarter, t)
            perm[quarter * QT + t, src] = 1.0
            member[quarter, src] = 1.0
            place[src, QT * (quarter % 4) + t] = 1.0
    return perm, member, place


def dot(a, b, ca=1, cb=0):
    return lax.dot_general(a, b, (((ca,), (cb,)), ((), ())), preferred_element_type=F32)


def position():
    lat = lax.axis_index("lat")
    lon = lax.axis_index("lon")
    return lat, lon


def wrap(value, count):
    return lax.rem(value + count, count)


SLOT_SENDS = ((2, "lat"), (5, "lon"), (7, "diag"), (6, "lat"), (3, "lat"))
KEPT_SLOTS = (0, 1, 4)

BLOCKS = {"A": (("x", "even"), ("y", "even")), "B": (("x", "odd"), ("z", "odd")), "C": (("y", "odd"), ("z", "even"))}

GROUPS = (
    (0, 768, "ABC"),
    (768, 512, "CAB"),
    (1280, 768, "BCA"),
    (2048, 768, "ABC"),
    (2816, 512, "CAB"),
    (3328, 768, "BCA"),
)
WAVES = ((0, 1, 2), (3, 4, 5))


def slot_pieces(slot):
    if slot < 4:
        first = 2 * (slot // 2)
        kind = "xg"[slot % 2]
        return ((kind, first), (kind, first + 1))
    return (("x", slot), ("g", slot))


def coordinates():
    lat, lon = position()
    core = lax.rem(lat, 2)
    y = (lat // 2) * 2 + lon // 16
    x = lax.rem(lon // 4, 4)
    z = lax.rem(lon, 4)
    return {"x": x, "y": y, "z": z, "core": core}


def device_at(co):
    return ((co["y"] // 2) * 2 + co["core"], lax.rem(co["y"], 2) * 16 + co["x"] * 4 + co["z"])


def pair_bit(at, kind):
    return lax.rem(at // 2 + at, 2) if kind == "even" else at // 2


def pair_mate(at, kind):
    return at + 1 - 2 * lax.rem(at, 2) if kind == "even" else 3 - at


def block_members(co, name):
    members = []
    for flip in range(4):
        moved, index = dict(co), 0
        for i, (axis, kind) in enumerate(BLOCKS[name]):
            bit = pair_bit(co[axis], kind)
            if flip >> i & 1:
                moved[axis] = pair_mate(co[axis], kind)
                bit = 1 - bit
            index = index + bit * (1 << i)
        members.append((index, device_at(moved)))
    return members


def sibling(co):
    moved = dict(co)
    moved["core"] = 1 - co["core"]
    return device_at(moved)


def block_kernel(
    x_hbm, g_hbm, keep_hbm, perm_hbm, member_hbm, place_hbm, wqkv_hbm, wproj_hbm, gain_hbm, scale_hbm,
    ret_ref, sum_ref, small_out_ref,
    x_ref, g_ref, keep_ref, perm_ref, member_ref, place_ref, wqkv_ref, wproj_ref, gain_ref, scale_ref, in_buf, win_ref, back_ref,
    x_s, xh_s, rstd_s, y_s, g_s, rq_s, rk_s, rq_rows_s, q_s, k_s, qd_s, kd_s, v_s, do_s, dq_s, dk_s, dv_s, att_s, allow_s, gs_s, small_s,
    grads_ref, r0, a1, r1, a2, r2, a3, sv0, sv1, sv2, sv3,
    w_sem, in_send, in_recv, out_send, out_recv, sib_send, sib_recv, st_send, st_recv, sv_send, sv_recv,
):
    lat, lon = position()
    lat_lo, lat_hi = wrap(lat - 1, 4), wrap(lat + 1, 4)
    lon_lo, lon_hi = wrap(lon - 1, 32), wrap(lon + 1, 32)
    co = coordinates()
    core = co["core"]
    sib = sibling(co)
    peers, turns = {}, {}
    for name in BLOCKS:
        members = block_members(co, name)
        turns[name] = [index for index, _ in members]
        peers[name] = [dev for _, dev in members[1:]]

    loads = {}
    for i, (name, src, dst) in enumerate((
        ("perm", perm_hbm, perm_ref),
        ("x", x_hbm, x_ref),
        ("keep", keep_hbm, keep_ref),
        ("member", member_hbm, member_ref),
        ("place", place_hbm, place_ref),
        ("g", g_hbm, g_ref),
        ("gain", gain_hbm, gain_ref),
        ("qkv", wqkv_hbm, wqkv_ref),
        ("proj", wproj_hbm, wproj_ref),
        ("scale", scale_hbm, scale_ref),
    )):
        loads[name] = pltpu.make_async_copy(src, dst, w_sem.at[i])
        loads[name].start()

    barrier = pltpu.get_barrier_semaphore()
    greet = [(lat_lo, lon), (lat, lon_lo), (lat_lo, lon_lo), (lat_hi, lon), (lat, lon_hi), (lat_hi, lon_hi), sib]
    for name in BLOCKS:
        greet.extend(peers[name])
    for dev in greet:
        pl.semaphore_signal(barrier, inc=1, device_id=dev, device_id_type=MESH)

    started = []

    def send(src, dst, s_sem, r_sem, dev):
        copy = pltpu.make_async_remote_copy(
            src_ref=src, dst_ref=dst, send_sem=s_sem, recv_sem=r_sem, device_id=dev, device_id_type=MESH
        )
        copy.start()
        started.append(copy)
        return copy

    for name in ("perm", "x", "keep", "member", "place", "g"):
        loads[name].wait()
    perm = perm_ref[...]
    xs = dot(perm, x_ref[...])
    gs = dot(perm, g_ref[...])
    keep_rows = [keep_ref[row, lev : lev + 1, :].astype(F32) for lev in range(2) for row in range(6)]
    marks = (jnp.concatenate(keep_rows, axis=1) * member_ref[...].astype(F32)).astype(BF)
    flags = dot(marks, place_ref[...])
    row_id = lax.broadcasted_iota(jnp.int32, (QT, 512), 0)

    def piece(kind, quarter):
        rows = slice(quarter * QT, (quarter + 1) * QT)
        if kind == "g":
            return gs[rows]
        flag = jnp.concatenate([flags[quarter : quarter + 1], jnp.zeros((1, 256), F32)], axis=1)
        return jnp.where(row_id == FLAG_ROW, flag, xs[rows])

    def payload(slot):
        return jnp.concatenate([piece(*p) for p in slot_pieces(slot)], axis=0).astype(BF)

    for i, (slot, _) in enumerate(SLOT_SENDS):
        in_buf[i] = payload(slot)
    pl.semaphore_wait(barrier, len(greet))
    low = {"lat": (lat_lo, lon), "lon": (lat, lon_lo), "diag": (lat_lo, lon_lo)}
    high = {"lat": (lat_hi, lon), "lon": (lat, lon_hi), "diag": (lat_hi, lon_hi)}
    arrive = {}
    for i, (slot, way) in enumerate(SLOT_SENDS):
        arrive[slot] = send(in_buf.at[i], win_ref.at[slot], in_send.at[i], in_recv.at[i], low[way])
    for slot in KEPT_SLOTS:
        win_ref[slot] = payload(slot)
    loads["gain"].wait()
    loads["qkv"].wait()

    gain = gain_ref[...]
    r = lax.broadcasted_iota(jnp.int32, (256, 256), 0)
    c = lax.broadcasted_iota(jnp.int32, (256, 256), 1)
    ones = jnp.where((r // 64) == (c // 64), 1.0, 0.0).astype(BF)

    r = lax.broadcasted_iota(jnp.int32, (8, 512), 0)
    c = lax.broadcasted_iota(jnp.int32, (8, 512), 1)
    head_of = jnp.where(r == c // 64, 1.0, 0.0).astype(BF)

    def head_sum(values):
        hi = values.astype(BF)
        lo = (values - hi.astype(F32)).astype(BF)
        halves = [dot(hi[:, i : i + 256], ones) + dot(lo[:, i : i + 256], ones) for i in (0, 256)]
        return jnp.concatenate(halves, axis=1)

    real = lax.broadcasted_iota(jnp.int32, (QT, 512), 0) < 36
    key_id = lax.broadcasted_iota(jnp.int32, (WIN, WIN), 0)
    query_id = lax.broadcasted_iota(jnp.int32, (WIN, WIN), 1)
    same_half = (key_id >= 2 * QT) == (query_id >= 2 * QT)
    joined = jnp.logical_or(same_half, lat != 3)
    first_row = lax.broadcasted_iota(jnp.int32, (8, WIN), 0) == 0
    one_row = jnp.where(first_row, 1.0, 0.0).astype(BF)

    def front(w):
        rows = slice(w * WIN, (w + 1) * WIN)
        if w == 0:
            data = jnp.concatenate([win_ref[0].astype(F32), win_ref[2].astype(F32)], axis=0)
        else:
            data = jnp.concatenate([win_ref[slot].astype(F32)[:QT] for slot in (4, 5, 6, 7)], axis=0)
        data = data.reshape(4, QT, 512)
        x = jnp.where(real[None], data, 0.0).reshape(WIN, 512)
        marks = data[0, FLAG_ROW : FLAG_ROW + 1, :]
        for i in range(1, 4):
            marks = marks + data[i, FLAG_ROW : FLAG_ROW + 1, :]
        marks = jnp.where(first_row, marks[:, :WIN], 0.0).astype(BF)
        keep = jnp.where(joined, dot(marks, one_row, 0, 0), 0.0)
        allow_s[w] = jnp.where(key_id == query_id, 1.0, keep)
        mean = jnp.mean(x, axis=-1, keepdims=True)
        xc = x - mean
        var = jnp.mean(xc * xc, axis=-1, keepdims=True)
        rstd = lax.rsqrt(var + EPS_NORM)
        xhat = xc * rstd
        y = (xhat * gain).astype(BF)
        x_s[rows] = x
        xh_s[rows] = xhat
        rstd_s[rows] = jnp.broadcast_to(rstd, (WIN, 128))
        y_s[rows] = y
        q_b = dot(y, wqkv_ref[:, 0:512]).astype(BF)
        k_b = dot(y, wqkv_ref[:, 512:1024]).astype(BF)
        q_s[rows] = q_b
        k_s[rows] = k_b
        q = q_b.astype(F32)
        k = k_b.astype(F32)
        v_s[rows] = dot(y, wqkv_ref[:, 1024:1536]).astype(BF)
        q_sq = q * q
        rq = lax.rsqrt(head_sum(q_sq) + EPS_DIR)
        sq_hi = q_sq.astype(BF)
        sq_lo = (q_sq - sq_hi.astype(F32)).astype(BF)
        rq_rows_s[w] = lax.rsqrt(dot(head_of, sq_hi, 1, 1) + dot(head_of, sq_lo, 1, 1) + EPS_DIR)
        rk = lax.rsqrt(head_sum(k * k) + EPS_DIR)
        rq_s[rows] = rq
        rk_s[rows] = rk
        qd_s[rows] = (q * rq).astype(BF)
        kd_s[rows] = (k * rk).astype(BF)

    arrive[2].wait_recv()
    front(0)
    for slot in (5, 7, 6):
        arrive[slot].wait_recv()
    front(1)
    arrive[3].wait_recv()
    g = jnp.concatenate(
        [win_ref[1].astype(F32), win_ref[3].astype(F32)] + [win_ref[slot].astype(F32)[QT:] for slot in (4, 5, 6, 7)],
        axis=0,
    ).astype(BF)
    g_s[...] = g
    loads["proj"].wait()
    loads["scale"].wait()
    do_s[...] = dot(g, wproj_ref[...], 1, 1).astype(BF)
    y_t = jnp.transpose(y_s[...])

    flight = {}

    def send_stage(group, stage, axis, pairs):
        copies = []
        for j in range(3):
            src, dst = pairs(j)
            index = (group, stage, j)
            copies.append(send(src, dst, st_send.at[index], st_recv.at[index], peers[axis][j]))
        flight[group] = copies

    def arrived(group):
        for copy in flight[group]:
            copy.wait_recv()

    def size_of(group, level):
        return GROUPS[group][1] // (4, 16)[level]

    def start_of(group, level):
        return GROUPS[group][0] // (1, 4)[level]

    def own_rows(group, level, j=0):
        first, size = start_of(group, level), size_of(group, level)
        turn = turns[GROUPS[group][2][level]][j]
        return pl.ds(pl.multiple_of(first + turn * size, 16), size)

    def landing(group, level):
        return pl.ds(GROUPS[group][0] // (4, 16)[level], size_of(group, level))

    def scatter(group, level, src, dst):
        def pairs(j):
            return src.at[own_rows(group, level, j + 1)], dst.at[j, landing(group, level)]

        send_stage(group, level, GROUPS[group][2][level], pairs)

    def gathered(group, level, src, dst):
        arrived(group)
        total = src[own_rows(group, level)].astype(F32)
        for j in range(3):
            total = total + dst[j, landing(group, level)].astype(F32)
        return total.astype(BF)

    def final_rows(group, level):
        first, rows, axes = GROUPS[group]
        off = first + turns[axes[0]][0] * (rows // 4)
        if level == 1:
            off = off + turns[axes[1]][0] * (rows // 16)
        return pl.ds(pl.multiple_of(off, 16), size_of(group, level))

    def spread(group, level):
        where = sum_ref.at[core, final_rows(group, level)]
        send_stage(group, 4 - level, GROUPS[group][2][level], lambda j: (where, where))

    sib_in = {}

    def begin(part):
        rows = pl.ds(part * 1024, 1024)
        sib_in[part] = send(grads_ref.at[1 - core, rows], r0.at[rows], sib_send.at[part], sib_recv.at[part], sib)

    def join(part):
        sib_in[part].wait_recv()
        rows = pl.ds(part * 1024, 1024)
        a1[rows] = (grads_ref[core, rows].astype(F32) + r0[rows].astype(F32)).astype(BF)

    def advance(group, stage):
        if stage == 0:
            scatter(group, 0, a1, r1)
        elif stage == 1:
            a2[landing(group, 0)] = gathered(group, 0, a1, r1)
            scatter(group, 1, a2, r2)
        elif stage == 2:
            me = turns[GROUPS[group][2][2]][0]
            a3[me, landing(group, 1)] = gathered(group, 1, a2, r2)
            here = a3.at[me, landing(group, 1)]
            send_stage(group, 2, GROUPS[group][2][2], lambda j: (here, here))
        elif stage == 3:
            arrived(group)
            total = a3[0, landing(group, 1)].astype(F32)
            for i in range(1, 4):
                total = total + a3[i, landing(group, 1)].astype(F32)
            sum_ref[core, final_rows(group, 1)] = total.astype(BF)
            spread(group, 1)
        elif stage == 4:
            arrived(group)
            spread(group, 0)
        elif stage == 5:
            arrived(group)
            whole = sum_ref.at[core, pl.ds(GROUPS[group][0], GROUPS[group][1])]
            flight[group] = [send(whole, whole, sib_send.at[4 + group], sib_recv.at[4 + group], sib)]
        else:
            arrived(group)

    def advance_wave(wave, stage):
        for group in WAVES[wave]:
            advance(group, stage)

    lane = lax.broadcasted_iota(jnp.int32, (1, 128), 1)
    small_ones = ones[:128, :128]

    def pair_of_heads(pair):
        cols = slice(pair * 128, (pair + 1) * 128)
        scales = [scale_ref[pair * 2 + i] for i in range(2)]
        s_lane = jnp.where(lane < 64, scales[0], scales[1])

        def window(w):
            rows = slice(w * WIN, (w + 1) * WIN)
            q_p = q_s[rows, cols]
            k_p = k_s[rows, cols]
            qd_p = qd_s[rows, cols]
            kd_p = kd_s[rows, cols]
            v_p = v_s[rows, cols]
            do_p = do_s[rows, cols]
            allow = allow_s[w]
            acc_o = jnp.zeros((WIN, 128), F32)
            acc_q = jnp.zeros((WIN, 128), F32)
            acc_k = jnp.zeros((WIN, 128), F32)
            acc_v = jnp.zeros((WIN, 128), F32)
            zero = jnp.zeros((WIN, 128), BF)
            for i in range(2):
                s = scales[i]
                mine = jnp.broadcast_to((lane < 64) if i == 0 else (lane >= 64), (WIN, 128))
                qd_h = jnp.where(mine, qd_p, zero)
                kd_h = jnp.where(mine, kd_p, zero)
                v_h = jnp.where(mine, v_p, zero)
                do_h = jnp.where(mine, do_p, zero)
                rq_row = rq_rows_s[w, pair * 2 + i : pair * 2 + i + 1, :]
                rk_col = rk_s[rows, pair * 128 + i * 64 : pair * 128 + i * 64 + 1]
                cos = dot(k_p, jnp.where(mine, q_p, zero), 1, 1) * rk_col * rq_row
                e = jnp.exp(s * cos - s) * allow
                p = e * (1.0 / jnp.sum(e, axis=0, keepdims=True))
                dp = dot(v_p, do_h, 1, 1)
                dl = p * (dp - jnp.sum(p * dp, axis=0, keepdims=True))
                gs_s[w * 4 + pair, i : i + 1, :] = jnp.sum(dl * cos, axis=0, keepdims=True)
                p_b = p.astype(BF)
                dl_b = dl.astype(BF)
                acc_o = acc_o + dot(p_b, v_h, 0, 0)
                acc_v = acc_v + dot(p_b, do_h)
                acc_k = acc_k + dot(dl_b, qd_h)
                acc_q = acc_q + dot(dl_b, kd_h, 0, 0)
            att_s[rows, cols] = acc_o.astype(BF)
            dv_s[rows, cols] = acc_v.astype(BF)
            qd = qd_p.astype(F32)
            kd = kd_p.astype(F32)
            dqd = acc_q * s_lane
            dkd = acc_k * s_lane
            dq_s[rows, cols] = (rq_s[rows, cols] * (dqd - qd * dot((qd * dqd).astype(BF), small_ones))).astype(BF)
            dk_s[rows, cols] = (rk_s[rows, cols] * (dkd - kd * dot((kd * dkd).astype(BF), small_ones))).astype(BF)

        window(0)
        window(1)
        d_all = jnp.concatenate([dq_s[:, cols], dk_s[:, cols], dv_s[:, cols]], axis=1)
        gq = dot(y_t, d_all).astype(BF)
        gp = dot(att_s[:, cols], g_s[...], 0, 0).astype(BF)
        for half in range(2):
            for i in range(3):
                first = pair * 1024 + i * 256
                grads_ref[half, first : first + 256] = gq[half * 256 : (half + 1) * 256, i * 128 : (i + 1) * 128]
            for ct in range(4):
                first = pair * 1024 + 768 + ct * 64
                grads_ref[half, first : first + 64] = gp[half * 64 : (half + 1) * 64, ct * 128 : (ct + 1) * 128]
        begin(pair)

    for pair in range(4):
        pair_of_heads(pair)
        if pair == 2:
            join(0)
            join(1)
            advance_wave(0, 0)

    def out_slot(slot, pieces):
        back_ref[slot] = jnp.concatenate(pieces, axis=0).astype(BF)

    back = {}

    def send_back(slots):
        for i, (slot, way) in enumerate(SLOT_SENDS):
            if slot in slots:
                back[slot] = send(back_ref.at[slot], ret_ref.at[slot], out_send.at[i], out_recv.at[i], high[way])

    mixed = x_s[...] + dot(att_s[...], wproj_ref[...])
    for slot in (0, 2):
        out_slot(slot, [mixed[slot * QT : (slot + 2) * QT]])
    send_back((2,))
    dn = dot(dq_s[...], wqkv_ref[:, 0:512], 1, 1)
    dn = dn + dot(dk_s[...], wqkv_ref[:, 512:1024], 1, 1)
    dn = dn + dot(dv_s[...], wqkv_ref[:, 1024:1536], 1, 1)
    xhat = xh_s[...]
    d_gain = jnp.sum(dn * xhat, axis=0, keepdims=True)
    small_s[...] = jnp.zeros((16, 128), F32)
    for i in range(4):
        small_s[i : i + 1, :] = d_gain[:, i * 128 : (i + 1) * 128]
    for h in range(8):
        row = gs_s[h // 2, h % 2 : h % 2 + 1, :] + gs_s[4 + h // 2, h % 2 : h % 2 + 1, :]
        small_s[8 + h : 9 + h, :] = jnp.broadcast_to(jnp.sum(row, axis=1, keepdims=True), (1, 128))

    def small_stage(stage, values):
        axis = ("core", "A", "B", "C")[stage]
        buf = (sv0, sv1, sv2, sv3)[stage]
        me = core if stage == 0 else turns[axis][0]
        buf[me] = values
        copies = []
        for j, dev in enumerate([sib] if stage == 0 else peers[axis]):
            index = 0 if stage == 0 else 1 + 3 * (stage - 1) + j
            copies.append(send(buf.at[me], buf.at[me], sv_send.at[index], sv_recv.at[index], dev))
        return copies

    def small_sum(stage, copies):
        buf = (sv0, sv1, sv2, sv3)[stage]
        for copy in copies:
            copy.wait_recv()
        total = buf[0]
        for i in range(1, 2 if stage == 0 else 4):
            total = total + buf[i]
        return total

    small_copies = small_stage(0, small_s[...])
    dxh = dn * gain
    rstd = rstd_s[:, 0:1]
    dx = rstd * (dxh - jnp.mean(dxh, axis=-1, keepdims=True) - xhat * jnp.mean(dxh * xhat, axis=-1, keepdims=True))
    gtok = g_s[...].astype(F32) + dx
    for slot in (1, 3):
        out_slot(slot, [gtok[(slot - 1) * QT : (slot + 1) * QT]])
    for slot in (4, 5, 6, 7):
        rows = slice(slot * QT, (slot + 1) * QT)
        out_slot(slot, [mixed[rows], gtok[rows]])
    for slot in KEPT_SLOTS:
        ret_ref[slot] = back_ref[slot]
    join(2)
    join(3)
    advance_wave(1, 0)
    send_back((5, 7, 6, 3))
    for stage in range(1, 7):
        advance_wave(0, stage)
        advance_wave(1, stage)
        if stage < 4:
            small_copies = small_stage(stage, small_sum(stage - 1, small_copies))
        elif stage == 4:
            small_out_ref[...] = small_sum(3, small_copies)
    for slot in back:
        back[slot].wait_recv()
    for copy in started:
        copy.wait_send()


def finish_kernel(ret_ref, sum_ref, small_ref, perm_ref, mixed_ref, gtok_ref, gqkv_ref, gproj_ref, gain_ref, gscale_ref):
    ret = ret_ref[...].astype(F32)
    perm = perm_ref[...]
    mixed = jnp.concatenate([ret[0], ret[2]] + [ret[slot][:QT] for slot in (4, 5, 6, 7)], axis=0).astype(BF)
    gtok = jnp.concatenate([ret[1], ret[3]] + [ret[slot][QT:] for slot in (4, 5, 6, 7)], axis=0).astype(BF)
    mixed_ref[...] = dot(perm, mixed, 0, 0).astype(BF)
    gtok_ref[...] = dot(perm, gtok, 0, 0).astype(BF)
    for half in range(2):
        for p in range(4):
            for i in range(3):
                cols = slice(i * 512 + p * 128, i * 512 + (p + 1) * 128)
                first = p * 1024 + i * 256
                tile = sum_ref[half, first : first + 256]
                gqkv_ref[half * 256 : (half + 1) * 256, cols] = tile.astype(F32)
            for ct in range(4):
                first = p * 1024 + 768 + ct * 64
                tile = sum_ref[half, first : first + 64]
                rows = slice(p * 128 + half * 64, p * 128 + (half + 1) * 64)
                gproj_ref[rows, ct * 128 : (ct + 1) * 128] = tile.astype(F32)
    for i in range(4):
        gain_ref[:, i * 128 : (i + 1) * 128] = small_ref[i : i + 1, :]
    eye = lax.broadcasted_iota(jnp.int32, (8, 128), 0) == lax.broadcasted_iota(jnp.int32, (8, 128), 1)
    row = jnp.sum(jnp.where(eye, small_ref[8:16, :], 0.0), axis=0, keepdims=True)
    gscale_ref[...] = row[:, :8]


VM = pl.BlockSpec(memory_space=pltpu.VMEM)
HBM = pl.BlockSpec(memory_space=pltpu.HBM)
DMA = pltpu.SemaphoreType.DMA
MIB = 1024 * 1024


def per_device(tokens, cotangent, key_keep, norm_gain, w_qkv, w_proj, attn_scale):
    perm, member, place = tables()
    perm = jnp.asarray(perm, BF)
    x = tokens.reshape(288, 512)
    g = cotangent.reshape(288, 512)
    tok = (2 * WIN, 512)
    operands = (
        x, g, key_keep.transpose(1, 0, 2), perm, jnp.asarray(member, BF), jnp.asarray(place, BF),
        w_qkv, w_proj, norm_gain.reshape(1, 512), attn_scale,
    )
    operands = [pltpu.with_memory_space_constraint(operand, pltpu.HBM) for operand in operands]
    ret, total, small = pl.pallas_call(
        block_kernel,
        out_shape=(
            jax.ShapeDtypeStruct((8, ROWS, 512), BF),
            jax.ShapeDtypeStruct((2, 4096, 128), BF),
            jax.ShapeDtypeStruct((16, 128), F32),
        ),
        in_specs=[HBM] * 10,
        out_specs=(VM,) * 3,
        scratch_shapes=[
            pltpu.VMEM((288, 512), BF),
            pltpu.VMEM((288, 512), BF),
            pltpu.VMEM((6, 2, 24), jnp.int32),
            pltpu.VMEM((8 * QT, 288), BF),
            pltpu.VMEM((8, 288), BF),
            pltpu.VMEM((288, 256), BF),
            pltpu.VMEM((512, 1536), BF),
            pltpu.VMEM((512, 512), BF),
            pltpu.VMEM((1, 512), F32),
            pltpu.SMEM((8,), F32),
            pltpu.VMEM((5, ROWS, 512), BF),
            pltpu.VMEM((8, ROWS, 512), BF),
            pltpu.VMEM((8, ROWS, 512), BF),
            pltpu.VMEM(tok, F32),
            pltpu.VMEM(tok, F32),
            pltpu.VMEM((2 * WIN, 128), F32),
            pltpu.VMEM(tok, BF),
            pltpu.VMEM(tok, BF),
            pltpu.VMEM(tok, F32),
            pltpu.VMEM(tok, F32),
        ]
        + [pltpu.VMEM((2, 8, WIN), F32)]
        + [pltpu.VMEM(tok, BF)] * 10
        + [
            pltpu.VMEM((2, WIN, WIN), F32),
            pltpu.VMEM((8, 2, WIN), F32),
            pltpu.VMEM((16, 128), F32),
            pltpu.VMEM((2, 4096, 128), BF),
            pltpu.VMEM((4096, 128), BF),
            pltpu.VMEM((4096, 128), BF),
            pltpu.VMEM((3, 1024, 128), BF),
            pltpu.VMEM((1024, 128), BF),
            pltpu.VMEM((3, 256, 128), BF),
            pltpu.VMEM((4, 256, 128), BF),
            pltpu.VMEM((2, 16, 128), F32),
            pltpu.VMEM((4, 16, 128), F32),
            pltpu.VMEM((4, 16, 128), F32),
            pltpu.VMEM((4, 16, 128), F32),
            DMA((10,)),
            DMA((5,)), DMA((5,)),
            DMA((5,)), DMA((5,)),
            DMA((10,)), DMA((10,)),
            DMA((6, 5, 3)), DMA((6, 5, 3)),
            DMA((10,)), DMA((10,)),
        ],
        compiler_params=pltpu.CompilerParams(collective_id=1, has_side_effects=True, vmem_limit_bytes=40 * MIB),
        name="block",
    )(*operands)

    mixed, gtok, gqkv, gproj, gain, gscale = pl.pallas_call(
        finish_kernel,
        out_shape=(
            jax.ShapeDtypeStruct((288, 512), BF),
            jax.ShapeDtypeStruct((288, 512), BF),
            jax.ShapeDtypeStruct((512, 1536), F32),
            jax.ShapeDtypeStruct((512, 512), F32),
            jax.ShapeDtypeStruct((1, 512), F32),
            jax.ShapeDtypeStruct((1, 8), F32),
        ),
        in_specs=[VM] * 4,
        out_specs=(VM,) * 6,
        compiler_params=pltpu.CompilerParams(vmem_limit_bytes=24 * MIB),
        name="finish",
    )(ret, total, small, perm)
    return (
        mixed.reshape(tokens.shape),
        gtok.reshape(tokens.shape),
        gqkv,
        gproj,
        gain.reshape(512),
        gscale.reshape(8),
    )


def solution(mesh):
    grid = P(None, "lat", "lon", None)
    return jax.shard_map(
        per_device,
        mesh=mesh,
        in_specs=(grid, grid, P(None, "lat", "lon"), P(), P(), P(), P()),
        out_specs=(grid, grid, P(), P(), P(), P()),
        check_vma=False,
    )
```

```python
import functools

import jax
import jax.numpy as jnp
import numpy as np
from jax import lax
from jax.experimental import pallas as pl
from jax.experimental.pallas import tpu as pltpu
from jax.sharding import PartitionSpec as P

EPS_NORM = 1e-05
EPS_DIR = 1e-06
MESH = pl.DeviceIdType.MESH
BF = jnp.bfloat16
F32 = jnp.float32

QUARTERS = ((1, 1), (1, 2), (0, 1), (0, 2), (1, 3), (1, 0), (0, 3), (0, 0))
QT = 40
ROWS = 80
WIN = 160
FLAG_ROW = 36


def token_of(quarter, t):
    half, cq = QUARTERS[quarter]
    lev, rest = divmod(t, 18)
    rr, cc = divmod(rest, 6)
    return lev * 144 + (half * 3 + rr) * 24 + cq * 6 + cc


def tables():
    perm = np.zeros((8 * QT, 288), np.float32)
    member = np.zeros((8, 288), np.float32)
    place = np.zeros((288, 256), np.float32)
    for quarter in range(8):
        for t in range(36):
            src = token_of(quarter, t)
            perm[quarter * QT + t, src] = 1.0
            member[quarter, src] = 1.0
            place[src, QT * (quarter % 4) + t] = 1.0
    return perm, member, place


def dot(a, b, ca=1, cb=0):
    return lax.dot_general(a, b, (((ca,), (cb,)), ((), ())), preferred_element_type=F32)


def position():
    lat = lax.axis_index("lat")
    lon = lax.axis_index("lon")
    return lat, lon


def wrap(value, count):
    return lax.rem(value + count, count)


SLOT_SENDS = ((2, "lat"), (5, "lon"), (7, "diag"), (6, "lat"), (3, "lat"))
KEPT_SLOTS = (0, 1, 4)

GROUPS = (
    (0, 768, "xzy"),
    (768, 512, "yxz"),
    (1280, 768, "zyx"),
    (2048, 512, "xzy"),
    (2560, 256, "yxz"),
    (2816, 256, "zyx"),
    (3072, 256, "xzy"),
    (3328, 256, "yxz"),
    (3584, 512, "zyx"),
)
WAVES = ((0, 1, 2), (3, 4, 5), (6, 7, 8))


def slot_pieces(slot):
    if slot < 4:
        first = 2 * (slot // 2)
        kind = "xg"[slot % 2]
        return ((kind, first), (kind, first + 1))
    return (("x", slot), ("g", slot))


def coordinates():
    lat, lon = position()
    core = lax.rem(lat, 2)
    y = (lat // 2) * 2 + lon // 16
    x = lax.rem(lon // 4, 4)
    z = lax.rem(lon, 4)
    return {"x": x, "y": y, "z": z, "core": core}


def device_at(co):
    return ((co["y"] // 2) * 2 + co["core"], lax.rem(co["y"], 2) * 16 + co["x"] * 4 + co["z"])


def peer(co, axis, j):
    moved = dict(co)
    moved[axis] = lax.rem(co[axis] + j, 4)
    return device_at(moved)


def sibling(co):
    moved = dict(co)
    moved["core"] = 1 - co["core"]
    return device_at(moved)


def block_kernel(
    x_hbm, g_hbm, keep_hbm, perm_hbm, member_hbm, place_hbm, wqkv_hbm, wproj_hbm, gain_hbm, scale_hbm,
    ret_ref, sum_ref, small_out_ref,
    x_ref, g_ref, keep_ref, perm_ref, member_ref, place_ref, wqkv_ref, wproj_ref, gain_ref, scale_ref, in_buf, win_ref, back_ref,
    x_s, xh_s, rstd_s, y_s, g_s, rq_s, rk_s, rq_rows_s, q_s, k_s, qd_s, kd_s, v_s, do_s, dq_s, dk_s, dv_s, att_s, allow_s, gs_s, small_s,
    grads_ref, r0, a1, r1, a2, r2, a3, sv0, sv1, sv2, sv3,
    w_sem, in_send, in_recv, out_send, out_recv, sib_send, sib_recv, st_send, st_recv, sv_send, sv_recv,
):
    lat, lon = position()
    lat_lo, lat_hi = wrap(lat - 1, 4), wrap(lat + 1, 4)
    lon_lo, lon_hi = wrap(lon - 1, 32), wrap(lon + 1, 32)
    co = coordinates()
    core = co["core"]
    sib = sibling(co)
    peers = {axis: [peer(co, axis, j) for j in (1, 2, 3)] for axis in "xyz"}

    loads = {}
    for i, (name, src, dst) in enumerate((
        ("perm", perm_hbm, perm_ref),
        ("x", x_hbm, x_ref),
        ("keep", keep_hbm, keep_ref),
        ("member", member_hbm, member_ref),
        ("place", place_hbm, place_ref),
        ("g", g_hbm, g_ref),
        ("gain", gain_hbm, gain_ref),
        ("qkv", wqkv_hbm, wqkv_ref),
        ("proj", wproj_hbm, wproj_ref),
        ("scale", scale_hbm, scale_ref),
    )):
        loads[name] = pltpu.make_async_copy(src, dst, w_sem.at[i])
    first_loads = ("x", "perm", "keep", "member", "place", "g")
    for name in first_loads:
        loads[name].start()

    barrier = pltpu.get_barrier_semaphore()
    greet = [(lat_lo, lon), (lat, lon_lo), (lat_lo, lon_lo), (lat_hi, lon), (lat, lon_hi), (lat_hi, lon_hi), sib]
    for axis in "xyz":
        greet.extend(peers[axis])
    for dev in greet:
        pl.semaphore_signal(barrier, inc=1, device_id=dev, device_id_type=MESH)

    started = []

    def send(src, dst, s_sem, r_sem, dev):
        copy = pltpu.make_async_remote_copy(
            src_ref=src, dst_ref=dst, send_sem=s_sem, recv_sem=r_sem, device_id=dev, device_id_type=MESH
        )
        copy.start()
        started.append(copy)
        return copy

    for name in first_loads:
        loads[name].wait()
    for name in ("gain", "qkv", "proj", "scale"):
        loads[name].start()
    perm = perm_ref[...]
    xs = dot(perm, x_ref[...])
    gs = dot(perm, g_ref[...])
    keep_rows = [keep_ref[row, lev : lev + 1, :].astype(F32) for lev in range(2) for row in range(6)]
    marks = (jnp.concatenate(keep_rows, axis=1) * member_ref[...].astype(F32)).astype(BF)
    flags = dot(marks, place_ref[...])
    row_id = lax.broadcasted_iota(jnp.int32, (QT, 512), 0)

    def piece(kind, quarter):
        rows = slice(quarter * QT, (quarter + 1) * QT)
        if kind == "g":
            return gs[rows]
        flag = jnp.concatenate([flags[quarter : quarter + 1], jnp.zeros((1, 256), F32)], axis=1)
        return jnp.where(row_id == FLAG_ROW, flag, xs[rows])

    def payload(slot):
        return jnp.concatenate([piece(*p) for p in slot_pieces(slot)], axis=0).astype(BF)

    for i, (slot, _) in enumerate(SLOT_SENDS):
        in_buf[i] = payload(slot)
    pl.semaphore_wait(barrier, len(greet))
    low = {"lat": (lat_lo, lon), "lon": (lat, lon_lo), "diag": (lat_lo, lon_lo)}
    high = {"lat": (lat_hi, lon), "lon": (lat, lon_hi), "diag": (lat_hi, lon_hi)}
    arrive = {}
    for i, (slot, way) in enumerate(SLOT_SENDS):
        arrive[slot] = send(in_buf.at[i], win_ref.at[slot], in_send.at[i], in_recv.at[i], low[way])
    for slot in KEPT_SLOTS:
        win_ref[slot] = payload(slot)
    loads["gain"].wait()
    loads["qkv"].wait()

    gain = gain_ref[...]
    r = lax.broadcasted_iota(jnp.int32, (256, 256), 0)
    c = lax.broadcasted_iota(jnp.int32, (256, 256), 1)
    ones = jnp.where((r // 64) == (c // 64), 1.0, 0.0).astype(BF)

    r = lax.broadcasted_iota(jnp.int32, (8, 512), 0)
    c = lax.broadcasted_iota(jnp.int32, (8, 512), 1)
    head_of = jnp.where(r == c // 64, 1.0, 0.0).astype(BF)

    def head_sum(values):
        hi = values.astype(BF)
        lo = (values - hi.astype(F32)).astype(BF)
        halves = [dot(hi[:, i : i + 256], ones) + dot(lo[:, i : i + 256], ones) for i in (0, 256)]
        return jnp.concatenate(halves, axis=1)

    real = lax.broadcasted_iota(jnp.int32, (QT, 512), 0) < 36
    key_id = lax.broadcasted_iota(jnp.int32, (WIN, WIN), 0)
    query_id = lax.broadcasted_iota(jnp.int32, (WIN, WIN), 1)
    same_half = (key_id >= 2 * QT) == (query_id >= 2 * QT)
    joined = jnp.logical_or(same_half, lat != 3)
    first_row = lax.broadcasted_iota(jnp.int32, (8, WIN), 0) == 0
    one_row = jnp.where(first_row, 1.0, 0.0).astype(BF)

    def front(w):
        rows = slice(w * WIN, (w + 1) * WIN)
        if w == 0:
            data = jnp.concatenate([win_ref[0].astype(F32), win_ref[2].astype(F32)], axis=0)
        else:
            data = jnp.concatenate([win_ref[slot].astype(F32)[:QT] for slot in (4, 5, 6, 7)], axis=0)
        data = data.reshape(4, QT, 512)
        x = jnp.where(real[None], data, 0.0).reshape(WIN, 512)
        marks = data[0, FLAG_ROW : FLAG_ROW + 1, :]
        for i in range(1, 4):
            marks = marks + data[i, FLAG_ROW : FLAG_ROW + 1, :]
        marks = jnp.where(first_row, marks[:, :WIN], 0.0).astype(BF)
        keep = jnp.where(joined, dot(marks, one_row, 0, 0), 0.0)
        allow_s[w] = jnp.where(key_id == query_id, 1.0, keep)
        mean = jnp.mean(x, axis=-1, keepdims=True)
        xc = x - mean
        var = jnp.mean(xc * xc, axis=-1, keepdims=True)
        rstd = lax.rsqrt(var + EPS_NORM)
        xhat = xc * rstd
        y = (xhat * gain).astype(BF)
        x_s[rows] = x
        xh_s[rows] = xhat
        rstd_s[rows] = jnp.broadcast_to(rstd, (WIN, 128))
        y_s[rows] = y
        q_b = dot(y, wqkv_ref[:, 0:512]).astype(BF)
        k_b = dot(y, wqkv_ref[:, 512:1024]).astype(BF)
        q_s[rows] = q_b
        k_s[rows] = k_b
        q = q_b.astype(F32)
        k = k_b.astype(F32)
        v_s[rows] = dot(y, wqkv_ref[:, 1024:1536]).astype(BF)
        q_sq = q * q
        rq = lax.rsqrt(head_sum(q_sq) + EPS_DIR)
        sq_hi = q_sq.astype(BF)
        sq_lo = (q_sq - sq_hi.astype(F32)).astype(BF)
        rq_rows_s[w] = lax.rsqrt(dot(head_of, sq_hi, 1, 1) + dot(head_of, sq_lo, 1, 1) + EPS_DIR)
        rk = lax.rsqrt(head_sum(k * k) + EPS_DIR)
        rq_s[rows] = rq
        rk_s[rows] = rk
        qd_s[rows] = (q * rq).astype(BF)
        kd_s[rows] = (k * rk).astype(BF)

    arrive[2].wait_recv()
    front(0)
    for slot in (5, 7, 6):
        arrive[slot].wait_recv()
    front(1)
    arrive[3].wait_recv()
    g = jnp.concatenate(
        [win_ref[1].astype(F32), win_ref[3].astype(F32)] + [win_ref[slot].astype(F32)[QT:] for slot in (4, 5, 6, 7)],
        axis=0,
    ).astype(BF)
    g_s[...] = g
    loads["proj"].wait()
    loads["scale"].wait()
    do_s[...] = dot(g, wproj_ref[...], 1, 1).astype(BF)
    y_t = jnp.transpose(y_s[...])

    flight = {}

    def send_stage(group, stage, axis, pairs):
        copies = []
        for j in range(3):
            src, dst = pairs(j)
            index = (group, stage, j)
            copies.append(send(src, dst, st_send.at[index], st_recv.at[index], peers[axis][j]))
        flight[group] = copies

    def arrived(group):
        for copy in flight[group]:
            copy.wait_recv()

    def size_of(group, level):
        return GROUPS[group][1] // (4, 16)[level]

    def start_of(group, level):
        return GROUPS[group][0] // (1, 4)[level]

    def own_rows(group, level, j=0):
        first, size = start_of(group, level), size_of(group, level)
        turn = lax.rem(co[GROUPS[group][2][level]] + j, 4)
        return pl.ds(pl.multiple_of(first + turn * size, 16), size)

    def landing(group, level):
        return pl.ds(GROUPS[group][0] // (4, 16)[level], size_of(group, level))

    def scatter(group, level, src, dst):
        def pairs(j):
            return src.at[own_rows(group, level, j + 1)], dst.at[j, landing(group, level)]

        send_stage(group, level, GROUPS[group][2][level], pairs)

    def gathered(group, level, src, dst):
        arrived(group)
        total = src[own_rows(group, level)].astype(F32)
        for j in range(3):
            total = total + dst[j, landing(group, level)].astype(F32)
        return total.astype(BF)

    def final_rows(group, level):
        first, rows, axes = GROUPS[group]
        off = first + co[axes[0]] * (rows // 4)
        if level == 1:
            off = off + co[axes[1]] * (rows // 16)
        return pl.ds(pl.multiple_of(off, 16), size_of(group, level))

    def spread(group, level):
        where = sum_ref.at[core, final_rows(group, level)]
        send_stage(group, 4 - level, GROUPS[group][2][level], lambda j: (where, where))

    sib_in = {}

    def begin(part):
        rows = pl.ds(part * 1024, 1024)
        sib_in[part] = send(grads_ref.at[1 - core, rows], r0.at[rows], sib_send.at[part], sib_recv.at[part], sib)

    def join(part):
        sib_in[part].wait_recv()
        rows = pl.ds(part * 1024, 1024)
        a1[rows] = (grads_ref[core, rows].astype(F32) + r0[rows].astype(F32)).astype(BF)

    def advance(group, stage):
        if stage == 0:
            scatter(group, 0, a1, r1)
        elif stage == 1:
            a2[landing(group, 0)] = gathered(group, 0, a1, r1)
            scatter(group, 1, a2, r2)
        elif stage == 2:
            me = co[GROUPS[group][2][2]]
            a3[me, landing(group, 1)] = gathered(group, 1, a2, r2)
            here = a3.at[me, landing(group, 1)]
            send_stage(group, 2, GROUPS[group][2][2], lambda j: (here, here))
        elif stage == 3:
            arrived(group)
            total = a3[0, landing(group, 1)].astype(F32)
            for i in range(1, 4):
                total = total + a3[i, landing(group, 1)].astype(F32)
            sum_ref[core, final_rows(group, 1)] = total.astype(BF)
            spread(group, 1)
        elif stage == 4:
            arrived(group)
            spread(group, 0)
        elif stage == 5:
            arrived(group)
            whole = sum_ref.at[core, pl.ds(GROUPS[group][0], GROUPS[group][1])]
            flight[group] = [send(whole, whole, sib_send.at[4 + group], sib_recv.at[4 + group], sib)]
        else:
            arrived(group)

    def advance_wave(wave, stage):
        for group in WAVES[wave]:
            advance(group, stage)

    lane = lax.broadcasted_iota(jnp.int32, (1, 128), 1)
    small_ones = ones[:128, :128]

    def pair_of_heads(pair):
        cols = slice(pair * 128, (pair + 1) * 128)
        scales = [scale_ref[pair * 2 + i] for i in range(2)]
        s_lane = jnp.where(lane < 64, scales[0], scales[1])

        def window(w):
            rows = slice(w * WIN, (w + 1) * WIN)
            q_p = q_s[rows, cols]
            k_p = k_s[rows, cols]
            qd_p = qd_s[rows, cols]
            kd_p = kd_s[rows, cols]
            v_p = v_s[rows, cols]
            do_p = do_s[rows, cols]
            allow = allow_s[w]
            acc_o = jnp.zeros((WIN, 128), F32)
            acc_q = jnp.zeros((WIN, 128), F32)
            acc_k = jnp.zeros((WIN, 128), F32)
            acc_v = jnp.zeros((WIN, 128), F32)
            zero = jnp.zeros((WIN, 128), BF)
            for i in range(2):
                s = scales[i]
                mine = jnp.broadcast_to((lane < 64) if i == 0 else (lane >= 64), (WIN, 128))
                qd_h = jnp.where(mine, qd_p, zero)
                kd_h = jnp.where(mine, kd_p, zero)
                v_h = jnp.where(mine, v_p, zero)
                do_h = jnp.where(mine, do_p, zero)
                rq_row = rq_rows_s[w, pair * 2 + i : pair * 2 + i + 1, :]
                rk_col = rk_s[rows, pair * 128 + i * 64 : pair * 128 + i * 64 + 1]
                cos = dot(k_p, jnp.where(mine, q_p, zero), 1, 1) * rk_col * rq_row
                e = jnp.exp(s * cos - s) * allow
                p = e * (1.0 / jnp.sum(e, axis=0, keepdims=True))
                dp = dot(v_p, do_h, 1, 1)
                dl = p * (dp - jnp.sum(p * dp, axis=0, keepdims=True))
                gs_s[w * 4 + pair, i : i + 1, :] = jnp.sum(dl * cos, axis=0, keepdims=True)
                p_b = p.astype(BF)
                dl_b = dl.astype(BF)
                acc_o = acc_o + dot(p_b, v_h, 0, 0)
                acc_v = acc_v + dot(p_b, do_h)
                acc_k = acc_k + dot(dl_b, qd_h)
                acc_q = acc_q + dot(dl_b, kd_h, 0, 0)
            att_s[rows, cols] = acc_o.astype(BF)
            dv_s[rows, cols] = acc_v.astype(BF)
            qd = qd_p.astype(F32)
            kd = kd_p.astype(F32)
            dqd = acc_q * s_lane
            dkd = acc_k * s_lane
            dq_s[rows, cols] = (rq_s[rows, cols] * (dqd - qd * dot((qd * dqd).astype(BF), small_ones))).astype(BF)
            dk_s[rows, cols] = (rk_s[rows, cols] * (dkd - kd * dot((kd * dkd).astype(BF), small_ones))).astype(BF)

        window(0)
        window(1)
        d_all = jnp.concatenate([dq_s[:, cols], dk_s[:, cols], dv_s[:, cols]], axis=1)
        gq = dot(y_t, d_all).astype(BF)
        gp = dot(att_s[:, cols], g_s[...], 0, 0).astype(BF)
        for half in range(2):
            for i in range(3):
                first = pair * 1024 + i * 256
                grads_ref[half, first : first + 256] = gq[half * 256 : (half + 1) * 256, i * 128 : (i + 1) * 128]
            for ct in range(4):
                first = pair * 1024 + 768 + ct * 64
                grads_ref[half, first : first + 64] = gp[half * 64 : (half + 1) * 64, ct * 128 : (ct + 1) * 128]
        begin(pair)

    for pair in range(4):
        pair_of_heads(pair)
        if pair == 2:
            join(0)
            join(1)
            advance_wave(0, 0)
        elif pair == 3:
            join(2)
            advance_wave(1, 0)

    def out_slot(slot, pieces):
        back_ref[slot] = jnp.concatenate(pieces, axis=0).astype(BF)

    back = {}

    def send_back(slots):
        for i, (slot, way) in enumerate(SLOT_SENDS):
            if slot in slots:
                back[slot] = send(back_ref.at[slot], ret_ref.at[slot], out_send.at[i], out_recv.at[i], high[way])

    mixed = x_s[...] + dot(att_s[...], wproj_ref[...])
    for slot in (0, 2):
        out_slot(slot, [mixed[slot * QT : (slot + 2) * QT]])
    send_back((2,))
    dn = dot(dq_s[...], wqkv_ref[:, 0:512], 1, 1)
    dn = dn + dot(dk_s[...], wqkv_ref[:, 512:1024], 1, 1)
    dn = dn + dot(dv_s[...], wqkv_ref[:, 1024:1536], 1, 1)
    xhat = xh_s[...]
    d_gain = jnp.sum(dn * xhat, axis=0, keepdims=True)
    small_s[...] = jnp.zeros((16, 128), F32)
    for i in range(4):
        small_s[i : i + 1, :] = d_gain[:, i * 128 : (i + 1) * 128]
    for h in range(8):
        row = gs_s[h // 2, h % 2 : h % 2 + 1, :] + gs_s[4 + h // 2, h % 2 : h % 2 + 1, :]
        small_s[8 + h : 9 + h, :] = jnp.broadcast_to(jnp.sum(row, axis=1, keepdims=True), (1, 128))

    def small_stage(stage, values):
        axis = ("core", "x", "y", "z")[stage]
        buf = (sv0, sv1, sv2, sv3)[stage]
        me = co[axis]
        buf[me] = values
        copies = []
        for j, dev in enumerate([sib] if stage == 0 else peers[axis]):
            index = 0 if stage == 0 else 1 + 3 * (stage - 1) + j
            copies.append(send(buf.at[me], buf.at[me], sv_send.at[index], sv_recv.at[index], dev))
        return copies

    def small_sum(stage, copies):
        buf = (sv0, sv1, sv2, sv3)[stage]
        for copy in copies:
            copy.wait_recv()
        total = buf[0]
        for i in range(1, 2 if stage == 0 else 4):
            total = total + buf[i]
        return total

    small_copies = small_stage(0, small_s[...])
    dxh = dn * gain
    rstd = rstd_s[:, 0:1]
    dx = rstd * (dxh - jnp.mean(dxh, axis=-1, keepdims=True) - xhat * jnp.mean(dxh * xhat, axis=-1, keepdims=True))
    gtok = g_s[...].astype(F32) + dx
    for slot in (1, 3):
        out_slot(slot, [gtok[(slot - 1) * QT : (slot + 1) * QT]])
    for slot in (4, 5, 6, 7):
        rows = slice(slot * QT, (slot + 1) * QT)
        out_slot(slot, [mixed[rows], gtok[rows]])
    for slot in KEPT_SLOTS:
        ret_ref[slot] = back_ref[slot]
    advance_wave(0, 1)
    join(3)
    advance_wave(2, 0)
    advance_wave(1, 1)
    send_back((5, 7, 6, 3))
    for stage in range(1, 7):
        if stage < 6:
            advance_wave(0, stage + 1)
        advance_wave(2, stage)
        if stage < 6:
            advance_wave(1, stage + 1)
        if stage < 4:
            small_copies = small_stage(stage, small_sum(stage - 1, small_copies))
        elif stage == 4:
            small_out_ref[...] = small_sum(3, small_copies)
    for slot in back:
        back[slot].wait_recv()
    for copy in started:
        copy.wait_send()


def finish_kernel(ret_ref, sum_ref, small_ref, perm_ref, mixed_ref, gtok_ref, gqkv_ref, gproj_ref, gain_ref, gscale_ref):
    ret = ret_ref[...].astype(F32)
    perm = perm_ref[...]
    mixed = jnp.concatenate([ret[0], ret[2]] + [ret[slot][:QT] for slot in (4, 5, 6, 7)], axis=0).astype(BF)
    gtok = jnp.concatenate([ret[1], ret[3]] + [ret[slot][QT:] for slot in (4, 5, 6, 7)], axis=0).astype(BF)
    mixed_ref[...] = dot(perm, mixed, 0, 0).astype(BF)
    gtok_ref[...] = dot(perm, gtok, 0, 0).astype(BF)
    for half in range(2):
        for p in range(4):
            for i in range(3):
                cols = slice(i * 512 + p * 128, i * 512 + (p + 1) * 128)
                first = p * 1024 + i * 256
                tile = sum_ref[half, first : first + 256]
                gqkv_ref[half * 256 : (half + 1) * 256, cols] = tile.astype(F32)
            for ct in range(4):
                first = p * 1024 + 768 + ct * 64
                tile = sum_ref[half, first : first + 64]
                rows = slice(p * 128 + half * 64, p * 128 + (half + 1) * 64)
                gproj_ref[rows, ct * 128 : (ct + 1) * 128] = tile.astype(F32)
    for i in range(4):
        gain_ref[:, i * 128 : (i + 1) * 128] = small_ref[i : i + 1, :]
    eye = lax.broadcasted_iota(jnp.int32, (8, 128), 0) == lax.broadcasted_iota(jnp.int32, (8, 128), 1)
    row = jnp.sum(jnp.where(eye, small_ref[8:16, :], 0.0), axis=0, keepdims=True)
    gscale_ref[...] = row[:, :8]


VM = pl.BlockSpec(memory_space=pltpu.VMEM)
HBM = pl.BlockSpec(memory_space=pltpu.HBM)
DMA = pltpu.SemaphoreType.DMA
MIB = 1024 * 1024


def per_device(tokens, cotangent, key_keep, norm_gain, w_qkv, w_proj, attn_scale):
    perm, member, place = tables()
    perm = jnp.asarray(perm, BF)
    x = tokens.reshape(288, 512)
    g = cotangent.reshape(288, 512)
    tok = (2 * WIN, 512)
    operands = (
        x, g, key_keep.transpose(1, 0, 2), perm, jnp.asarray(member, BF), jnp.asarray(place, BF),
        w_qkv, w_proj, norm_gain.reshape(1, 512), attn_scale,
    )
    operands = [pltpu.with_memory_space_constraint(operand, pltpu.HBM) for operand in operands]
    ret, total, small = pl.pallas_call(
        block_kernel,
        out_shape=(
            jax.ShapeDtypeStruct((8, ROWS, 512), BF),
            jax.ShapeDtypeStruct((2, 4096, 128), BF),
            jax.ShapeDtypeStruct((16, 128), F32),
        ),
        in_specs=[HBM] * 10,
        out_specs=(VM,) * 3,
        scratch_shapes=[
            pltpu.VMEM((288, 512), BF),
            pltpu.VMEM((288, 512), BF),
            pltpu.VMEM((6, 2, 24), jnp.int32),
            pltpu.VMEM((8 * QT, 288), BF),
            pltpu.VMEM((8, 288), BF),
            pltpu.VMEM((288, 256), BF),
            pltpu.VMEM((512, 1536), BF),
            pltpu.VMEM((512, 512), BF),
            pltpu.VMEM((1, 512), F32),
            pltpu.SMEM((8,), F32),
            pltpu.VMEM((5, ROWS, 512), BF),
            pltpu.VMEM((8, ROWS, 512), BF),
            pltpu.VMEM((8, ROWS, 512), BF),
            pltpu.VMEM(tok, F32),
            pltpu.VMEM(tok, F32),
            pltpu.VMEM((2 * WIN, 128), F32),
            pltpu.VMEM(tok, BF),
            pltpu.VMEM(tok, BF),
            pltpu.VMEM(tok, F32),
            pltpu.VMEM(tok, F32),
        ]
        + [pltpu.VMEM((2, 8, WIN), F32)]
        + [pltpu.VMEM(tok, BF)] * 10
        + [
            pltpu.VMEM((2, WIN, WIN), F32),
            pltpu.VMEM((8, 2, WIN), F32),
            pltpu.VMEM((16, 128), F32),
            pltpu.VMEM((2, 4096, 128), BF),
            pltpu.VMEM((4096, 128), BF),
            pltpu.VMEM((4096, 128), BF),
            pltpu.VMEM((3, 1024, 128), BF),
            pltpu.VMEM((1024, 128), BF),
            pltpu.VMEM((3, 256, 128), BF),
            pltpu.VMEM((4, 256, 128), BF),
            pltpu.VMEM((2, 16, 128), F32),
            pltpu.VMEM((4, 16, 128), F32),
            pltpu.VMEM((4, 16, 128), F32),
            pltpu.VMEM((4, 16, 128), F32),
            DMA((10,)),
            DMA((5,)), DMA((5,)),
            DMA((5,)), DMA((5,)),
            DMA((13,)), DMA((13,)),
            DMA((9, 5, 3)), DMA((9, 5, 3)),
            DMA((10,)), DMA((10,)),
        ],
        compiler_params=pltpu.CompilerParams(collective_id=1, has_side_effects=True, vmem_limit_bytes=40 * MIB),
        name="block",
    )(*operands)

    mixed, gtok, gqkv, gproj, gain, gscale = pl.pallas_call(
        finish_kernel,
        out_shape=(
            jax.ShapeDtypeStruct((288, 512), BF),
            jax.ShapeDtypeStruct((288, 512), BF),
            jax.ShapeDtypeStruct((512, 1536), F32),
            jax.ShapeDtypeStruct((512, 512), F32),
            jax.ShapeDtypeStruct((1, 512), F32),
            jax.ShapeDtypeStruct((1, 8), F32),
        ),
        in_specs=[VM] * 4,
        out_specs=(VM,) * 6,
        compiler_params=pltpu.CompilerParams(vmem_limit_bytes=24 * MIB),
        name="finish",
    )(ret, total, small, perm)
    return (
        mixed.reshape(tokens.shape),
        gtok.reshape(tokens.shape),
        gqkv,
        gproj,
        gain.reshape(512),
        gscale.reshape(8),
    )


def solution(mesh):
    grid = P(None, "lat", "lon", None)
    return jax.shard_map(
        per_device,
        mesh=mesh,
        in_specs=(grid, grid, P(None, "lat", "lon"), P(), P(), P(), P()),
        out_specs=(grid, grid, P(), P(), P(), P()),
        check_vma=False,
    )
```

```python
import functools

import jax
import jax.numpy as jnp
import numpy as np
from jax import lax
from jax.experimental import pallas as pl
from jax.experimental.pallas import tpu as pltpu
from jax.sharding import PartitionSpec as P

EPS_NORM = 1e-05
EPS_DIR = 1e-06
MESH = pl.DeviceIdType.MESH
BF = jnp.bfloat16
F32 = jnp.float32

QUARTERS = ((1, 1), (1, 2), (0, 1), (0, 2), (1, 3), (1, 0), (0, 3), (0, 0))
QT = 40
ROWS = 80
WIN = 160
FLAG_ROW = 36


def token_of(quarter, t):
    half, cq = QUARTERS[quarter]
    lev, rest = divmod(t, 18)
    rr, cc = divmod(rest, 6)
    return lev * 144 + (half * 3 + rr) * 24 + cq * 6 + cc


def tables():
    perm = np.zeros((8 * QT, 288), np.float32)
    member = np.zeros((8, 288), np.float32)
    place = np.zeros((288, 256), np.float32)
    for quarter in range(8):
        for t in range(36):
            src = token_of(quarter, t)
            perm[quarter * QT + t, src] = 1.0
            member[quarter, src] = 1.0
            place[src, QT * (quarter % 4) + t] = 1.0
    return perm, member, place


def dot(a, b, ca=1, cb=0):
    return lax.dot_general(a, b, (((ca,), (cb,)), ((), ())), preferred_element_type=F32)


def position():
    lat = lax.axis_index("lat")
    lon = lax.axis_index("lon")
    return lat, lon


def wrap(value, count):
    return lax.rem(value + count, count)


SLOT_SENDS = ((2, "lat"), (5, "lon"), (7, "diag"), (6, "lat"), (3, "lat"))
KEPT_SLOTS = (0, 1, 4)

GROUPS = (
    (0, 768, "xzy"),
    (768, 512, "yxz"),
    (1280, 768, "zyx"),
    (2048, 768, "xzy"),
    (2816, 512, "yxz"),
    (3328, 768, "zyx"),
)
WAVES = ((0, 1, 2), (3, 4, 5))


def slot_pieces(slot):
    if slot < 4:
        first = 2 * (slot // 2)
        kind = "xg"[slot % 2]
        return ((kind, first), (kind, first + 1))
    return (("x", slot), ("g", slot))


def coordinates():
    lat, lon = position()
    core = lax.rem(lat, 2)
    y = (lat // 2) * 2 + lon // 16
    x = lax.rem(lon // 4, 4)
    z = lax.rem(lon, 4)
    return {"x": x, "y": y, "z": z, "core": core}


def device_at(co):
    return ((co["y"] // 2) * 2 + co["core"], lax.rem(co["y"], 2) * 16 + co["x"] * 4 + co["z"])


def peer(co, axis, j):
    moved = dict(co)
    moved[axis] = lax.rem(co[axis] + j, 4)
    return device_at(moved)


def sibling(co):
    moved = dict(co)
    moved["core"] = 1 - co["core"]
    return device_at(moved)


def block_kernel(
    x_hbm, g_hbm, keep_hbm, perm_hbm, member_hbm, place_hbm, wqkv_hbm, wproj_hbm, gain_hbm, scale_hbm,
    ret_ref, sum_ref, small_out_ref,
    x_ref, g_ref, keep_ref, perm_ref, member_ref, place_ref, wqkv_ref, wproj_ref, gain_ref, scale_ref, in_buf, win_ref, back_ref,
    x_s, xh_s, rstd_s, y_s, g_s, rq_s, rk_s, rq_rows_s, q_s, k_s, qd_s, kd_s, v_s, do_s, dq_s, dk_s, dv_s, att_s, allow_s, gs_s, small_s,
    grads_ref, r0, a1, r1, a2, r2, a3, sv0, sv1, sv2, sv3,
    w_sem, in_send, in_recv, out_send, out_recv, sib_send, sib_recv, st_send, st_recv, sv_send, sv_recv,
):
    lat, lon = position()
    lat_lo, lat_hi = wrap(lat - 1, 4), wrap(lat + 1, 4)
    lon_lo, lon_hi = wrap(lon - 1, 32), wrap(lon + 1, 32)
    co = coordinates()
    core = co["core"]
    sib = sibling(co)
    peers = {axis: [peer(co, axis, j) for j in (1, 2, 3)] for axis in "xyz"}

    loads = {}
    for i, (name, src, dst) in enumerate((
        ("perm", perm_hbm, perm_ref),
        ("x", x_hbm, x_ref),
        ("keep", keep_hbm, keep_ref),
        ("member", member_hbm, member_ref),
        ("place", place_hbm, place_ref),
        ("g", g_hbm, g_ref),
        ("gain", gain_hbm, gain_ref),
        ("qkv", wqkv_hbm, wqkv_ref),
        ("proj", wproj_hbm, wproj_ref),
        ("scale", scale_hbm, scale_ref),
    )):
        loads[name] = pltpu.make_async_copy(src, dst, w_sem.at[i])
    first_loads = ("x", "perm", "keep", "member", "place", "g")
    for name in first_loads:
        loads[name].start()

    barrier = pltpu.get_barrier_semaphore()
    greet = [(lat_lo, lon), (lat, lon_lo), (lat_lo, lon_lo), (lat_hi, lon), (lat, lon_hi), (lat_hi, lon_hi), sib]
    for axis in "xyz":
        greet.extend(peers[axis])
    for dev in greet:
        pl.semaphore_signal(barrier, inc=1, device_id=dev, device_id_type=MESH)

    started = []

    def send(src, dst, s_sem, r_sem, dev):
        copy = pltpu.make_async_remote_copy(
            src_ref=src, dst_ref=dst, send_sem=s_sem, recv_sem=r_sem, device_id=dev, device_id_type=MESH
        )
        copy.start()
        started.append(copy)
        return copy

    for name in first_loads:
        loads[name].wait()
    for name in ("gain", "qkv", "proj", "scale"):
        loads[name].start()
    perm = perm_ref[...]
    xs = dot(perm, x_ref[...])
    gs = dot(perm, g_ref[...])
    keep_rows = [keep_ref[row, lev : lev + 1, :].astype(F32) for lev in range(2) for row in range(6)]
    marks = (jnp.concatenate(keep_rows, axis=1) * member_ref[...].astype(F32)).astype(BF)
    flags = dot(marks, place_ref[...])
    row_id = lax.broadcasted_iota(jnp.int32, (QT, 512), 0)

    def piece(kind, quarter):
        rows = slice(quarter * QT, (quarter + 1) * QT)
        if kind == "g":
            return gs[rows]
        flag = jnp.concatenate([flags[quarter : quarter + 1], jnp.zeros((1, 256), F32)], axis=1)
        return jnp.where(row_id == FLAG_ROW, flag, xs[rows])

    def payload(slot):
        return jnp.concatenate([piece(*p) for p in slot_pieces(slot)], axis=0).astype(BF)

    for i, (slot, _) in enumerate(SLOT_SENDS):
        in_buf[i] = payload(slot)
    pl.semaphore_wait(barrier, len(greet))
    low = {"lat": (lat_lo, lon), "lon": (lat, lon_lo), "diag": (lat_lo, lon_lo)}
    high = {"lat": (lat_hi, lon), "lon": (lat, lon_hi), "diag": (lat_hi, lon_hi)}
    arrive = {}
    for i, (slot, way) in enumerate(SLOT_SENDS):
        arrive[slot] = send(in_buf.at[i], win_ref.at[slot], in_send.at[i], in_recv.at[i], low[way])
    for slot in KEPT_SLOTS:
        win_ref[slot] = payload(slot)
    loads["gain"].wait()
    loads["qkv"].wait()

    gain = gain_ref[...]
    r = lax.broadcasted_iota(jnp.int32, (256, 256), 0)
    c = lax.broadcasted_iota(jnp.int32, (256, 256), 1)
    ones = jnp.where((r // 64) == (c // 64), 1.0, 0.0).astype(BF)

    r = lax.broadcasted_iota(jnp.int32, (8, 512), 0)
    c = lax.broadcasted_iota(jnp.int32, (8, 512), 1)
    head_of = jnp.where(r == c // 64, 1.0, 0.0).astype(BF)

    def head_sum(values):
        hi = values.astype(BF)
        lo = (values - hi.astype(F32)).astype(BF)
        halves = [dot(hi[:, i : i + 256], ones) + dot(lo[:, i : i + 256], ones) for i in (0, 256)]
        return jnp.concatenate(halves, axis=1)

    real = lax.broadcasted_iota(jnp.int32, (QT, 512), 0) < 36
    key_id = lax.broadcasted_iota(jnp.int32, (WIN, WIN), 0)
    query_id = lax.broadcasted_iota(jnp.int32, (WIN, WIN), 1)
    same_half = (key_id >= 2 * QT) == (query_id >= 2 * QT)
    joined = jnp.logical_or(same_half, lat != 3)
    first_row = lax.broadcasted_iota(jnp.int32, (8, WIN), 0) == 0
    one_row = jnp.where(first_row, 1.0, 0.0).astype(BF)

    def front(w):
        rows = slice(w * WIN, (w + 1) * WIN)
        if w == 0:
            data = jnp.concatenate([win_ref[0].astype(F32), win_ref[2].astype(F32)], axis=0)
        else:
            data = jnp.concatenate([win_ref[slot].astype(F32)[:QT] for slot in (4, 5, 6, 7)], axis=0)
        data = data.reshape(4, QT, 512)
        x = jnp.where(real[None], data, 0.0).reshape(WIN, 512)
        marks = data[0, FLAG_ROW : FLAG_ROW + 1, :]
        for i in range(1, 4):
            marks = marks + data[i, FLAG_ROW : FLAG_ROW + 1, :]
        marks = jnp.where(first_row, marks[:, :WIN], 0.0).astype(BF)
        keep = jnp.where(joined, dot(marks, one_row, 0, 0), 0.0)
        allow_s[w] = jnp.where(key_id == query_id, 1.0, keep)
        mean = jnp.mean(x, axis=-1, keepdims=True)
        xc = x - mean
        var = jnp.mean(xc * xc, axis=-1, keepdims=True)
        rstd = lax.rsqrt(var + EPS_NORM)
        xhat = xc * rstd
        y = (xhat * gain).astype(BF)
        x_s[rows] = x
        xh_s[rows] = xhat
        rstd_s[rows] = jnp.broadcast_to(rstd, (WIN, 128))
        y_s[rows] = y
        q_b = dot(y, wqkv_ref[:, 0:512]).astype(BF)
        k_b = dot(y, wqkv_ref[:, 512:1024]).astype(BF)
        q_s[rows] = q_b
        k_s[rows] = k_b
        q = q_b.astype(F32)
        k = k_b.astype(F32)
        v_s[rows] = dot(y, wqkv_ref[:, 1024:1536]).astype(BF)
        q_sq = q * q
        rq = lax.rsqrt(head_sum(q_sq) + EPS_DIR)
        sq_hi = q_sq.astype(BF)
        sq_lo = (q_sq - sq_hi.astype(F32)).astype(BF)
        rq_rows_s[w] = lax.rsqrt(dot(head_of, sq_hi, 1, 1) + dot(head_of, sq_lo, 1, 1) + EPS_DIR)
        rk = lax.rsqrt(head_sum(k * k) + EPS_DIR)
        rq_s[rows] = rq
        rk_s[rows] = rk
        qd_s[rows] = (q * rq).astype(BF)
        kd_s[rows] = (k * rk).astype(BF)

    arrive[2].wait_recv()
    front(0)
    for slot in (5, 7, 6):
        arrive[slot].wait_recv()
    front(1)
    arrive[3].wait_recv()
    g = jnp.concatenate(
        [win_ref[1].astype(F32), win_ref[3].astype(F32)] + [win_ref[slot].astype(F32)[QT:] for slot in (4, 5, 6, 7)],
        axis=0,
    ).astype(BF)
    g_s[...] = g
    loads["proj"].wait()
    loads["scale"].wait()
    do_s[...] = dot(g, wproj_ref[...], 1, 1).astype(BF)
    y_t = jnp.transpose(y_s[...])

    flight = {}

    def send_stage(group, stage, axis, pairs):
        copies = []
        for j in range(3):
            src, dst = pairs(j)
            index = (group, stage, j)
            copies.append(send(src, dst, st_send.at[index], st_recv.at[index], peers[axis][j]))
        flight[group] = copies

    def arrived(group):
        for copy in flight[group]:
            copy.wait_recv()

    def size_of(group, level):
        return GROUPS[group][1] // (4, 16)[level]

    def start_of(group, level):
        return GROUPS[group][0] // (1, 4)[level]

    def own_rows(group, level, j=0):
        first, size = start_of(group, level), size_of(group, level)
        turn = lax.rem(co[GROUPS[group][2][level]] + j, 4)
        return pl.ds(pl.multiple_of(first + turn * size, 16), size)

    def landing(group, level):
        return pl.ds(GROUPS[group][0] // (4, 16)[level], size_of(group, level))

    def scatter(group, level, src, dst):
        def pairs(j):
            return src.at[own_rows(group, level, j + 1)], dst.at[j, landing(group, level)]

        send_stage(group, level, GROUPS[group][2][level], pairs)

    def gathered(group, level, src, dst):
        arrived(group)
        total = src[own_rows(group, level)].astype(F32)
        for j in range(3):
            total = total + dst[j, landing(group, level)].astype(F32)
        return total.astype(BF)

    def final_rows(group, level):
        first, rows, axes = GROUPS[group]
        off = first + co[axes[0]] * (rows // 4)
        if level == 1:
            off = off + co[axes[1]] * (rows // 16)
        return pl.ds(pl.multiple_of(off, 16), size_of(group, level))

    def spread(group, level):
        where = sum_ref.at[core, final_rows(group, level)]
        send_stage(group, 4 - level, GROUPS[group][2][level], lambda j: (where, where))

    sib_in = {}

    def begin(part):
        rows = pl.ds(part * 1024, 1024)
        sib_in[part] = send(grads_ref.at[1 - core, rows], r0.at[rows], sib_send.at[part], sib_recv.at[part], sib)

    def join(part):
        sib_in[part].wait_recv()
        rows = pl.ds(part * 1024, 1024)
        a1[rows] = (grads_ref[core, rows].astype(F32) + r0[rows].astype(F32)).astype(BF)

    def advance(group, stage):
        if stage == 0:
            scatter(group, 0, a1, r1)
        elif stage == 1:
            a2[landing(group, 0)] = gathered(group, 0, a1, r1)
            scatter(group, 1, a2, r2)
        elif stage == 2:
            me = co[GROUPS[group][2][2]]
            a3[me, landing(group, 1)] = gathered(group, 1, a2, r2)
            here = a3.at[me, landing(group, 1)]
            send_stage(group, 2, GROUPS[group][2][2], lambda j: (here, here))
        elif stage == 3:
            arrived(group)
            total = a3[0, landing(group, 1)].astype(F32)
            for i in range(1, 4):
                total = total + a3[i, landing(group, 1)].astype(F32)
            sum_ref[core, final_rows(group, 1)] = total.astype(BF)
            spread(group, 1)
        elif stage == 4:
            arrived(group)
            spread(group, 0)
        elif stage == 5:
            arrived(group)
            whole = sum_ref.at[core, pl.ds(GROUPS[group][0], GROUPS[group][1])]
            flight[group] = [send(whole, whole, sib_send.at[4 + group], sib_recv.at[4 + group], sib)]
        else:
            arrived(group)

    def advance_wave(wave, stage):
        for group in WAVES[wave]:
            advance(group, stage)

    lane = lax.broadcasted_iota(jnp.int32, (1, 128), 1)
    small_ones = ones[:128, :128]

    def pair_of_heads(pair):
        cols = slice(pair * 128, (pair + 1) * 128)
        scales = [scale_ref[pair * 2 + i] for i in range(2)]
        s_lane = jnp.where(lane < 64, scales[0], scales[1])

        def window(w):
            rows = slice(w * WIN, (w + 1) * WIN)
            q_p = q_s[rows, cols]
            k_p = k_s[rows, cols]
            qd_p = qd_s[rows, cols]
            kd_p = kd_s[rows, cols]
            v_p = v_s[rows, cols]
            do_p = do_s[rows, cols]
            allow = allow_s[w]
            acc_o = jnp.zeros((WIN, 128), F32)
            acc_q = jnp.zeros((WIN, 128), F32)
            acc_k = jnp.zeros((WIN, 128), F32)
            acc_v = jnp.zeros((WIN, 128), F32)
            zero = jnp.zeros((WIN, 128), BF)
            for i in range(2):
                s = scales[i]
                mine = jnp.broadcast_to((lane < 64) if i == 0 else (lane >= 64), (WIN, 128))
                qd_h = jnp.where(mine, qd_p, zero)
                kd_h = jnp.where(mine, kd_p, zero)
                v_h = jnp.where(mine, v_p, zero)
                do_h = jnp.where(mine, do_p, zero)
                rq_row = rq_rows_s[w, pair * 2 + i : pair * 2 + i + 1, :]
                rk_col = rk_s[rows, pair * 128 + i * 64 : pair * 128 + i * 64 + 1]
                cos = dot(k_p, jnp.where(mine, q_p, zero), 1, 1) * rk_col * rq_row
                e = jnp.exp(s * cos - s) * allow
                p = e * (1.0 / jnp.sum(e, axis=0, keepdims=True))
                dp = dot(v_p, do_h, 1, 1)
                dl = p * (dp - jnp.sum(p * dp, axis=0, keepdims=True))
                gs_s[w * 4 + pair, i : i + 1, :] = jnp.sum(dl * cos, axis=0, keepdims=True)
                p_b = p.astype(BF)
                dl_b = dl.astype(BF)
                acc_o = acc_o + dot(p_b, v_h, 0, 0)
                acc_v = acc_v + dot(p_b, do_h)
                acc_k = acc_k + dot(dl_b, qd_h)
                acc_q = acc_q + dot(dl_b, kd_h, 0, 0)
            att_s[rows, cols] = acc_o.astype(BF)
            dv_s[rows, cols] = acc_v.astype(BF)
            qd = qd_p.astype(F32)
            kd = kd_p.astype(F32)
            dqd = acc_q * s_lane
            dkd = acc_k * s_lane
            dq_s[rows, cols] = (rq_s[rows, cols] * (dqd - qd * dot((qd * dqd).astype(BF), small_ones))).astype(BF)
            dk_s[rows, cols] = (rk_s[rows, cols] * (dkd - kd * dot((kd * dkd).astype(BF), small_ones))).astype(BF)

        window(0)
        window(1)
        d_all = jnp.concatenate([dq_s[:, cols], dk_s[:, cols], dv_s[:, cols]], axis=1)
        gq = dot(y_t, d_all).astype(BF)
        gp = dot(att_s[:, cols], g_s[...], 0, 0).astype(BF)
        for half in range(2):
            for i in range(3):
                first = pair * 1024 + i * 256
                grads_ref[half, first : first + 256] = gq[half * 256 : (half + 1) * 256, i * 128 : (i + 1) * 128]
            for ct in range(4):
                first = pair * 1024 + 768 + ct * 64
                grads_ref[half, first : first + 64] = gp[half * 64 : (half + 1) * 64, ct * 128 : (ct + 1) * 128]
        begin(pair)

    for pair in range(4):
        pair_of_heads(pair)
        if pair == 2:
            join(0)
            join(1)
            advance_wave(0, 0)

    def out_slot(slot, pieces):
        back_ref[slot] = jnp.concatenate(pieces, axis=0).astype(BF)

    back = {}

    def send_back(slots):
        for i, (slot, way) in enumerate(SLOT_SENDS):
            if slot in slots:
                back[slot] = send(back_ref.at[slot], ret_ref.at[slot], out_send.at[i], out_recv.at[i], high[way])

    mixed = x_s[...] + dot(att_s[...], wproj_ref[...])
    for slot in (0, 2):
        out_slot(slot, [mixed[slot * QT : (slot + 2) * QT]])
    send_back((2,))
    dn = dot(dq_s[...], wqkv_ref[:, 0:512], 1, 1)
    dn = dn + dot(dk_s[...], wqkv_ref[:, 512:1024], 1, 1)
    dn = dn + dot(dv_s[...], wqkv_ref[:, 1024:1536], 1, 1)
    xhat = xh_s[...]
    d_gain = jnp.sum(dn * xhat, axis=0, keepdims=True)
    small_s[...] = jnp.zeros((16, 128), F32)
    for i in range(4):
        small_s[i : i + 1, :] = d_gain[:, i * 128 : (i + 1) * 128]
    for h in range(8):
        row = gs_s[h // 2, h % 2 : h % 2 + 1, :] + gs_s[4 + h // 2, h % 2 : h % 2 + 1, :]
        small_s[8 + h : 9 + h, :] = jnp.broadcast_to(jnp.sum(row, axis=1, keepdims=True), (1, 128))

    def small_stage(stage, values):
        axis = ("core", "x", "y", "z")[stage]
        buf = (sv0, sv1, sv2, sv3)[stage]
        me = co[axis]
        buf[me] = values
        copies = []
        for j, dev in enumerate([sib] if stage == 0 else peers[axis]):
            index = 0 if stage == 0 else 1 + 3 * (stage - 1) + j
            copies.append(send(buf.at[me], buf.at[me], sv_send.at[index], sv_recv.at[index], dev))
        return copies

    def small_sum(stage, copies):
        buf = (sv0, sv1, sv2, sv3)[stage]
        for copy in copies:
            copy.wait_recv()
        total = buf[0]
        for i in range(1, 2 if stage == 0 else 4):
            total = total + buf[i]
        return total

    small_copies = small_stage(0, small_s[...])
    dxh = dn * gain
    rstd = rstd_s[:, 0:1]
    dx = rstd * (dxh - jnp.mean(dxh, axis=-1, keepdims=True) - xhat * jnp.mean(dxh * xhat, axis=-1, keepdims=True))
    gtok = g_s[...].astype(F32) + dx
    for slot in (1, 3):
        out_slot(slot, [gtok[(slot - 1) * QT : (slot + 1) * QT]])
    for slot in (4, 5, 6, 7):
        rows = slice(slot * QT, (slot + 1) * QT)
        out_slot(slot, [mixed[rows], gtok[rows]])
    for slot in KEPT_SLOTS:
        ret_ref[slot] = back_ref[slot]
    join(2)
    join(3)
    advance_wave(1, 0)
    send_back((5, 7, 6, 3))
    for stage in range(1, 7):
        departed = len(started)
        advance_wave(0, stage)
        advance_wave(1, stage)
        if stage < 4:
            small_copies = small_stage(stage, small_sum(stage - 1, small_copies))
        elif stage == 4:
            small_out_ref[...] = small_sum(3, small_copies)
            for slot in back:
                back[slot].wait_recv()
        if stage < 6:
            for copy in started[:departed]:
                copy.wait_send()
            del started[:departed]
    for copy in started:
        copy.wait_send()


def finish_kernel(ret_ref, sum_ref, small_ref, perm_ref, mixed_ref, gtok_ref, gqkv_ref, gproj_ref, gain_ref, gscale_ref):
    ret = ret_ref[...].astype(F32)
    perm = perm_ref[...]
    mixed = jnp.concatenate([ret[0], ret[2]] + [ret[slot][:QT] for slot in (4, 5, 6, 7)], axis=0).astype(BF)
    gtok = jnp.concatenate([ret[1], ret[3]] + [ret[slot][QT:] for slot in (4, 5, 6, 7)], axis=0).astype(BF)
    mixed_ref[...] = dot(perm, mixed, 0, 0).astype(BF)
    gtok_ref[...] = dot(perm, gtok, 0, 0).astype(BF)
    for half in range(2):
        for p in range(4):
            for i in range(3):
                cols = slice(i * 512 + p * 128, i * 512 + (p + 1) * 128)
                first = p * 1024 + i * 256
                tile = sum_ref[half, first : first + 256]
                gqkv_ref[half * 256 : (half + 1) * 256, cols] = tile.astype(F32)
            for ct in range(4):
                first = p * 1024 + 768 + ct * 64
                tile = sum_ref[half, first : first + 64]
                rows = slice(p * 128 + half * 64, p * 128 + (half + 1) * 64)
                gproj_ref[rows, ct * 128 : (ct + 1) * 128] = tile.astype(F32)
    for i in range(4):
        gain_ref[:, i * 128 : (i + 1) * 128] = small_ref[i : i + 1, :]
    eye = lax.broadcasted_iota(jnp.int32, (8, 128), 0) == lax.broadcasted_iota(jnp.int32, (8, 128), 1)
    row = jnp.sum(jnp.where(eye, small_ref[8:16, :], 0.0), axis=0, keepdims=True)
    gscale_ref[...] = row[:, :8]


VM = pl.BlockSpec(memory_space=pltpu.VMEM)
HBM = pl.BlockSpec(memory_space=pltpu.HBM)
DMA = pltpu.SemaphoreType.DMA
MIB = 1024 * 1024


def per_device(tokens, cotangent, key_keep, norm_gain, w_qkv, w_proj, attn_scale):
    perm, member, place = tables()
    perm = jnp.asarray(perm, BF)
    x = tokens.reshape(288, 512)
    g = cotangent.reshape(288, 512)
    tok = (2 * WIN, 512)
    operands = (
        x, g, key_keep.transpose(1, 0, 2), perm, jnp.asarray(member, BF), jnp.asarray(place, BF),
        w_qkv, w_proj, norm_gain.reshape(1, 512), attn_scale,
    )
    operands = [pltpu.with_memory_space_constraint(operand, pltpu.HBM) for operand in operands]
    ret, total, small = pl.pallas_call(
        block_kernel,
        out_shape=(
            jax.ShapeDtypeStruct((8, ROWS, 512), BF),
            jax.ShapeDtypeStruct((2, 4096, 128), BF),
            jax.ShapeDtypeStruct((16, 128), F32),
        ),
        in_specs=[HBM] * 10,
        out_specs=(VM,) * 3,
        scratch_shapes=[
            pltpu.VMEM((288, 512), BF),
            pltpu.VMEM((288, 512), BF),
            pltpu.VMEM((6, 2, 24), jnp.int32),
            pltpu.VMEM((8 * QT, 288), BF),
            pltpu.VMEM((8, 288), BF),
            pltpu.VMEM((288, 256), BF),
            pltpu.VMEM((512, 1536), BF),
            pltpu.VMEM((512, 512), BF),
            pltpu.VMEM((1, 512), F32),
            pltpu.SMEM((8,), F32),
            pltpu.VMEM((5, ROWS, 512), BF),
            pltpu.VMEM((8, ROWS, 512), BF),
            pltpu.VMEM((8, ROWS, 512), BF),
            pltpu.VMEM(tok, F32),
            pltpu.VMEM(tok, F32),
            pltpu.VMEM((2 * WIN, 128), F32),
            pltpu.VMEM(tok, BF),
            pltpu.VMEM(tok, BF),
            pltpu.VMEM(tok, F32),
            pltpu.VMEM(tok, F32),
        ]
        + [pltpu.VMEM((2, 8, WIN), F32)]
        + [pltpu.VMEM(tok, BF)] * 10
        + [
            pltpu.VMEM((2, WIN, WIN), F32),
            pltpu.VMEM((8, 2, WIN), F32),
            pltpu.VMEM((16, 128), F32),
            pltpu.VMEM((2, 4096, 128), BF),
            pltpu.VMEM((4096, 128), BF),
            pltpu.VMEM((4096, 128), BF),
            pltpu.VMEM((3, 1024, 128), BF),
            pltpu.VMEM((1024, 128), BF),
            pltpu.VMEM((3, 256, 128), BF),
            pltpu.VMEM((4, 256, 128), BF),
            pltpu.VMEM((2, 16, 128), F32),
            pltpu.VMEM((4, 16, 128), F32),
            pltpu.VMEM((4, 16, 128), F32),
            pltpu.VMEM((4, 16, 128), F32),
            DMA((10,)),
            DMA((5,)), DMA((5,)),
            DMA((5,)), DMA((5,)),
            DMA((10,)), DMA((10,)),
            DMA((6, 5, 3)), DMA((6, 5, 3)),
            DMA((10,)), DMA((10,)),
        ],
        compiler_params=pltpu.CompilerParams(collective_id=1, has_side_effects=True, vmem_limit_bytes=40 * MIB),
        name="block",
    )(*operands)

    mixed, gtok, gqkv, gproj, gain, gscale = pl.pallas_call(
        finish_kernel,
        out_shape=(
            jax.ShapeDtypeStruct((288, 512), BF),
            jax.ShapeDtypeStruct((288, 512), BF),
            jax.ShapeDtypeStruct((512, 1536), F32),
            jax.ShapeDtypeStruct((512, 512), F32),
            jax.ShapeDtypeStruct((1, 512), F32),
            jax.ShapeDtypeStruct((1, 8), F32),
        ),
        in_specs=[VM] * 4,
        out_specs=(VM,) * 6,
        compiler_params=pltpu.CompilerParams(vmem_limit_bytes=24 * MIB),
        name="finish",
    )(ret, total, small, perm)
    return (
        mixed.reshape(tokens.shape),
        gtok.reshape(tokens.shape),
        gqkv,
        gproj,
        gain.reshape(512),
        gscale.reshape(8),
    )


def solution(mesh):
    grid = P(None, "lat", "lon", None)
    return jax.shard_map(
        per_device,
        mesh=mesh,
        in_specs=(grid, grid, P(None, "lat", "lon"), P(), P(), P(), P()),
        out_specs=(grid, grid, P(), P(), P(), P()),
        check_vma=False,
    )
```

```python
import functools

import jax
import jax.numpy as jnp
import numpy as np
from jax import lax
from jax.experimental import pallas as pl
from jax.experimental.pallas import tpu as pltpu
from jax.sharding import PartitionSpec as P

EPS_NORM = 1e-05
EPS_DIR = 1e-06
MESH = pl.DeviceIdType.MESH
BF = jnp.bfloat16
F32 = jnp.float32

QUARTERS = ((1, 1), (1, 2), (0, 1), (0, 2), (1, 3), (1, 0), (0, 3), (0, 0))
QT = 40
ROWS = 80
WIN = 160
FLAG_ROW = 36


def token_of(quarter, t):
    half, cq = QUARTERS[quarter]
    lev, rest = divmod(t, 18)
    rr, cc = divmod(rest, 6)
    return lev * 144 + (half * 3 + rr) * 24 + cq * 6 + cc


def tables():
    perm = np.zeros((8 * QT, 288), np.float32)
    member = np.zeros((8, 288), np.float32)
    place = np.zeros((288, 256), np.float32)
    for quarter in range(8):
        for t in range(36):
            src = token_of(quarter, t)
            perm[quarter * QT + t, src] = 1.0
            member[quarter, src] = 1.0
            place[src, QT * (quarter % 4) + t] = 1.0
    return perm, member, place


def dot(a, b, ca=1, cb=0):
    return lax.dot_general(a, b, (((ca,), (cb,)), ((), ())), preferred_element_type=F32)


def position():
    lat = lax.axis_index("lat")
    lon = lax.axis_index("lon")
    return lat, lon


def wrap(value, count):
    return lax.rem(value + count, count)


SLOT_SENDS = ((2, "lat"), (5, "lon"), (7, "diag"), (6, "lat"), (3, "lat"))
KEPT_SLOTS = (0, 1, 4)

GROUPS = (
    (0, 704, "xzy"),
    (704, 640, "yxz"),
    (1344, 704, "zyx"),
    (2048, 704, "xzy"),
    (2752, 640, "yxz"),
    (3392, 704, "zyx"),
)
WAVES = ((0, 1, 2), (3, 4, 5))


def slot_pieces(slot):
    if slot < 4:
        first = 2 * (slot // 2)
        kind = "xg"[slot % 2]
        return ((kind, first), (kind, first + 1))
    return (("x", slot), ("g", slot))


def coordinates():
    lat, lon = position()
    core = lax.rem(lat, 2)
    y = (lat // 2) * 2 + lon // 16
    x = lax.rem(lon // 4, 4)
    z = lax.rem(lon, 4)
    return {"x": x, "y": y, "z": z, "core": core}


def device_at(co):
    return ((co["y"] // 2) * 2 + co["core"], lax.rem(co["y"], 2) * 16 + co["x"] * 4 + co["z"])


def peer(co, axis, j):
    moved = dict(co)
    moved[axis] = lax.rem(co[axis] + j, 4)
    return device_at(moved)


def sibling(co):
    moved = dict(co)
    moved["core"] = 1 - co["core"]
    return device_at(moved)


def block_kernel(
    x_hbm, g_hbm, keep_hbm, perm_hbm, member_hbm, place_hbm, wqkv_hbm, wproj_hbm, gain_hbm, scale_hbm,
    ret_ref, sum_ref, small_out_ref,
    x_ref, g_ref, keep_ref, perm_ref, member_ref, place_ref, wqkv_ref, wproj_ref, gain_ref, scale_ref, in_buf, win_ref, back_ref,
    x_s, xh_s, rstd_s, y_s, g_s, rq_s, rk_s, rq_rows_s, q_s, k_s, qd_s, kd_s, v_s, do_s, dq_s, dk_s, dv_s, att_s, allow_s, gs_s, small_s,
    grads_ref, r0, a1, r1, a2, a3, sv0, sv1, sv2, sv3,
    w_sem, in_send, in_recv, out_send, out_recv, sib_send, sib_recv, st_send, st_recv, sv_send, sv_recv,
):
    lat, lon = position()
    lat_lo, lat_hi = wrap(lat - 1, 4), wrap(lat + 1, 4)
    lon_lo, lon_hi = wrap(lon - 1, 32), wrap(lon + 1, 32)
    co = coordinates()
    core = co["core"]
    sib = sibling(co)
    peers = {axis: [peer(co, axis, j) for j in (1, 2, 3)] for axis in "xyz"}

    loads = {}
    for i, (name, src, dst) in enumerate((
        ("perm", perm_hbm, perm_ref),
        ("x", x_hbm, x_ref),
        ("keep", keep_hbm, keep_ref),
        ("member", member_hbm, member_ref),
        ("place", place_hbm, place_ref),
        ("g", g_hbm, g_ref),
        ("gain", gain_hbm, gain_ref),
        ("qkv", wqkv_hbm, wqkv_ref),
        ("proj", wproj_hbm, wproj_ref),
        ("scale", scale_hbm, scale_ref),
    )):
        loads[name] = pltpu.make_async_copy(src, dst, w_sem.at[i])
    first_loads = ("x", "perm", "keep", "member", "place", "g")
    for name in first_loads:
        loads[name].start()

    barrier = pltpu.get_barrier_semaphore()
    greet = [(lat_lo, lon), (lat, lon_lo), (lat_lo, lon_lo), (lat_hi, lon), (lat, lon_hi), (lat_hi, lon_hi), sib]
    for axis in "xyz":
        greet.extend(peers[axis])
    for dev in greet:
        pl.semaphore_signal(barrier, inc=1, device_id=dev, device_id_type=MESH)

    started = []

    def send(src, dst, s_sem, r_sem, dev):
        copy = pltpu.make_async_remote_copy(
            src_ref=src, dst_ref=dst, send_sem=s_sem, recv_sem=r_sem, device_id=dev, device_id_type=MESH
        )
        copy.start()
        started.append(copy)
        return copy

    for name in first_loads:
        loads[name].wait()
    for name in ("gain", "qkv", "proj", "scale"):
        loads[name].start()
    perm = perm_ref[...]
    xs = dot(perm, x_ref[...])
    gs = dot(perm, g_ref[...])
    keep_rows = [keep_ref[row, lev : lev + 1, :].astype(F32) for lev in range(2) for row in range(6)]
    marks = (jnp.concatenate(keep_rows, axis=1) * member_ref[...].astype(F32)).astype(BF)
    flags = dot(marks, place_ref[...])
    row_id = lax.broadcasted_iota(jnp.int32, (QT, 512), 0)

    def piece(kind, quarter):
        rows = slice(quarter * QT, (quarter + 1) * QT)
        if kind == "g":
            return gs[rows]
        flag = jnp.concatenate([flags[quarter : quarter + 1], jnp.zeros((1, 256), F32)], axis=1)
        return jnp.where(row_id == FLAG_ROW, flag, xs[rows])

    def payload(slot):
        return jnp.concatenate([piece(*p) for p in slot_pieces(slot)], axis=0).astype(BF)

    for i, (slot, _) in enumerate(SLOT_SENDS):
        in_buf[i] = payload(slot)
    pl.semaphore_wait(barrier, len(greet))
    low = {"lat": (lat_lo, lon), "lon": (lat, lon_lo), "diag": (lat_lo, lon_lo)}
    high = {"lat": (lat_hi, lon), "lon": (lat, lon_hi), "diag": (lat_hi, lon_hi)}
    arrive = {}
    for i, (slot, way) in enumerate(SLOT_SENDS):
        arrive[slot] = send(in_buf.at[i], win_ref.at[slot], in_send.at[i], in_recv.at[i], low[way])
    for slot in KEPT_SLOTS:
        win_ref[slot] = payload(slot)
    loads["gain"].wait()
    loads["qkv"].wait()

    gain = gain_ref[...]
    r = lax.broadcasted_iota(jnp.int32, (256, 256), 0)
    c = lax.broadcasted_iota(jnp.int32, (256, 256), 1)
    ones = jnp.where((r // 64) == (c // 64), 1.0, 0.0).astype(BF)

    r = lax.broadcasted_iota(jnp.int32, (8, 512), 0)
    c = lax.broadcasted_iota(jnp.int32, (8, 512), 1)
    head_of = jnp.where(r == c // 64, 1.0, 0.0).astype(BF)

    def head_sum(values):
        hi = values.astype(BF)
        lo = (values - hi.astype(F32)).astype(BF)
        halves = [dot(hi[:, i : i + 256], ones) + dot(lo[:, i : i + 256], ones) for i in (0, 256)]
        return jnp.concatenate(halves, axis=1)

    real = lax.broadcasted_iota(jnp.int32, (QT, 512), 0) < 36
    key_id = lax.broadcasted_iota(jnp.int32, (WIN, WIN), 0)
    query_id = lax.broadcasted_iota(jnp.int32, (WIN, WIN), 1)
    same_half = (key_id >= 2 * QT) == (query_id >= 2 * QT)
    joined = jnp.logical_or(same_half, lat != 3)
    first_row = lax.broadcasted_iota(jnp.int32, (8, WIN), 0) == 0
    one_row = jnp.where(first_row, 1.0, 0.0).astype(BF)

    def front(w):
        rows = slice(w * WIN, (w + 1) * WIN)
        if w == 0:
            data = jnp.concatenate([win_ref[0].astype(F32), win_ref[2].astype(F32)], axis=0)
        else:
            data = jnp.concatenate([win_ref[slot].astype(F32)[:QT] for slot in (4, 5, 6, 7)], axis=0)
        data = data.reshape(4, QT, 512)
        x = jnp.where(real[None], data, 0.0).reshape(WIN, 512)
        marks = data[0, FLAG_ROW : FLAG_ROW + 1, :]
        for i in range(1, 4):
            marks = marks + data[i, FLAG_ROW : FLAG_ROW + 1, :]
        marks = jnp.where(first_row, marks[:, :WIN], 0.0).astype(BF)
        keep = jnp.where(joined, dot(marks, one_row, 0, 0), 0.0)
        allow_s[w] = jnp.where(key_id == query_id, 1.0, keep)
        mean = jnp.mean(x, axis=-1, keepdims=True)
        xc = x - mean
        var = jnp.mean(xc * xc, axis=-1, keepdims=True)
        rstd = lax.rsqrt(var + EPS_NORM)
        xhat = xc * rstd
        y = (xhat * gain).astype(BF)
        x_s[rows] = x
        xh_s[rows] = xhat
        rstd_s[rows] = jnp.broadcast_to(rstd, (WIN, 128))
        y_s[rows] = y
        q_b = dot(y, wqkv_ref[:, 0:512]).astype(BF)
        k_b = dot(y, wqkv_ref[:, 512:1024]).astype(BF)
        q_s[rows] = q_b
        k_s[rows] = k_b
        q = q_b.astype(F32)
        k = k_b.astype(F32)
        v_s[rows] = dot(y, wqkv_ref[:, 1024:1536]).astype(BF)
        q_sq = q * q
        rq = lax.rsqrt(head_sum(q_sq) + EPS_DIR)
        sq_hi = q_sq.astype(BF)
        sq_lo = (q_sq - sq_hi.astype(F32)).astype(BF)
        rq_rows_s[w] = lax.rsqrt(dot(head_of, sq_hi, 1, 1) + dot(head_of, sq_lo, 1, 1) + EPS_DIR)
        rk = lax.rsqrt(head_sum(k * k) + EPS_DIR)
        rq_s[rows] = rq
        rk_s[rows] = rk
        qd_s[rows] = (q * rq).astype(BF)
        kd_s[rows] = (k * rk).astype(BF)

    arrive[2].wait_recv()
    front(0)
    for slot in (5, 7, 6):
        arrive[slot].wait_recv()
    front(1)
    arrive[3].wait_recv()
    g = jnp.concatenate(
        [win_ref[1].astype(F32), win_ref[3].astype(F32)] + [win_ref[slot].astype(F32)[QT:] for slot in (4, 5, 6, 7)],
        axis=0,
    ).astype(BF)
    g_s[...] = g
    loads["proj"].wait()
    loads["scale"].wait()
    do_s[...] = dot(g, wproj_ref[...], 1, 1).astype(BF)
    y_t = jnp.transpose(y_s[...])

    flight = {}

    def send_stage(group, stage, axis, pairs):
        copies = []
        for j in range(3):
            src, dst = pairs(j)
            index = (group, stage, j)
            copies.append(send(src, dst, st_send.at[index], st_recv.at[index], peers[axis][j]))
        flight[group] = copies

    def arrived(group):
        for copy in flight[group]:
            copy.wait_recv()

    def own_rows(group, j=0):
        first, rows, axes = GROUPS[group]
        size = rows // 4
        turn = lax.rem(co[axes[0]] + j, 4)
        return pl.ds(pl.multiple_of(first + turn * size, 16), size)

    def landing(group):
        return pl.ds(GROUPS[group][0] // 4, GROUPS[group][1] // 4)

    def exchange(group, stage, buf, total):
        axis = GROUPS[group][2][stage]
        me = co[axis]
        buf[me, landing(group)] = total.astype(BF)
        here = buf.at[me, landing(group)]
        send_stage(group, stage, axis, lambda j: (here, here))

    def exchanged(group, buf):
        arrived(group)
        total = buf[0, landing(group)].astype(F32)
        for i in range(1, 4):
            total = total + buf[i, landing(group)].astype(F32)
        return total

    sib_in = {}

    def begin(part):
        rows = pl.ds(part * 1024, 1024)
        sib_in[part] = send(grads_ref.at[1 - core, rows], r0.at[rows], sib_send.at[part], sib_recv.at[part], sib)

    def join(part):
        sib_in[part].wait_recv()
        rows = pl.ds(part * 1024, 1024)
        a1[rows] = (grads_ref[core, rows].astype(F32) + r0[rows].astype(F32)).astype(BF)

    def advance(group, stage):
        if stage == 0:
            send_stage(
                group, 0, GROUPS[group][2][0], lambda j: (a1.at[own_rows(group, j + 1)], r1.at[j, landing(group)])
            )
        elif stage == 1:
            arrived(group)
            total = a1[own_rows(group)].astype(F32)
            for j in range(3):
                total = total + r1[j, landing(group)].astype(F32)
            exchange(group, 1, a2, total)
        elif stage == 2:
            exchange(group, 2, a3, exchanged(group, a2))
        elif stage == 3:
            sum_ref[core, own_rows(group)] = exchanged(group, a3).astype(BF)
            where = sum_ref.at[core, own_rows(group)]
            send_stage(group, 3, GROUPS[group][2][0], lambda j: (where, where))
        elif stage == 4:
            arrived(group)
            whole = sum_ref.at[core, pl.ds(GROUPS[group][0], GROUPS[group][1])]
            flight[group] = [send(whole, whole, sib_send.at[4 + group], sib_recv.at[4 + group], sib)]
        else:
            arrived(group)

    def advance_wave(wave, stage):
        for group in WAVES[wave]:
            advance(group, stage)

    lane = lax.broadcasted_iota(jnp.int32, (1, 128), 1)
    small_ones = ones[:128, :128]

    def pair_of_heads(pair):
        cols = slice(pair * 128, (pair + 1) * 128)
        scales = [scale_ref[pair * 2 + i] for i in range(2)]
        s_lane = jnp.where(lane < 64, scales[0], scales[1])

        def window(w):
            rows = slice(w * WIN, (w + 1) * WIN)
            q_p = q_s[rows, cols]
            k_p = k_s[rows, cols]
            qd_p = qd_s[rows, cols]
            kd_p = kd_s[rows, cols]
            v_p = v_s[rows, cols]
            do_p = do_s[rows, cols]
            allow = allow_s[w]
            acc_o = jnp.zeros((WIN, 128), F32)
            acc_q = jnp.zeros((WIN, 128), F32)
            acc_k = jnp.zeros((WIN, 128), F32)
            acc_v = jnp.zeros((WIN, 128), F32)
            zero = jnp.zeros((WIN, 128), BF)
            for i in range(2):
                s = scales[i]
                mine = jnp.broadcast_to((lane < 64) if i == 0 else (lane >= 64), (WIN, 128))
                qd_h = jnp.where(mine, qd_p, zero)
                kd_h = jnp.where(mine, kd_p, zero)
                v_h = jnp.where(mine, v_p, zero)
                do_h = jnp.where(mine, do_p, zero)
                rq_row = rq_rows_s[w, pair * 2 + i : pair * 2 + i + 1, :]
                rk_col = rk_s[rows, pair * 128 + i * 64 : pair * 128 + i * 64 + 1]
                cos = dot(k_p, jnp.where(mine, q_p, zero), 1, 1) * rk_col * rq_row
                e = jnp.exp(s * cos - s) * allow
                p = e * (1.0 / jnp.sum(e, axis=0, keepdims=True))
                dp = dot(v_p, do_h, 1, 1)
                dl = p * (dp - jnp.sum(p * dp, axis=0, keepdims=True))
                gs_s[w * 4 + pair, i : i + 1, :] = jnp.sum(dl * cos, axis=0, keepdims=True)
                p_b = p.astype(BF)
                dl_b = dl.astype(BF)
                acc_o = acc_o + dot(p_b, v_h, 0, 0)
                acc_v = acc_v + dot(p_b, do_h)
                acc_k = acc_k + dot(dl_b, qd_h)
                acc_q = acc_q + dot(dl_b, kd_h, 0, 0)
            att_s[rows, cols] = acc_o.astype(BF)
            dv_s[rows, cols] = acc_v.astype(BF)
            qd = qd_p.astype(F32)
            kd = kd_p.astype(F32)
            dqd = acc_q * s_lane
            dkd = acc_k * s_lane
            dq_s[rows, cols] = (rq_s[rows, cols] * (dqd - qd * dot((qd * dqd).astype(BF), small_ones))).astype(BF)
            dk_s[rows, cols] = (rk_s[rows, cols] * (dkd - kd * dot((kd * dkd).astype(BF), small_ones))).astype(BF)

        window(0)
        window(1)
        d_all = jnp.concatenate([dq_s[:, cols], dk_s[:, cols], dv_s[:, cols]], axis=1)
        gq = dot(y_t, d_all).astype(BF)
        gp = dot(att_s[:, cols], g_s[...], 0, 0).astype(BF)
        for half in range(2):
            for i in range(3):
                first = pair * 1024 + i * 256
                grads_ref[half, first : first + 256] = gq[half * 256 : (half + 1) * 256, i * 128 : (i + 1) * 128]
            for ct in range(4):
                first = pair * 1024 + 768 + ct * 64
                grads_ref[half, first : first + 64] = gp[half * 64 : (half + 1) * 64, ct * 128 : (ct + 1) * 128]
        begin(pair)

    for pair in range(4):
        pair_of_heads(pair)
        if pair == 2:
            join(0)
            join(1)
            advance_wave(0, 0)

    def out_slot(slot, pieces):
        back_ref[slot] = jnp.concatenate(pieces, axis=0).astype(BF)

    back = {}

    def send_back(slots):
        for i, (slot, way) in enumerate(SLOT_SENDS):
            if slot in slots:
                back[slot] = send(back_ref.at[slot], ret_ref.at[slot], out_send.at[i], out_recv.at[i], high[way])

    mixed = x_s[...] + dot(att_s[...], wproj_ref[...])
    for slot in (0, 2):
        out_slot(slot, [mixed[slot * QT : (slot + 2) * QT]])
    send_back((2,))
    dn = dot(dq_s[...], wqkv_ref[:, 0:512], 1, 1)
    dn = dn + dot(dk_s[...], wqkv_ref[:, 512:1024], 1, 1)
    dn = dn + dot(dv_s[...], wqkv_ref[:, 1024:1536], 1, 1)
    xhat = xh_s[...]
    d_gain = jnp.sum(dn * xhat, axis=0, keepdims=True)
    small_s[...] = jnp.zeros((16, 128), F32)
    for i in range(4):
        small_s[i : i + 1, :] = d_gain[:, i * 128 : (i + 1) * 128]
    for h in range(8):
        row = gs_s[h // 2, h % 2 : h % 2 + 1, :] + gs_s[4 + h // 2, h % 2 : h % 2 + 1, :]
        small_s[8 + h : 9 + h, :] = jnp.broadcast_to(jnp.sum(row, axis=1, keepdims=True), (1, 128))

    def small_stage(stage, values):
        axis = ("core", "x", "y", "z")[stage]
        buf = (sv0, sv1, sv2, sv3)[stage]
        me = co[axis]
        buf[me] = values
        copies = []
        for j, dev in enumerate([sib] if stage == 0 else peers[axis]):
            index = 0 if stage == 0 else 1 + 3 * (stage - 1) + j
            copies.append(send(buf.at[me], buf.at[me], sv_send.at[index], sv_recv.at[index], dev))
        return copies

    def small_sum(stage, copies):
        buf = (sv0, sv1, sv2, sv3)[stage]
        for copy in copies:
            copy.wait_recv()
        total = buf[0]
        for i in range(1, 2 if stage == 0 else 4):
            total = total + buf[i]
        return total

    small_copies = small_stage(0, small_s[...])
    dxh = dn * gain
    rstd = rstd_s[:, 0:1]
    dx = rstd * (dxh - jnp.mean(dxh, axis=-1, keepdims=True) - xhat * jnp.mean(dxh * xhat, axis=-1, keepdims=True))
    gtok = g_s[...].astype(F32) + dx
    for slot in (1, 3):
        out_slot(slot, [gtok[(slot - 1) * QT : (slot + 1) * QT]])
    for slot in (4, 5, 6, 7):
        rows = slice(slot * QT, (slot + 1) * QT)
        out_slot(slot, [mixed[rows], gtok[rows]])
    for slot in KEPT_SLOTS:
        ret_ref[slot] = back_ref[slot]
    join(2)
    join(3)
    advance_wave(1, 0)
    send_back((5, 7, 6, 3))
    for stage in range(1, 6):
        departed = len(started)
        advance_wave(0, stage)
        advance_wave(1, stage)
        if stage < 4:
            small_copies = small_stage(stage, small_sum(stage - 1, small_copies))
        elif stage == 4:
            small_out_ref[...] = small_sum(3, small_copies)
            for slot in back:
                back[slot].wait_recv()
        if stage < 5:
            for copy in started[:departed]:
                copy.wait_send()
            del started[:departed]
    for copy in started:
        copy.wait_send()


def finish_kernel(ret_ref, sum_ref, small_ref, perm_ref, mixed_ref, gtok_ref, gqkv_ref, gproj_ref, gain_ref, gscale_ref):
    ret = ret_ref[...].astype(F32)
    perm = perm_ref[...]
    mixed = jnp.concatenate([ret[0], ret[2]] + [ret[slot][:QT] for slot in (4, 5, 6, 7)], axis=0).astype(BF)
    gtok = jnp.concatenate([ret[1], ret[3]] + [ret[slot][QT:] for slot in (4, 5, 6, 7)], axis=0).astype(BF)
    mixed_ref[...] = dot(perm, mixed, 0, 0).astype(BF)
    gtok_ref[...] = dot(perm, gtok, 0, 0).astype(BF)
    for half in range(2):
        for p in range(4):
            for i in range(3):
                cols = slice(i * 512 + p * 128, i * 512 + (p + 1) * 128)
                first = p * 1024 + i * 256
                tile = sum_ref[half, first : first + 256]
                gqkv_ref[half * 256 : (half + 1) * 256, cols] = tile.astype(F32)
            for ct in range(4):
                first = p * 1024 + 768 + ct * 64
                tile = sum_ref[half, first : first + 64]
                rows = slice(p * 128 + half * 64, p * 128 + (half + 1) * 64)
                gproj_ref[rows, ct * 128 : (ct + 1) * 128] = tile.astype(F32)
    for i in range(4):
        gain_ref[:, i * 128 : (i + 1) * 128] = small_ref[i : i + 1, :]
    eye = lax.broadcasted_iota(jnp.int32, (8, 128), 0) == lax.broadcasted_iota(jnp.int32, (8, 128), 1)
    row = jnp.sum(jnp.where(eye, small_ref[8:16, :], 0.0), axis=0, keepdims=True)
    gscale_ref[...] = row[:, :8]


VM = pl.BlockSpec(memory_space=pltpu.VMEM)
HBM = pl.BlockSpec(memory_space=pltpu.HBM)
DMA = pltpu.SemaphoreType.DMA
MIB = 1024 * 1024


def per_device(tokens, cotangent, key_keep, norm_gain, w_qkv, w_proj, attn_scale):
    perm, member, place = tables()
    perm = jnp.asarray(perm, BF)
    x = tokens.reshape(288, 512)
    g = cotangent.reshape(288, 512)
    tok = (2 * WIN, 512)
    operands = (
        x, g, key_keep.transpose(1, 0, 2), perm, jnp.asarray(member, BF), jnp.asarray(place, BF),
        w_qkv, w_proj, norm_gain.reshape(1, 512), attn_scale,
    )
    operands = [pltpu.with_memory_space_constraint(operand, pltpu.HBM) for operand in operands]
    ret, total, small = pl.pallas_call(
        block_kernel,
        out_shape=(
            jax.ShapeDtypeStruct((8, ROWS, 512), BF),
            jax.ShapeDtypeStruct((2, 4096, 128), BF),
            jax.ShapeDtypeStruct((16, 128), F32),
        ),
        in_specs=[HBM] * 10,
        out_specs=(VM,) * 3,
        scratch_shapes=[
            pltpu.VMEM((288, 512), BF),
            pltpu.VMEM((288, 512), BF),
            pltpu.VMEM((6, 2, 24), jnp.int32),
            pltpu.VMEM((8 * QT, 288), BF),
            pltpu.VMEM((8, 288), BF),
            pltpu.VMEM((288, 256), BF),
            pltpu.VMEM((512, 1536), BF),
            pltpu.VMEM((512, 512), BF),
            pltpu.VMEM((1, 512), F32),
            pltpu.SMEM((8,), F32),
            pltpu.VMEM((5, ROWS, 512), BF),
            pltpu.VMEM((8, ROWS, 512), BF),
            pltpu.VMEM((8, ROWS, 512), BF),
            pltpu.VMEM(tok, F32),
            pltpu.VMEM(tok, F32),
            pltpu.VMEM((2 * WIN, 128), F32),
            pltpu.VMEM(tok, BF),
            pltpu.VMEM(tok, BF),
            pltpu.VMEM(tok, F32),
            pltpu.VMEM(tok, F32),
        ]
        + [pltpu.VMEM((2, 8, WIN), F32)]
        + [pltpu.VMEM(tok, BF)] * 10
        + [
            pltpu.VMEM((2, WIN, WIN), F32),
            pltpu.VMEM((8, 2, WIN), F32),
            pltpu.VMEM((16, 128), F32),
            pltpu.VMEM((2, 4096, 128), BF),
            pltpu.VMEM((4096, 128), BF),
            pltpu.VMEM((4096, 128), BF),
            pltpu.VMEM((3, 1024, 128), BF),
            pltpu.VMEM((4, 1024, 128), BF),
            pltpu.VMEM((4, 1024, 128), BF),
            pltpu.VMEM((2, 16, 128), F32),
            pltpu.VMEM((4, 16, 128), F32),
            pltpu.VMEM((4, 16, 128), F32),
            pltpu.VMEM((4, 16, 128), F32),
            DMA((10,)),
            DMA((5,)), DMA((5,)),
            DMA((5,)), DMA((5,)),
            DMA((10,)), DMA((10,)),
            DMA((6, 4, 3)), DMA((6, 4, 3)),
            DMA((10,)), DMA((10,)),
        ],
        compiler_params=pltpu.CompilerParams(collective_id=1, has_side_effects=True, vmem_limit_bytes=40 * MIB),
        name="block",
    )(*operands)

    mixed, gtok, gqkv, gproj, gain, gscale = pl.pallas_call(
        finish_kernel,
        out_shape=(
            jax.ShapeDtypeStruct((288, 512), BF),
            jax.ShapeDtypeStruct((288, 512), BF),
            jax.ShapeDtypeStruct((512, 1536), F32),
            jax.ShapeDtypeStruct((512, 512), F32),
            jax.ShapeDtypeStruct((1, 512), F32),
            jax.ShapeDtypeStruct((1, 8), F32),
        ),
        in_specs=[VM] * 4,
        out_specs=(VM,) * 6,
        compiler_params=pltpu.CompilerParams(vmem_limit_bytes=24 * MIB),
        name="finish",
    )(ret, total, small, perm)
    return (
        mixed.reshape(tokens.shape),
        gtok.reshape(tokens.shape),
        gqkv,
        gproj,
        gain.reshape(512),
        gscale.reshape(8),
    )


def solution(mesh):
    grid = P(None, "lat", "lon", None)
    return jax.shard_map(
        per_device,
        mesh=mesh,
        in_specs=(grid, grid, P(None, "lat", "lon"), P(), P(), P(), P()),
        out_specs=(grid, grid, P(), P(), P(), P()),
        check_vma=False,
    )
```

```python
import functools

import jax
import jax.numpy as jnp
import numpy as np
from jax import lax
from jax.experimental import pallas as pl
from jax.experimental.pallas import tpu as pltpu
from jax.sharding import PartitionSpec as P

EPS_NORM = 1e-05
EPS_DIR = 1e-06
MESH = pl.DeviceIdType.MESH
BF = jnp.bfloat16
F32 = jnp.float32

QUARTERS = ((1, 1), (1, 2), (0, 1), (0, 2), (1, 3), (1, 0), (0, 3), (0, 0))
QT = 40
ROWS = 80
WIN = 160
FLAG_ROW = 36


def token_of(quarter, t):
    half, cq = QUARTERS[quarter]
    lev, rest = divmod(t, 18)
    rr, cc = divmod(rest, 6)
    return lev * 144 + (half * 3 + rr) * 24 + cq * 6 + cc


def tables():
    perm = np.zeros((8 * QT, 288), np.float32)
    member = np.zeros((8, 288), np.float32)
    place = np.zeros((288, 256), np.float32)
    for quarter in range(8):
        for t in range(36):
            src = token_of(quarter, t)
            perm[quarter * QT + t, src] = 1.0
            member[quarter, src] = 1.0
            place[src, QT * (quarter % 4) + t] = 1.0
    return perm, member, place


def dot(a, b, ca=1, cb=0):
    return lax.dot_general(a, b, (((ca,), (cb,)), ((), ())), preferred_element_type=F32)


def position():
    lat = lax.axis_index("lat")
    lon = lax.axis_index("lon")
    return lat, lon


def wrap(value, count):
    return lax.rem(value + count, count)


SLOT_SENDS = ((2, "lat"), (5, "lon"), (7, "diag"), (6, "lat"), (3, "lat"))
KEPT_SLOTS = (0, 1, 4)

GROUPS = (
    (0, 768, "xzy"),
    (768, 512, "yxz"),
    (1280, 768, "zyx"),
    (2048, 768, "xzy"),
    (2816, 512, "yxz"),
    (3328, 768, "zyx"),
)
WAVES = ((0, 1, 2), (3, 4, 5))


def slot_pieces(slot):
    if slot < 4:
        first = 2 * (slot // 2)
        kind = "xg"[slot % 2]
        return ((kind, first), (kind, first + 1))
    return (("x", slot), ("g", slot))


def coordinates():
    lat, lon = position()
    core = lax.rem(lat, 2)
    y = (lat // 2) * 2 + lon // 16
    x = lax.rem(lon // 4, 4)
    z = lax.rem(lon, 4)
    return {"x": x, "y": y, "z": z, "core": core}


def device_at(co):
    return ((co["y"] // 2) * 2 + co["core"], lax.rem(co["y"], 2) * 16 + co["x"] * 4 + co["z"])


def peer(co, axis, j):
    moved = dict(co)
    moved[axis] = lax.rem(co[axis] + j, 4)
    return device_at(moved)


def sibling(co):
    moved = dict(co)
    moved["core"] = 1 - co["core"]
    return device_at(moved)


def block_kernel(
    x_hbm, g_hbm, keep_hbm, perm_hbm, member_hbm, place_hbm, wqkv_hbm, wproj_hbm, gain_hbm, scale_hbm,
    ret_ref, sum_ref, small_out_ref,
    x_ref, g_ref, keep_ref, perm_ref, member_ref, place_ref, wqkv_ref, wproj_ref, gain_ref, scale_ref, in_buf, win_ref, back_ref,
    x_s, xh_s, rstd_s, y_s, g_s, rq_s, rk_s, rq_rows_s, q_s, k_s, qd_s, kd_s, v_s, do_s, dq_s, dk_s, dv_s, att_s, allow_s, gs_s, small_s,
    grads_ref, r0, a1, r1, a2, r2, a3, sv0, sv1, sv2, sv3,
    w_sem, in_send, in_recv, out_send, out_recv, sib_send, sib_recv, st_send, st_recv, sv_send, sv_recv,
):
    lat, lon = position()
    lat_lo, lat_hi = wrap(lat - 1, 4), wrap(lat + 1, 4)
    lon_lo, lon_hi = wrap(lon - 1, 32), wrap(lon + 1, 32)
    co = coordinates()
    core = co["core"]
    sib = sibling(co)
    peers = {axis: [peer(co, axis, j) for j in (1, 2, 3)] for axis in "xyz"}

    loads = {}
    for i, (name, src, dst) in enumerate((
        ("perm", perm_hbm, perm_ref),
        ("x", x_hbm, x_ref),
        ("keep", keep_hbm, keep_ref),
        ("member", member_hbm, member_ref),
        ("place", place_hbm, place_ref),
        ("g", g_hbm, g_ref),
        ("gain", gain_hbm, gain_ref),
        ("qkv", wqkv_hbm, wqkv_ref),
        ("proj", wproj_hbm, wproj_ref),
        ("scale", scale_hbm, scale_ref),
    )):
        loads[name] = pltpu.make_async_copy(src, dst, w_sem.at[i])
    first_loads = ("x", "perm", "keep", "member", "place", "g")
    for name in first_loads:
        loads[name].start()

    barrier = pltpu.get_barrier_semaphore()
    greet = [(lat_lo, lon), (lat, lon_lo), (lat_lo, lon_lo), (lat_hi, lon), (lat, lon_hi), (lat_hi, lon_hi), sib]
    for axis in "xyz":
        greet.extend(peers[axis])
    for dev in greet:
        pl.semaphore_signal(barrier, inc=1, device_id=dev, device_id_type=MESH)

    started = []

    def send(src, dst, s_sem, r_sem, dev):
        copy = pltpu.make_async_remote_copy(
            src_ref=src, dst_ref=dst, send_sem=s_sem, recv_sem=r_sem, device_id=dev, device_id_type=MESH
        )
        copy.start()
        started.append(copy)
        return copy

    for name in first_loads:
        loads[name].wait()
    for name in ("gain", "qkv", "proj", "scale"):
        loads[name].start()
    perm = perm_ref[...]
    xs = dot(perm, x_ref[...])
    gs = dot(perm, g_ref[...])
    keep_rows = [keep_ref[row, lev : lev + 1, :].astype(F32) for lev in range(2) for row in range(6)]
    marks = (jnp.concatenate(keep_rows, axis=1) * member_ref[...].astype(F32)).astype(BF)
    flags = dot(marks, place_ref[...])
    row_id = lax.broadcasted_iota(jnp.int32, (QT, 512), 0)

    def piece(kind, quarter):
        rows = slice(quarter * QT, (quarter + 1) * QT)
        if kind == "g":
            return gs[rows]
        flag = jnp.concatenate([flags[quarter : quarter + 1], jnp.zeros((1, 256), F32)], axis=1)
        return jnp.where(row_id == FLAG_ROW, flag, xs[rows])

    def payload(slot):
        return jnp.concatenate([piece(*p) for p in slot_pieces(slot)], axis=0).astype(BF)

    for i, (slot, _) in enumerate(SLOT_SENDS):
        in_buf[i] = payload(slot)
    pl.semaphore_wait(barrier, len(greet))
    low = {"lat": (lat_lo, lon), "lon": (lat, lon_lo), "diag": (lat_lo, lon_lo)}
    high = {"lat": (lat_hi, lon), "lon": (lat, lon_hi), "diag": (lat_hi, lon_hi)}
    arrive = {}
    for i, (slot, way) in enumerate(SLOT_SENDS):
        arrive[slot] = send(in_buf.at[i], win_ref.at[slot], in_send.at[i], in_recv.at[i], low[way])
    for slot in KEPT_SLOTS:
        win_ref[slot] = payload(slot)
    loads["gain"].wait()
    loads["qkv"].wait()

    gain = gain_ref[...]
    r = lax.broadcasted_iota(jnp.int32, (256, 256), 0)
    c = lax.broadcasted_iota(jnp.int32, (256, 256), 1)
    ones = jnp.where((r // 64) == (c // 64), 1.0, 0.0).astype(BF)

    r = lax.broadcasted_iota(jnp.int32, (8, 512), 0)
    c = lax.broadcasted_iota(jnp.int32, (8, 512), 1)
    head_of = jnp.where(r == c // 64, 1.0, 0.0).astype(BF)

    def head_sum(values):
        hi = values.astype(BF)
        lo = (values - hi.astype(F32)).astype(BF)
        halves = [dot(hi[:, i : i + 256], ones) + dot(lo[:, i : i + 256], ones) for i in (0, 256)]
        return jnp.concatenate(halves, axis=1)

    real = lax.broadcasted_iota(jnp.int32, (QT, 512), 0) < 36
    key_id = lax.broadcasted_iota(jnp.int32, (WIN, WIN), 0)
    query_id = lax.broadcasted_iota(jnp.int32, (WIN, WIN), 1)
    same_half = (key_id >= 2 * QT) == (query_id >= 2 * QT)
    joined = jnp.logical_or(same_half, lat != 3)
    first_row = lax.broadcasted_iota(jnp.int32, (8, WIN), 0) == 0
    one_row = jnp.where(first_row, 1.0, 0.0).astype(BF)

    def front(w):
        rows = slice(w * WIN, (w + 1) * WIN)
        if w == 0:
            data = jnp.concatenate([win_ref[0].astype(F32), win_ref[2].astype(F32)], axis=0)
        else:
            data = jnp.concatenate([win_ref[slot].astype(F32)[:QT] for slot in (4, 5, 6, 7)], axis=0)
        data = data.reshape(4, QT, 512)
        x = jnp.where(real[None], data, 0.0).reshape(WIN, 512)
        marks = data[0, FLAG_ROW : FLAG_ROW + 1, :]
        for i in range(1, 4):
            marks = marks + data[i, FLAG_ROW : FLAG_ROW + 1, :]
        marks = jnp.where(first_row, marks[:, :WIN], 0.0).astype(BF)
        keep = jnp.where(joined, dot(marks, one_row, 0, 0), 0.0)
        allow_s[w] = jnp.where(key_id == query_id, 1.0, keep)
        mean = jnp.mean(x, axis=-1, keepdims=True)
        xc = x - mean
        var = jnp.mean(xc * xc, axis=-1, keepdims=True)
        rstd = lax.rsqrt(var + EPS_NORM)
        xhat = xc * rstd
        y = (xhat * gain).astype(BF)
        x_s[rows] = x
        xh_s[rows] = xhat
        rstd_s[rows] = jnp.broadcast_to(rstd, (WIN, 128))
        y_s[rows] = y
        q_b = dot(y, wqkv_ref[:, 0:512]).astype(BF)
        k_b = dot(y, wqkv_ref[:, 512:1024]).astype(BF)
        q_s[rows] = q_b
        k_s[rows] = k_b
        q = q_b.astype(F32)
        k = k_b.astype(F32)
        v_s[rows] = dot(y, wqkv_ref[:, 1024:1536]).astype(BF)
        q_sq = q * q
        rq = lax.rsqrt(head_sum(q_sq) + EPS_DIR)
        sq_hi = q_sq.astype(BF)
        sq_lo = (q_sq - sq_hi.astype(F32)).astype(BF)
        rq_rows_s[w] = lax.rsqrt(dot(head_of, sq_hi, 1, 1) + dot(head_of, sq_lo, 1, 1) + EPS_DIR)
        rk = lax.rsqrt(head_sum(k * k) + EPS_DIR)
        rq_s[rows] = rq
        rk_s[rows] = rk
        qd_s[rows] = (q * rq).astype(BF)
        kd_s[rows] = (k * rk).astype(BF)

    arrive[2].wait_recv()
    front(0)
    for slot in (5, 7, 6):
        arrive[slot].wait_recv()
    front(1)
    arrive[3].wait_recv()
    g = jnp.concatenate(
        [win_ref[1].astype(F32), win_ref[3].astype(F32)] + [win_ref[slot].astype(F32)[QT:] for slot in (4, 5, 6, 7)],
        axis=0,
    ).astype(BF)
    g_s[...] = g
    loads["proj"].wait()
    loads["scale"].wait()
    do_s[...] = dot(g, wproj_ref[...], 1, 1).astype(BF)
    y_t = jnp.transpose(y_s[...])

    flight = {}

    def send_stage(group, stage, axis, pairs):
        copies = []
        for j in range(3):
            src, dst = pairs(j)
            index = (group, stage, j)
            copies.append(send(src, dst, st_send.at[index], st_recv.at[index], peers[axis][j]))
        flight[group] = copies

    def arrived(group):
        for copy in flight[group]:
            copy.wait_recv()

    def size_of(group, level):
        return GROUPS[group][1] // (4, 16)[level]

    def start_of(group, level):
        return GROUPS[group][0] // (1, 4)[level]

    def own_rows(group, level, j=0):
        first, size = start_of(group, level), size_of(group, level)
        turn = lax.rem(co[GROUPS[group][2][level]] + j, 4)
        return pl.ds(pl.multiple_of(first + turn * size, 16), size)

    def landing(group, level):
        return pl.ds(GROUPS[group][0] // (4, 16)[level], size_of(group, level))

    def scatter(group, level, src, dst):
        def pairs(j):
            return src.at[own_rows(group, level, j + 1)], dst.at[j, landing(group, level)]

        send_stage(group, level, GROUPS[group][2][level], pairs)

    def gathered(group, level, src, dst):
        arrived(group)
        total = src[own_rows(group, level)].astype(F32)
        for j in range(3):
            total = total + dst[j, landing(group, level)].astype(F32)
        return total.astype(BF)

    def final_rows(group, level):
        first, rows, axes = GROUPS[group]
        off = first + co[axes[0]] * (rows // 4)
        if level == 1:
            off = off + co[axes[1]] * (rows // 16)
        return pl.ds(pl.multiple_of(off, 16), size_of(group, level))

    def spread(group, level):
        where = sum_ref.at[core, final_rows(group, level)]
        send_stage(group, 4 - level, GROUPS[group][2][level], lambda j: (where, where))

    sib_in = {}

    def begin(part):
        rows = pl.ds(part * 1024, 1024)
        sib_in[part] = send(grads_ref.at[1 - core, rows], r0.at[rows], sib_send.at[part], sib_recv.at[part], sib)

    def join(part):
        sib_in[part].wait_recv()
        rows = pl.ds(part * 1024, 1024)
        a1[rows] = (grads_ref[core, rows].astype(F32) + r0[rows].astype(F32)).astype(BF)

    def advance(group, stage):
        if stage == 0:
            scatter(group, 0, a1, r1)
        elif stage == 1:
            a2[landing(group, 0)] = gathered(group, 0, a1, r1)
            scatter(group, 1, a2, r2)
        elif stage == 2:
            me = co[GROUPS[group][2][2]]
            a3[me, landing(group, 1)] = gathered(group, 1, a2, r2)
            here = a3.at[me, landing(group, 1)]
            send_stage(group, 2, GROUPS[group][2][2], lambda j: (here, here))
        elif stage == 3:
            arrived(group)
            total = a3[0, landing(group, 1)].astype(F32)
            for i in range(1, 4):
                total = total + a3[i, landing(group, 1)].astype(F32)
            sum_ref[core, final_rows(group, 1)] = total.astype(BF)
            spread(group, 1)
        elif stage == 4:
            arrived(group)
            spread(group, 0)
        elif stage == 5:
            arrived(group)
            whole = sum_ref.at[core, pl.ds(GROUPS[group][0], GROUPS[group][1])]
            flight[group] = [send(whole, whole, sib_send.at[4 + group], sib_recv.at[4 + group], sib)]
        else:
            arrived(group)

    def advance_wave(wave, stage):
        for group in WAVES[wave]:
            advance(group, stage)

    lane = lax.broadcasted_iota(jnp.int32, (1, 128), 1)
    small_ones = ones[:128, :128]

    def pair_of_heads(pair):
        cols = slice(pair * 128, (pair + 1) * 128)
        scales = [scale_ref[pair * 2 + i] for i in range(2)]
        s_lane = jnp.where(lane < 64, scales[0], scales[1])

        def window(w):
            rows = slice(w * WIN, (w + 1) * WIN)
            q_p = q_s[rows, cols]
            k_p = k_s[rows, cols]
            qd_p = qd_s[rows, cols]
            kd_p = kd_s[rows, cols]
            v_p = v_s[rows, cols]
            do_p = do_s[rows, cols]
            allow = allow_s[w]
            acc_o = jnp.zeros((WIN, 128), F32)
            acc_q = jnp.zeros((WIN, 128), F32)
            acc_k = jnp.zeros((WIN, 128), F32)
            acc_v = jnp.zeros((WIN, 128), F32)
            zero = jnp.zeros((WIN, 128), BF)
            for i in range(2):
                s = scales[i]
                mine = jnp.broadcast_to((lane < 64) if i == 0 else (lane >= 64), (WIN, 128))
                qd_h = jnp.where(mine, qd_p, zero)
                kd_h = jnp.where(mine, kd_p, zero)
                v_h = jnp.where(mine, v_p, zero)
                do_h = jnp.where(mine, do_p, zero)
                rq_row = rq_rows_s[w, pair * 2 + i : pair * 2 + i + 1, :]
                rk_col = rk_s[rows, pair * 128 + i * 64 : pair * 128 + i * 64 + 1]
                cos = dot(k_p, jnp.where(mine, q_p, zero), 1, 1) * rk_col * rq_row
                e = jnp.exp(s * cos - s) * allow
                p = e * (1.0 / jnp.sum(e, axis=0, keepdims=True))
                dp = dot(v_p, do_h, 1, 1)
                dl = p * (dp - jnp.sum(p * dp, axis=0, keepdims=True))
                gs_s[w * 4 + pair, i : i + 1, :] = jnp.sum(dl * cos, axis=0, keepdims=True)
                p_b = p.astype(BF)
                dl_b = dl.astype(BF)
                acc_o = acc_o + dot(p_b, v_h, 0, 0)
                acc_v = acc_v + dot(p_b, do_h)
                acc_k = acc_k + dot(dl_b, qd_h)
                acc_q = acc_q + dot(dl_b, kd_h, 0, 0)
            att_s[rows, cols] = acc_o.astype(BF)
            dv_s[rows, cols] = acc_v.astype(BF)
            qd = qd_p.astype(F32)
            kd = kd_p.astype(F32)
            dqd = acc_q * s_lane
            dkd = acc_k * s_lane
            dq_s[rows, cols] = (rq_s[rows, cols] * (dqd - qd * dot((qd * dqd).astype(BF), small_ones))).astype(BF)
            dk_s[rows, cols] = (rk_s[rows, cols] * (dkd - kd * dot((kd * dkd).astype(BF), small_ones))).astype(BF)

        window(0)
        window(1)
        d_all = jnp.concatenate([dq_s[:, cols], dk_s[:, cols], dv_s[:, cols]], axis=1)
        gq = dot(y_t, d_all).astype(BF)
        gp = dot(att_s[:, cols], g_s[...], 0, 0).astype(BF)
        for half in range(2):
            for i in range(3):
                first = pair * 1024 + i * 256
                grads_ref[half, first : first + 256] = gq[half * 256 : (half + 1) * 256, i * 128 : (i + 1) * 128]
            for ct in range(4):
                first = pair * 1024 + 768 + ct * 64
                grads_ref[half, first : first + 64] = gp[half * 64 : (half + 1) * 64, ct * 128 : (ct + 1) * 128]
        begin(pair)

    for pair in range(4):
        pair_of_heads(pair)
        if pair == 2:
            join(0)
            join(1)
            advance_wave(0, 0)
        elif pair == 3:
            join(2)

    def out_slot(slot, pieces):
        back_ref[slot] = jnp.concatenate(pieces, axis=0).astype(BF)

    back = {}

    def send_back(slots):
        for i, (slot, way) in enumerate(SLOT_SENDS):
            if slot in slots:
                back[slot] = send(back_ref.at[slot], ret_ref.at[slot], out_send.at[i], out_recv.at[i], high[way])

    mixed = x_s[...] + dot(att_s[...], wproj_ref[...])
    for slot in (0, 2):
        out_slot(slot, [mixed[slot * QT : (slot + 2) * QT]])
    send_back((2,))
    dn = dot(dq_s[...], wqkv_ref[:, 0:512], 1, 1)
    dn = dn + dot(dk_s[...], wqkv_ref[:, 512:1024], 1, 1)
    dn = dn + dot(dv_s[...], wqkv_ref[:, 1024:1536], 1, 1)
    xhat = xh_s[...]
    d_gain = jnp.sum(dn * xhat, axis=0, keepdims=True)
    small_s[...] = jnp.zeros((16, 128), F32)
    for i in range(4):
        small_s[i : i + 1, :] = d_gain[:, i * 128 : (i + 1) * 128]
    for h in range(8):
        row = gs_s[h // 2, h % 2 : h % 2 + 1, :] + gs_s[4 + h // 2, h % 2 : h % 2 + 1, :]
        small_s[8 + h : 9 + h, :] = jnp.broadcast_to(jnp.sum(row, axis=1, keepdims=True), (1, 128))

    def small_stage(stage, values):
        axis = ("core", "x", "y", "z")[stage]
        buf = (sv0, sv1, sv2, sv3)[stage]
        me = co[axis]
        buf[me] = values
        copies = []
        for j, dev in enumerate([sib] if stage == 0 else peers[axis]):
            index = 0 if stage == 0 else 1 + 3 * (stage - 1) + j
            copies.append(send(buf.at[me], buf.at[me], sv_send.at[index], sv_recv.at[index], dev))
        return copies

    def small_sum(stage, copies):
        buf = (sv0, sv1, sv2, sv3)[stage]
        for copy in copies:
            copy.wait_recv()
        total = buf[0]
        for i in range(1, 2 if stage == 0 else 4):
            total = total + buf[i]
        return total

    small_copies = small_stage(0, small_s[...])
    join(3)
    advance_wave(1, 0)
    dxh = dn * gain
    rstd = rstd_s[:, 0:1]
    dx = rstd * (dxh - jnp.mean(dxh, axis=-1, keepdims=True) - xhat * jnp.mean(dxh * xhat, axis=-1, keepdims=True))
    gtok = g_s[...].astype(F32) + dx
    for slot in (1, 3):
        out_slot(slot, [gtok[(slot - 1) * QT : (slot + 1) * QT]])
    for slot in (4, 5, 6, 7):
        rows = slice(slot * QT, (slot + 1) * QT)
        out_slot(slot, [mixed[rows], gtok[rows]])
    for slot in KEPT_SLOTS:
        ret_ref[slot] = back_ref[slot]
    send_back((5, 7, 6, 3))
    for stage in range(1, 7):
        departed = len(started)
        advance_wave(0, stage)
        advance_wave(1, stage)
        if stage < 4:
            small_copies = small_stage(stage, small_sum(stage - 1, small_copies))
        elif stage == 4:
            small_out_ref[...] = small_sum(3, small_copies)
            for slot in back:
                back[slot].wait_recv()
        if stage < 6:
            for copy in started[:departed]:
                copy.wait_send()
            del started[:departed]
    for copy in started:
        copy.wait_send()


def finish_kernel(ret_ref, sum_ref, small_ref, perm_ref, mixed_ref, gtok_ref, gqkv_ref, gproj_ref, gain_ref, gscale_ref):
    ret = ret_ref[...].astype(F32)
    perm = perm_ref[...]
    mixed = jnp.concatenate([ret[0], ret[2]] + [ret[slot][:QT] for slot in (4, 5, 6, 7)], axis=0).astype(BF)
    gtok = jnp.concatenate([ret[1], ret[3]] + [ret[slot][QT:] for slot in (4, 5, 6, 7)], axis=0).astype(BF)
    mixed_ref[...] = dot(perm, mixed, 0, 0).astype(BF)
    gtok_ref[...] = dot(perm, gtok, 0, 0).astype(BF)
    for half in range(2):
        for p in range(4):
            for i in range(3):
                cols = slice(i * 512 + p * 128, i * 512 + (p + 1) * 128)
                first = p * 1024 + i * 256
                tile = sum_ref[half, first : first + 256]
                gqkv_ref[half * 256 : (half + 1) * 256, cols] = tile.astype(F32)
            for ct in range(4):
                first = p * 1024 + 768 + ct * 64
                tile = sum_ref[half, first : first + 64]
                rows = slice(p * 128 + half * 64, p * 128 + (half + 1) * 64)
                gproj_ref[rows, ct * 128 : (ct + 1) * 128] = tile.astype(F32)
    for i in range(4):
        gain_ref[:, i * 128 : (i + 1) * 128] = small_ref[i : i + 1, :]
    eye = lax.broadcasted_iota(jnp.int32, (8, 128), 0) == lax.broadcasted_iota(jnp.int32, (8, 128), 1)
    row = jnp.sum(jnp.where(eye, small_ref[8:16, :], 0.0), axis=0, keepdims=True)
    gscale_ref[...] = row[:, :8]


VM = pl.BlockSpec(memory_space=pltpu.VMEM)
HBM = pl.BlockSpec(memory_space=pltpu.HBM)
DMA = pltpu.SemaphoreType.DMA
MIB = 1024 * 1024


def per_device(tokens, cotangent, key_keep, norm_gain, w_qkv, w_proj, attn_scale):
    perm, member, place = tables()
    perm = jnp.asarray(perm, BF)
    x = tokens.reshape(288, 512)
    g = cotangent.reshape(288, 512)
    tok = (2 * WIN, 512)
    operands = (
        x, g, key_keep.transpose(1, 0, 2), perm, jnp.asarray(member, BF), jnp.asarray(place, BF),
        w_qkv, w_proj, norm_gain.reshape(1, 512), attn_scale,
    )
    operands = [pltpu.with_memory_space_constraint(operand, pltpu.HBM) for operand in operands]
    ret, total, small = pl.pallas_call(
        block_kernel,
        out_shape=(
            jax.ShapeDtypeStruct((8, ROWS, 512), BF),
            jax.ShapeDtypeStruct((2, 4096, 128), BF),
            jax.ShapeDtypeStruct((16, 128), F32),
        ),
        in_specs=[HBM] * 10,
        out_specs=(VM,) * 3,
        scratch_shapes=[
            pltpu.VMEM((288, 512), BF),
            pltpu.VMEM((288, 512), BF),
            pltpu.VMEM((6, 2, 24), jnp.int32),
            pltpu.VMEM((8 * QT, 288), BF),
            pltpu.VMEM((8, 288), BF),
            pltpu.VMEM((288, 256), BF),
            pltpu.VMEM((512, 1536), BF),
            pltpu.VMEM((512, 512), BF),
            pltpu.VMEM((1, 512), F32),
            pltpu.SMEM((8,), F32),
            pltpu.VMEM((5, ROWS, 512), BF),
            pltpu.VMEM((8, ROWS, 512), BF),
            pltpu.VMEM((8, ROWS, 512), BF),
            pltpu.VMEM(tok, F32),
            pltpu.VMEM(tok, F32),
            pltpu.VMEM((2 * WIN, 128), F32),
            pltpu.VMEM(tok, BF),
            pltpu.VMEM(tok, BF),
            pltpu.VMEM(tok, F32),
            pltpu.VMEM(tok, F32),
        ]
        + [pltpu.VMEM((2, 8, WIN), F32)]
        + [pltpu.VMEM(tok, BF)] * 10
        + [
            pltpu.VMEM((2, WIN, WIN), F32),
            pltpu.VMEM((8, 2, WIN), F32),
            pltpu.VMEM((16, 128), F32),
            pltpu.VMEM((2, 4096, 128), BF),
            pltpu.VMEM((4096, 128), BF),
            pltpu.VMEM((4096, 128), BF),
            pltpu.VMEM((3, 1024, 128), BF),
            pltpu.VMEM((1024, 128), BF),
            pltpu.VMEM((3, 256, 128), BF),
            pltpu.VMEM((4, 256, 128), BF),
            pltpu.VMEM((2, 16, 128), F32),
            pltpu.VMEM((4, 16, 128), F32),
            pltpu.VMEM((4, 16, 128), F32),
            pltpu.VMEM((4, 16, 128), F32),
            DMA((10,)),
            DMA((5,)), DMA((5,)),
            DMA((5,)), DMA((5,)),
            DMA((10,)), DMA((10,)),
            DMA((6, 5, 3)), DMA((6, 5, 3)),
            DMA((10,)), DMA((10,)),
        ],
        compiler_params=pltpu.CompilerParams(collective_id=1, has_side_effects=True, vmem_limit_bytes=40 * MIB),
        name="block",
    )(*operands)

    mixed, gtok, gqkv, gproj, gain, gscale = pl.pallas_call(
        finish_kernel,
        out_shape=(
            jax.ShapeDtypeStruct((288, 512), BF),
            jax.ShapeDtypeStruct((288, 512), BF),
            jax.ShapeDtypeStruct((512, 1536), F32),
            jax.ShapeDtypeStruct((512, 512), F32),
            jax.ShapeDtypeStruct((1, 512), F32),
            jax.ShapeDtypeStruct((1, 8), F32),
        ),
        in_specs=[VM] * 4,
        out_specs=(VM,) * 6,
        compiler_params=pltpu.CompilerParams(vmem_limit_bytes=24 * MIB),
        name="finish",
    )(ret, total, small, perm)
    return (
        mixed.reshape(tokens.shape),
        gtok.reshape(tokens.shape),
        gqkv,
        gproj,
        gain.reshape(512),
        gscale.reshape(8),
    )


def solution(mesh):
    grid = P(None, "lat", "lon", None)
    return jax.shard_map(
        per_device,
        mesh=mesh,
        in_specs=(grid, grid, P(None, "lat", "lon"), P(), P(), P(), P()),
        out_specs=(grid, grid, P(), P(), P(), P()),
        check_vma=False,
    )
```
